256 devices in a mesh: seq: 32 (over y, z_lo, core), tensor: 8 (over x, z_hi).
Axes of the slice: x: 4, y: 4, z: 8 (z_hi: 2, z_lo: 4; z = z_hi * 4 + z_lo), core: 2. Of those that a mesh axis runs over, the one named last changes fastest.
Arguments:
- features: bfloat16 [4, 40, 64, 512], P(None, 'tensor', 'seq'), may hold values from -6 to 6
- conv_weight: bfloat16 [3, 3, 3, 512, 16], replicated, may hold values from -0.0546875 to 0.0546875
- conv_bias: float32 [16], replicated, may hold values from -4 to 4
- embed_weight: bfloat16 [16, 5120], replicated, may hold values from -1.5 to 1.5
- position_table: bfloat16 [10240, 5120], P('seq'), may hold values from -6 to 6
- norm_gain: bfloat16 [5120], replicated, may hold values from 0.099609375 to 1.8984375
- qkv_weight: bfloat16 [5120, 6144], P('seq', 'tensor'), may hold values from -1 to 1
- page_owner: int32 [1280], P('seq'), may hold values from 0 to 31, as said below
- page_slot: int32 [1280], P('seq'), may hold values from 0 to 39, as said below
Outputs:
- attention: bfloat16 [10240, 4096], P('seq', 'tensor')
- kv_cache: bfloat16 [1280, 8, 2, 1024], P('seq', None, None, 'tensor')
The draws below stay inside these ranges and needn't reach their ends.
Inputs may be any that keep to these rules, and one draw needn't show every extreme that they name: `page_owner`: of the 40 pages of one index of seq, at most 3 have the same owner, and exactly 3 for some owner. Every owner keeps exactly 40 pages. `page_slot`: the pages of one owner use each slot 0 to 39 once.
All inputs are finite; a program needn't handle non-finite values.
Results may differ from the reference program's by a relative error of at most 0.0084.
Values may be sent and summed in bfloat16 or wider, within the bound.
No kernel may reach another device: no remote copies, remote signals or barrier semaphores. Data moves between devices by JAX's collectives and lax.ppermute only.
A program may use at most 128 MiB of HBM per device.

```python
import math
import jax
import jax.numpy as jnp
from jax import lax

D = 5120
HEADS = 32
KVH = 8
HD = 128
CH = 512
LAT = 16
LT = 4
LH = 40
PAGE = 8
GROUP = 4
QKVW = 6144
LW = 64
TOKENS = 10240
BLK_DEV = 40
BLOCKS = 1280
CAP = 3
N_SEQ = 32


def page_table(key):
    groups = (BLK_DEV + CAP - 1) // CAP
    first_key, second_key, third_key = jax.random.split(key, 3)
    offsets = jax.random.permutation(first_key, N_SEQ)[:groups].astype(jnp.int32)
    device_keys = jax.random.split(second_key, N_SEQ)
    ranking = jax.vmap(lambda device_key: jax.random.permutation(device_key, BLK_DEV))(device_keys).astype(jnp.int32)
    source = jnp.arange(N_SEQ, dtype=jnp.int32)[:, None]
    owner = (source + offsets[ranking // CAP]) % N_SEQ
    rotation = jax.random.randint(third_key, (N_SEQ,), 0, BLK_DEV).astype(jnp.int32)
    slot = (ranking + rotation[owner]) % BLK_DEV
    return (owner.reshape(-1).astype(jnp.int32), slot.reshape(-1).astype(jnp.int32))


def draw_page_owner(key, part):
    owner, slot = page_table(key)
    return owner


def draw_page_slot(key, part):
    owner, slot = page_table(key)
    return slot


def draw_qkv_weight(key, part):
    key = jax.random.fold_in(key, 7)
    base_key, direction_key, sign_key, pick_key, strength_key = jax.random.split(key, 5)
    entries = jax.random.truncated_normal(base_key, -3.0, 3.0, (D, QKVW), jnp.float32)
    lowest, highest = (8.0, 24.0)
    entries = entries * D ** (-0.5)
    direction = jax.random.truncated_normal(direction_key, -3.0, 3.0, (D, KVH), jnp.float32) * D ** (-0.5)
    signs = jnp.where(jax.random.bernoulli(sign_key, 0.5, (KVH, HD)), 1.0, -1.0).astype(jnp.float32)
    chosen = (jax.random.permutation(pick_key, KVH) < (KVH + 1) // 2).astype(jnp.float32)
    strength = jnp.exp(jax.random.uniform(strength_key, (KVH, GROUP), jnp.float32, math.log(lowest), math.log(highest)))
    query_gain = strength * HD ** (-0.5) * chosen[:, None]
    gains = jnp.concatenate([query_gain, chosen[:, None], jnp.zeros((KVH, 1), jnp.float32)], axis=1)
    aligned = direction[:, :, None, None] * gains[None, :, :, None] * signs[None, :, None, :]
    weight = entries + aligned.reshape(D, QKVW)
    return jnp.clip(weight, -1.0, 1.0).astype(jnp.bfloat16)


def steps_of(key, shape, pieces, smallest, high):
    gain, own = 1.0, jax.random.fold_in(key, 6)
    for dim, parts in pieces:
        draws = jnp.exp(jax.random.uniform(jax.random.fold_in(own, dim), (parts,), jnp.float32, smallest / len(pieces), high / len(pieces)))
        gain = gain * jnp.repeat(draws, shape[dim] // parts).reshape([-1 if axis == dim else 1 for axis in range(len(shape))])
    return gain


def bell_draw(key, shape, deviation, limit, shards=(), kind=jnp.bfloat16):
    values = deviation * jax.random.normal(key, shape, jnp.float32)
    if shards:
        values = values * steps_of(key, shape, shards, -0.22, 0.18)
    return jnp.clip(values, -limit, limit).astype(kind)


def setup_inputs(seed: int = 0) -> dict:
    arg_keys = jax.random.split(jax.random.key(seed), 10)
    features = bell_draw(arg_keys[0], (LT, LH, LW, CH), 1.0, 6.0, ((1, 8), (2, 32)))
    conv_weight = bell_draw(arg_keys[1], (3, 3, 3, CH, LAT), (27 * CH) ** -0.5, 0.0546875)
    conv_bias = bell_draw(arg_keys[2], (LAT,), 1.0, 4.0, (), jnp.float32)
    embed_weight = bell_draw(arg_keys[3], (LAT, D), LAT ** -0.5, 1.5)
    position_table = bell_draw(arg_keys[4], (TOKENS, D), 1.0, 6.0, ((0, 32),))
    norm_gain = jnp.clip(1.0 + 0.18 * jax.random.normal(arg_keys[5], (D,), jnp.float32), 0.099609375, 1.8984375).astype(jnp.bfloat16)
    qkv_weight = draw_qkv_weight(jax.random.fold_in(arg_keys[9], 71), 0)
    page_owner = draw_page_owner(jax.random.fold_in(arg_keys[9], 71), 0)
    page_slot = draw_page_slot(jax.random.fold_in(arg_keys[9], 71), 0)
    return {"features": features, "conv_weight": conv_weight, "conv_bias": conv_bias, "embed_weight": embed_weight, "position_table": position_table, "norm_gain": norm_gain, "qkv_weight": qkv_weight, "page_owner": page_owner, "page_slot": page_slot}


def pick_block(length):
    for candidate in range(min(length, 1024), 0, -1):
        if length % candidate == 0:
            return candidate
    return 1

def reference(features, conv_weight, conv_bias, embed_weight, position_table, norm_gain, qkv_weight, page_owner, page_slot):
    active = jax.nn.silu(features.astype(jnp.float32)).astype(jnp.bfloat16)
    padded = jnp.pad(active, ((2, 0), (1, 1), (1, 1), (0, 0)))
    latent = jnp.zeros((LT * LH * LW, LAT), jnp.float32)
    for offset_time in range(3):
        for offset_row in range(3):
            for offset_col in range(3):
                shifted = padded[offset_time:offset_time + LT, offset_row:offset_row + LH, offset_col:offset_col + LW, :]
                latent = latent + jnp.dot(shifted.reshape(-1, CH), conv_weight[offset_time, offset_row, offset_col], preferred_element_type=jnp.float32)
    latent = latent + conv_bias.astype(jnp.float32)
    hidden = jnp.dot(latent, embed_weight.astype(jnp.float32), precision=lax.Precision.HIGHEST) + position_table.astype(jnp.float32)
    normed = (hidden * lax.rsqrt(lax.optimization_barrier(jnp.mean(hidden * hidden, axis=-1, keepdims=True)) + 1e-05) * norm_gain.astype(jnp.float32)).astype(jnp.bfloat16)
    qkv = jnp.dot(normed, qkv_weight, preferred_element_type=jnp.float32).astype(jnp.bfloat16)
    split = qkv.reshape(TOKENS, KVH, GROUP + 2, HD)
    queries = split[:, :, :GROUP, :]
    keys = split[:, :, GROUP, :]
    values = split[:, :, GROUP + 1, :]
    scale = 1.0 / HD ** 0.5
    qblock = pick_block(TOKENS)
    nblocks = TOKENS // qblock
    key_index = jnp.arange(TOKENS, dtype=jnp.int32)

    def per_head(operands):
        head_queries, head_keys, head_values = operands
        keys_wide = head_keys.astype(jnp.float32)
        values_wide = head_values.astype(jnp.float32)

        def per_block(block_index):
            first = (block_index * qblock).astype(jnp.int32)
            block_queries = lax.dynamic_slice_in_dim(head_queries, first, qblock, 0).astype(jnp.float32)
            scores = jnp.einsum('qgd,kd->gqk', block_queries, keys_wide) * scale
            query_index = first + jnp.arange(qblock, dtype=jnp.int32)
            allowed = key_index[None, :] <= query_index[:, None]
            scores = jnp.where(allowed[None], scores, -1e+30)
            largest = lax.optimization_barrier(jnp.max(scores, axis=-1, keepdims=True))
            weights = jnp.where(allowed[None], jnp.exp(scores - largest), 0.0)
            totals = lax.optimization_barrier(jnp.sum(weights, axis=-1))
            rounded = weights.astype(jnp.bfloat16).astype(jnp.float32)
            output = jnp.einsum('gqk,kd->qgd', rounded, values_wide) / jnp.transpose(totals)[:, :, None]
            return output.astype(jnp.bfloat16)
        return lax.map(per_block, jnp.arange(nblocks, dtype=jnp.int32))
    per_heads = lax.map(per_head, (jnp.transpose(queries, (1, 0, 2, 3)), jnp.transpose(keys, (1, 0, 2)), jnp.transpose(values, (1, 0, 2))))
    attention = jnp.transpose(per_heads, (1, 2, 0, 3, 4)).reshape(TOKENS, HEADS * HD)
    pages = jnp.stack([keys.reshape(TOKENS, KVH * HD), values.reshape(TOKENS, KVH * HD)], axis=1).reshape(BLOCKS, PAGE, 2, KVH * HD)
    target = page_owner.astype(jnp.int32) * BLK_DEV + page_slot.astype(jnp.int32)
    kv_cache = jnp.zeros((BLOCKS, PAGE, 2, KVH * HD), jnp.bfloat16).at[target].set(pages)
    return (attention, kv_cache)
```

```python
import functools

import jax
import jax.numpy as jnp
import numpy as np
from jax import lax
from jax.experimental import pallas as pl
from jax.experimental.pallas import tpu as pltpu
from jax.sharding import PartitionSpec as P

HD = 128
PAGE = 8
GROUP = 4
LAT = 16
BLK = 320
PAGES = 40
SEQ = 32
ROWS = 5
COLS = 2
FRAMES = 4
EXT = (ROWS + 2) * (COLS + 2)
TOK = 384
CHUNK = 1280
TILE = 256
QROWS = GROUP * BLK
VMEM = 56 * 1024 * 1024


def params(**extra):
    return pltpu.CompilerParams(vmem_limit_bytes=VMEM, **extra)


def roll_lanes(value, shift):
    shift = shift % value.shape[1]
    return pltpu.roll(value, shift, 1) if shift else value


def conv_kernel(feat_ref, weight_ref, out_ref, grid_ref):
    grid_ref[...] = jnp.zeros_like(grid_ref)
    for frame in range(FRAMES):
        for row in range(ROWS):
            start = frame * EXT + (row + 1) * (COLS + 2) + 1
            value = feat_ref[frame, row].astype(jnp.float32)
            grid_ref[start : start + COLS, :] = value / (1.0 + jnp.exp(-value))
    active = grid_ref[...].astype(jnp.bfloat16)
    product = lax.dot_general(
        weight_ref[...], active, (((1,), (1,)), ((), ())), preferred_element_type=jnp.float32
    )
    lane = lax.broadcasted_iota(jnp.int32, (LAT, 128), 1)
    total = jnp.zeros((LAT, 128), jnp.float32)
    for time in range(3):
        part = jnp.zeros((LAT, 128), jnp.float32)
        for row in range(3):
            for col in range(3):
                index = (time * 3 + row) * 3 + col
                piece = product[index * LAT : (index + 1) * LAT, :]
                part = part + roll_lanes(piece, -((row - 1) * (COLS + 2) + col - 1))
        delay = (2 - time) * EXT
        if delay:
            part = jnp.where(lane >= delay, roll_lanes(part, delay), 0.0)
        total = total + part
    padded = jnp.concatenate([total, jnp.zeros((128 - LAT, 128), jnp.float32)], axis=0)
    out_ref[...] = jnp.transpose(padded)[:, :LAT]


def partial_latents(features, conv_weight):
    weight = jnp.transpose(conv_weight, (0, 1, 2, 4, 3)).reshape(-1, conv_weight.shape[3])
    return pl.pallas_call(
        conv_kernel,
        out_shape=jax.ShapeDtypeStruct((128, LAT), jnp.float32),
        scratch_shapes=[pltpu.VMEM((128, features.shape[-1]), jnp.float32)],
        compiler_params=params(),
        name="conv",
    )(features, weight)


def split_three(value):
    high = value.astype(jnp.bfloat16)
    rest = value - high.astype(jnp.float32)
    middle = rest.astype(jnp.bfloat16)
    low = (rest - middle.astype(jnp.float32)).astype(jnp.bfloat16)
    return high, middle, low


def place_kernel(parts_ref, token_ref, out_ref):
    count = parts_ref.shape[0]
    token = lax.broadcasted_iota(jnp.int32, (count, TOK), 1)
    pick = jnp.where(token == token_ref[...], 1.0, 0.0).astype(jnp.bfloat16)
    total = jnp.zeros((LAT, TOK), jnp.float32)
    for part in reversed(split_three(parts_ref[...])):
        total = total + lax.dot_general(
            part, pick, (((0,), (0,)), ((), ())), preferred_element_type=jnp.float32
        )
    out_ref[...] = total


def place_table():
    table = np.full((3, SEQ, ROWS + 2, COLS + 2), -1, np.int32)
    for case in range(3):
        for source in range(SEQ):
            for row in range(ROWS + 2):
                for col in range(COLS + 2):
                    height = row - 1 + ROWS * (case - 1)
                    width = source * COLS - 1 + col
                    if 0 <= height < ROWS and 0 <= width < SEQ * COLS:
                        table[case, source, row, col] = height * SEQ * COLS + width
    return table.reshape(3, SEQ * EXT, 1)


def place_latents(parts, offset):
    table = jnp.asarray(place_table())
    token = lax.dynamic_index_in_dim(table, jnp.clip(offset + 1, 0, 2), 0, keepdims=False)
    token = jnp.where(jnp.abs(offset) <= 1, token, -1)
    return pl.pallas_call(
        place_kernel,
        out_shape=jax.ShapeDtypeStruct((LAT, TOK), jnp.float32),
        compiler_params=params(),
        name="place",
    )(parts, token)


def hidden_kernel(latent_ref, bias_ref, embed_ref, table_ref, gain_ref, out_ref, hid_ref, sq_ref):
    step = pl.program_id(0)
    width = table_ref.shape[1]
    latent = latent_ref[...][:, :BLK] + bias_ref[...]
    latent = jnp.concatenate(split_three(latent), axis=0)
    embed = embed_ref[...]
    hidden = lax.dot_general(
        latent,
        jnp.concatenate([embed, embed, embed], axis=0),
        (((0,), (0,)), ((), ())),
        preferred_element_type=jnp.float32,
    ) + table_ref[...].astype(jnp.float32)
    hid_ref[step] = hidden
    squares = jnp.zeros((BLK, 128), jnp.float32)
    for lane in range(0, width, 128):
        piece = hidden[:, lane : lane + 128]
        squares = squares + piece * piece

    @pl.when(step == 0)
    def _():
        sq_ref[...] = squares

    @pl.when(step > 0)
    def _():
        sq_ref[...] += squares

    @pl.when(step == pl.num_programs(0) - 1)
    def _():
        count = hid_ref.shape[0]
        mean = jnp.sum(sq_ref[...], axis=1, keepdims=True) / (count * width)
        factor = lax.rsqrt(mean + 1e-05)
        for tile in range(count):
            cut = slice(tile * width, (tile + 1) * width)
            gain = gain_ref[:, cut].astype(jnp.float32)
            out_ref[:, cut] = (hid_ref[tile] * factor * gain).astype(jnp.bfloat16)


def normed_hidden(latent, conv_bias, embed_weight, position_table, norm_gain):
    depth = position_table.shape[1]
    steps = 8
    width = depth // steps
    return pl.pallas_call(
        hidden_kernel,
        grid=(steps,),
        in_specs=[
            pl.BlockSpec((LAT, TOK), lambda i: (0, 0)),
            pl.BlockSpec((LAT, 1), lambda i: (0, 0)),
            pl.BlockSpec((LAT, width), lambda i: (0, i)),
            pl.BlockSpec((BLK, width), lambda i: (0, i)),
            pl.BlockSpec((1, depth), lambda i: (0, 0)),
        ],
        out_specs=pl.BlockSpec((BLK, depth), lambda i: (0, 0)),
        out_shape=jax.ShapeDtypeStruct((BLK, depth), jnp.bfloat16),
        scratch_shapes=[
            pltpu.VMEM((steps, BLK, width), jnp.float32),
            pltpu.VMEM((BLK, 128), jnp.float32),
        ],
        compiler_params=params(dimension_semantics=("arbitrary",)),
        name="hidden",
    )(latent, conv_bias.reshape(LAT, 1), embed_weight, position_table, norm_gain.reshape(1, depth))


def attend_chunk(masked, first_key, first_query, q_ref, kv_ref, best_ref, total_ref, sum_ref):
    scale = 1.4426950408889634 / HD**0.5
    keys = kv_ref[:, :HD]
    values = kv_ref[:, HD:]
    for start in range(0, QROWS, TILE):
        cut = slice(start, start + TILE)
        scores = lax.dot_general(
            keys, q_ref[cut, :], (((1,), (1,)), ((), ())), preferred_element_type=jnp.float32
        )
        if masked:
            key = first_key + lax.broadcasted_iota(jnp.int32, scores.shape, 0)
            query = start + lax.broadcasted_iota(jnp.int32, (1, TILE), 1)
            for head in range(GROUP - 1, 0, -1):
                query = jnp.where(query >= head * BLK, query - head * BLK, query)
            scores = jnp.where(key <= first_query + query, scores, -1e30)
        old = best_ref[:, cut]
        best = jnp.maximum(old, jnp.max(scores, axis=0, keepdims=True))
        factor = jnp.exp2((old - best) * scale)
        weights = jnp.exp2((scores - best) * scale)
        best_ref[:, cut] = best
        total_ref[:, cut] = total_ref[:, cut] * factor + jnp.sum(weights, axis=0, keepdims=True)
        sum_ref[:, cut] = sum_ref[:, cut] * factor + lax.dot_general(
            values,
            weights.astype(jnp.bfloat16),
            (((0,), (0,)), ((), ())),
            preferred_element_type=jnp.float32,
        )


def attention_kernel(me_ref, qkv_ref, kv_ref, out_ref, q_ref, best_ref, total_ref, sum_ref, row_ref):
    step = pl.program_id(0)
    me = me_ref[0]
    mine = me // (CHUNK // BLK)

    @pl.when(step == 0)
    def _():
        best_ref[...] = jnp.full_like(best_ref, -1e30)
        total_ref[...] = jnp.zeros_like(total_ref)
        sum_ref[...] = jnp.zeros_like(sum_ref)
        for head in range(GROUP):
            q_ref[head * BLK : (head + 1) * BLK, :] = qkv_ref[:, head * HD : (head + 1) * HD]

    state = (q_ref, kv_ref, best_ref, total_ref, sum_ref)

    @pl.when(step < mine)
    def _():
        attend_chunk(False, 0, 0, *state)

    @pl.when(step == mine)
    def _():
        attend_chunk(True, step * CHUNK, me * BLK, *state)

    @pl.when(step == pl.num_programs(0) - 1)
    def _():
        for start in range(0, QROWS, TILE):
            cut = slice(start, start + TILE)
            row_ref[cut, :] = jnp.transpose(sum_ref[:, cut] / total_ref[:, cut])
        for head in range(GROUP):
            rows = row_ref[head * BLK : (head + 1) * BLK, :]
            out_ref[:, head * HD : (head + 1) * HD] = rows.astype(jnp.bfloat16)


def attend(me, qkv, kv):
    steps = kv.shape[0] // CHUNK
    return pl.pallas_call(
        attention_kernel,
        grid_spec=pltpu.PrefetchScalarGridSpec(
            num_scalar_prefetch=1,
            grid=(steps,),
            in_specs=[
                pl.BlockSpec(qkv.shape, lambda i, me: (0, 0)),
                pl.BlockSpec(
                    (CHUNK, 2 * HD), lambda i, me: (jnp.minimum(i, me[0] // (CHUNK // BLK)), 0)
                ),
            ],
            out_specs=pl.BlockSpec((BLK, GROUP * HD), lambda i, me: (0, 0)),
            scratch_shapes=[
                pltpu.VMEM((QROWS, HD), jnp.bfloat16),
                pltpu.VMEM((1, QROWS), jnp.float32),
                pltpu.VMEM((1, QROWS), jnp.float32),
                pltpu.VMEM((HD, QROWS), jnp.float32),
                pltpu.VMEM((QROWS, HD), jnp.float32),
            ],
        ),
        out_shape=jax.ShapeDtypeStruct((BLK, GROUP * HD), jnp.bfloat16),
        compiler_params=params(dimension_semantics=("arbitrary",)),
        name="attend",
    )(me.reshape(1), qkv, kv)


def page_kernel(page_ref, kv_ref, out_ref, held_ref, sems):
    def copy(slot):
        first = pl.multiple_of((page_ref[slot] // 2) * 2 * PAGE, 2 * PAGE)
        return pltpu.make_async_copy(
            kv_ref.at[pl.ds(first, 2 * PAGE), :], held_ref.at[slot], sems.at[slot]
        )

    for slot in range(PAGES):
        copy(slot).start()
    for pair in range(PAGES // 2):
        halves = []
        for slot in (2 * pair, 2 * pair + 1):
            copy(slot).wait()
            rows = held_ref[slot].astype(jnp.float32)
            odd = page_ref[slot] % 2 == 1
            halves.append(jnp.where(odd, rows[PAGE:], rows[:PAGE]))
        both = jnp.concatenate(halves, axis=0).astype(jnp.bfloat16)
        out_ref[pair * 2 * PAGE : (pair + 1) * 2 * PAGE, :] = both


def fetch_pages(pages, kv):
    return pl.pallas_call(
        page_kernel,
        in_specs=[
            pl.BlockSpec(memory_space=pltpu.SMEM),
            pl.BlockSpec(memory_space=pl.ANY),
        ],
        out_shape=jax.ShapeDtypeStruct((PAGES * PAGE, 2 * HD), jnp.bfloat16),
        scratch_shapes=[
            pltpu.VMEM((PAGES, 2 * PAGE, 2 * HD), jnp.bfloat16),
            pltpu.SemaphoreType.DMA((PAGES,)),
        ],
        compiler_params=params(),
        name="pages",
    )(pages, kv)


def on_device(
    features,
    conv_weight,
    conv_bias,
    embed_weight,
    position_table,
    norm_gain,
    qkv_weight,
    page_owner,
    page_slot,
):
    me = lax.axis_index("seq").astype(jnp.int32)
    tensor = lax.axis_index("tensor").astype(jnp.int32)
    tensor_count = lax.axis_size("tensor")
    weight = lax.all_gather(qkv_weight, "seq", axis=0, tiled=True)
    parts = partial_latents(features, conv_weight)
    own = parts[: FRAMES * EXT].reshape(FRAMES, EXT * LAT)
    target = (page_owner * PAGES + page_slot).astype(jnp.float32)
    target = jnp.broadcast_to(target, (FRAMES, PAGES))
    message = jnp.concatenate([own, target], axis=1)
    message = jnp.pad(message, ((0, 0), (0, 512 - message.shape[1])))
    message = jnp.broadcast_to(message[:, None], (FRAMES, SEQ // FRAMES, 512)).reshape(SEQ, 512)
    message = lax.all_to_all(message, "seq", split_axis=0, concat_axis=0, tiled=True)
    targets = message[:, EXT * LAT : EXT * LAT + PAGES].astype(jnp.int32).reshape(-1)
    mine = me * PAGES + jnp.arange(PAGES, dtype=jnp.int32)
    index = jnp.arange(SEQ * PAGES, dtype=jnp.int32)
    pages = jnp.sum(jnp.where(targets[None, :] == mine[:, None], index[None, :], 0), axis=1)
    offset = tensor - me % (SEQ // FRAMES)
    latent = place_latents(message[:, : EXT * LAT].reshape(SEQ * EXT, LAT), offset)
    for bit in (1, 2, 4):
        swap = [(i, i ^ bit) for i in range(tensor_count)]
        latent = latent + lax.ppermute(latent, "tensor", swap)
    normed = normed_hidden(latent, conv_bias, embed_weight, position_table, norm_gain)
    qkv = jnp.dot(normed, weight, preferred_element_type=jnp.float32).astype(jnp.bfloat16)
    kv = lax.all_gather(qkv[:, GROUP * HD :], "seq", axis=0, tiled=True)
    attention = attend(me, qkv, kv)
    kv_cache = fetch_pages(pages, kv).reshape(PAGES, PAGE, 2, HD)
    return (attention, kv_cache)


def solution(mesh):
    placed = (
        P(None, "tensor", "seq", None),
        P(),
        P(),
        P(),
        P("seq", None),
        P(),
        P("seq", "tensor"),
        P("seq"),
        P("seq"),
    )
    return jax.shard_map(
        on_device,
        mesh=mesh,
        in_specs=placed,
        out_specs=(P("seq", "tensor"), P("seq", None, None, "tensor")),
        check_vma=False,
    )
```

```python
import functools

import jax
import jax.numpy as jnp
import numpy as np
from jax import lax
from jax.experimental import pallas as pl
from jax.experimental.pallas import tpu as pltpu
from jax.sharding import PartitionSpec as P

HD = 128
PAGE = 8
GROUP = 4
LAT = 16
BLK = 320
PAGES = 40
SEQ = 32
ROWS = 5
COLS = 2
FRAMES = 4
EXT = (ROWS + 2) * (COLS + 2)
TOK = 384
TILE = 256
QROWS = GROUP * BLK
STATE = HD + 8
VMEM = 24 * 1024 * 1024


def params(**extra):
    return pltpu.CompilerParams(vmem_limit_bytes=VMEM, **extra)


def cost(blocks):
    scores = blocks * 2 * QROWS * BLK
    return pl.CostEstimate(flops=4 * HD * scores, bytes_accessed=3 << 20, transcendentals=scores)


def roll_lanes(value, shift):
    shift = shift % value.shape[1]
    return pltpu.roll(value, shift, 1) if shift else value


def conv_kernel(feat_ref, weight_ref, out_ref, grid_ref):
    grid_ref[...] = jnp.zeros_like(grid_ref)
    for frame in range(FRAMES):
        for row in range(ROWS):
            start = frame * EXT + (row + 1) * (COLS + 2) + 1
            value = feat_ref[frame, row].astype(jnp.float32)
            grid_ref[start : start + COLS, :] = value / (1.0 + jnp.exp(-value))
    active = grid_ref[...].astype(jnp.bfloat16)
    product = lax.dot_general(
        weight_ref[...], active, (((1,), (1,)), ((), ())), preferred_element_type=jnp.float32
    )
    lane = lax.broadcasted_iota(jnp.int32, (LAT, 128), 1)
    total = jnp.zeros((LAT, 128), jnp.float32)
    for time in range(3):
        part = jnp.zeros((LAT, 128), jnp.float32)
        for row in range(3):
            for col in range(3):
                index = (time * 3 + row) * 3 + col
                piece = product[index * LAT : (index + 1) * LAT, :]
                part = part + roll_lanes(piece, -((row - 1) * (COLS + 2) + col - 1))
        delay = (2 - time) * EXT
        if delay:
            part = jnp.where(lane >= delay, roll_lanes(part, delay), 0.0)
        total = total + part
    padded = jnp.concatenate([total, jnp.zeros((128 - LAT, 128), jnp.float32)], axis=0)
    out_ref[...] = jnp.transpose(padded)[:, :LAT]


def partial_latents(features, conv_weight):
    weight = jnp.transpose(conv_weight, (0, 1, 2, 4, 3)).reshape(-1, conv_weight.shape[3])
    return pl.pallas_call(
        conv_kernel,
        out_shape=jax.ShapeDtypeStruct((128, LAT), jnp.float32),
        scratch_shapes=[pltpu.VMEM((128, features.shape[-1]), jnp.float32)],
        compiler_params=params(),
        name="conv",
    )(features, weight)


def split_three(value):
    high = value.astype(jnp.bfloat16)
    rest = value - high.astype(jnp.float32)
    middle = rest.astype(jnp.bfloat16)
    low = (rest - middle.astype(jnp.float32)).astype(jnp.bfloat16)
    return high, middle, low


def place_kernel(parts_ref, token_ref, out_ref):
    count = parts_ref.shape[0]
    token = lax.broadcasted_iota(jnp.int32, (count, TOK), 1)
    pick = jnp.where(token == token_ref[...], 1.0, 0.0).astype(jnp.bfloat16)
    total = jnp.zeros((LAT, TOK), jnp.float32)
    for part in reversed(split_three(parts_ref[...])):
        total = total + lax.dot_general(
            part, pick, (((0,), (0,)), ((), ())), preferred_element_type=jnp.float32
        )
    out_ref[...] = total


def place_table():
    table = np.full((3, SEQ, ROWS + 2, COLS + 2), -1, np.int32)
    for case in range(3):
        for source in range(SEQ):
            for row in range(ROWS + 2):
                for col in range(COLS + 2):
                    height = row - 1 + ROWS * (case - 1)
                    width = source * COLS - 1 + col
                    if 0 <= height < ROWS and 0 <= width < SEQ * COLS:
                        table[case, source, row, col] = height * SEQ * COLS + width
    return table.reshape(3, SEQ * EXT, 1)


def place_latents(parts, offset):
    table = jnp.asarray(place_table())
    token = lax.dynamic_index_in_dim(table, jnp.clip(offset + 1, 0, 2), 0, keepdims=False)
    token = jnp.where(jnp.abs(offset) <= 1, token, -1)
    return pl.pallas_call(
        place_kernel,
        out_shape=jax.ShapeDtypeStruct((LAT, TOK), jnp.float32),
        compiler_params=params(),
        name="place",
    )(parts, token)


def hidden_kernel(latent_ref, bias_ref, embed_ref, table_ref, gain_ref, out_ref, hid_ref, sq_ref):
    step = pl.program_id(0)
    width = table_ref.shape[1]
    latent = latent_ref[...][:, :BLK] + bias_ref[...]
    latent = jnp.concatenate(split_three(latent), axis=0)
    embed = embed_ref[...]
    hidden = lax.dot_general(
        latent,
        jnp.concatenate([embed, embed, embed], axis=0),
        (((0,), (0,)), ((), ())),
        preferred_element_type=jnp.float32,
    ) + table_ref[...].astype(jnp.float32)
    hid_ref[step] = hidden
    squares = jnp.zeros((BLK, 128), jnp.float32)
    for lane in range(0, width, 128):
        piece = hidden[:, lane : lane + 128]
        squares = squares + piece * piece

    @pl.when(step == 0)
    def _():
        sq_ref[...] = squares

    @pl.when(step > 0)
    def _():
        sq_ref[...] += squares

    @pl.when(step == pl.num_programs(0) - 1)
    def _():
        count = hid_ref.shape[0]
        mean = jnp.sum(sq_ref[...], axis=1, keepdims=True) / (count * width)
        factor = lax.rsqrt(mean + 1e-05)
        for tile in range(count):
            cut = slice(tile * width, (tile + 1) * width)
            gain = gain_ref[:, cut].astype(jnp.float32)
            out_ref[:, cut] = (hid_ref[tile] * factor * gain).astype(jnp.bfloat16)


def normed_hidden(latent, conv_bias, embed_weight, position_table, norm_gain):
    depth = position_table.shape[1]
    steps = 8
    width = depth // steps
    return pl.pallas_call(
        hidden_kernel,
        grid=(steps,),
        in_specs=[
            pl.BlockSpec((LAT, TOK), lambda i: (0, 0)),
            pl.BlockSpec((LAT, 1), lambda i: (0, 0)),
            pl.BlockSpec((LAT, width), lambda i: (0, i)),
            pl.BlockSpec((BLK, width), lambda i: (0, i)),
            pl.BlockSpec((1, depth), lambda i: (0, 0)),
        ],
        out_specs=pl.BlockSpec((BLK, depth), lambda i: (0, 0)),
        out_shape=jax.ShapeDtypeStruct((BLK, depth), jnp.bfloat16),
        scratch_shapes=[
            pltpu.VMEM((steps, BLK, width), jnp.float32),
            pltpu.VMEM((BLK, 128), jnp.float32),
        ],
        compiler_params=params(dimension_semantics=("arbitrary",)),
        name="hidden",
    )(latent, conv_bias.reshape(LAT, 1), embed_weight, position_table, norm_gain.reshape(1, depth))


def attend_block(masked, partner_full, keys, values, q_ref, state_ref):
    scale = 1.4426950408889634 / HD**0.5
    tiles = 2 * QROWS // TILE

    def score(tile):
        return lax.dot_general(
            keys,
            q_ref[tile * TILE : (tile + 1) * TILE, :],
            (((1,), (1,)), ((), ())),
            preferred_element_type=jnp.float32,
        )

    upcoming = score(0)
    for tile in range(tiles):
        scores = upcoming
        if tile + 1 < tiles:
            upcoming = score(tile + 1)
        cut = slice(tile * TILE, (tile + 1) * TILE)
        allowed = None
        if masked:
            key = lax.broadcasted_iota(jnp.int32, scores.shape, 0)
            query = tile * TILE + lax.broadcasted_iota(jnp.int32, (1, TILE), 1)
            if tile * TILE >= QROWS:
                query = jnp.where(partner_full, BLK, -1) + 0 * query
            else:
                for head in range(GROUP - 1, 0, -1):
                    query = jnp.where(query >= head * BLK, query - head * BLK, query)
            allowed = key <= query
            scores = jnp.where(allowed, scores, -1e30)
        peak = jnp.max(scores, axis=0, keepdims=True)
        if masked:
            best = peak
        else:
            old = state_ref[HD : HD + 1, cut]
            best = jnp.maximum(old, peak)
            factor = jnp.exp2((old - best) * scale)
        weights = jnp.exp2((scores - best) * scale)
        if masked:
            weights = jnp.where(allowed, weights, 0.0)
        total = jnp.sum(weights, axis=0, keepdims=True)
        summed = lax.dot_general(
            values,
            weights.astype(jnp.bfloat16),
            (((0,), (0,)), ((), ())),
            preferred_element_type=jnp.float32,
        )
        if not masked:
            total = total + state_ref[HD + 1 : HD + 2, cut] * factor
            summed = summed + state_ref[:HD, cut] * factor
        state_ref[HD : HD + 1, cut] = best
        state_ref[HD + 1 : HD + 2, cut] = total
        state_ref[:HD, cut] = summed


def set_queries(own_ref, pair_ref, q_ref):
    for index, ref in enumerate((own_ref, pair_ref)):
        for head in range(GROUP):
            start = (index * GROUP + head) * BLK
            q_ref[start : start + BLK, :] = ref[:, head * HD : (head + 1) * HD]


def first_kernel(core_ref, own_ref, pair_ref, kv_ref, state_ref, q_ref):
    set_queries(own_ref, pair_ref, q_ref)
    state_ref[HD + 2 :, :] = jnp.zeros((STATE - HD - 2, 2 * QROWS), jnp.float32)
    attend_block(True, core_ref[0] == 0, kv_ref[:, :HD], kv_ref[:, HD:], q_ref, state_ref)


def attend_first(core, own, pair, kv):
    return pl.pallas_call(
        first_kernel,
        in_specs=[pl.BlockSpec(memory_space=pltpu.SMEM)]
        + [pl.BlockSpec(memory_space=pltpu.VMEM)] * 3,
        out_shape=jax.ShapeDtypeStruct((STATE, 2 * QROWS), jnp.float32),
        scratch_shapes=[pltpu.VMEM((2 * QROWS, HD), jnp.bfloat16)],
        compiler_params=params(),
        cost_estimate=cost(1),
        name="first",
    )(core.reshape(1), own, pair, kv)


def more_kernel(sizes, split, flag_ref, own_ref, pair_ref, state_ref, *rest):
    arrays, rest = rest[: len(sizes)], rest[len(sizes) :]
    if split:
        own_out_ref, pair_out_ref, q_ref, held_ref, sems, work_ref = rest
    else:
        work_ref, q_ref, held_ref, sems = rest
    copies = []
    first = 0
    for index, size in enumerate(sizes):
        copies.append(
            pltpu.make_async_copy(
                arrays[index], held_ref.at[pl.ds(first, size * BLK), :], sems.at[index]
            )
        )
        copies[-1].start()
        first += size * BLK
    set_queries(own_ref, pair_ref, q_ref)
    work_ref[...] = state_ref[...]
    for copy in copies:
        copy.wait()

    def body(index, carry):
        @pl.when(flag_ref[index] != 0)
        def _():
            rows = pl.ds(pl.multiple_of(index * BLK, BLK), BLK)
            attend_block(False, None, held_ref[rows, :HD], held_ref[rows, HD:], q_ref, work_ref)

        return carry

    lax.fori_loop(0, sum(sizes), body, 0)
    if split:
        own_out_ref[...] = work_ref[:, :QROWS]
        pair_out_ref[...] = work_ref[:, QROWS:]


def attend_more(flags, own, pair, state, arrays, split=False):
    sizes = tuple(array.shape[0] // BLK for array in arrays)
    half = jax.ShapeDtypeStruct((STATE, QROWS), jnp.float32)
    whole = jax.ShapeDtypeStruct((STATE, 2 * QROWS), jnp.float32)
    scratch = [
        pltpu.VMEM((2 * QROWS, HD), jnp.bfloat16),
        pltpu.VMEM((sum(sizes) * BLK, 2 * HD), jnp.bfloat16),
        pltpu.SemaphoreType.DMA((len(sizes),)),
    ]
    if split:
        scratch.append(pltpu.VMEM((STATE, 2 * QROWS), jnp.float32))
    return pl.pallas_call(
        functools.partial(more_kernel, sizes, split),
        in_specs=[pl.BlockSpec(memory_space=pltpu.SMEM)]
        + [pl.BlockSpec(memory_space=pltpu.VMEM)] * 3
        + [pl.BlockSpec(memory_space=pl.ANY)] * len(sizes),
        out_shape=(half, half) if split else whole,
        scratch_shapes=scratch,
        compiler_params=params(),
        cost_estimate=cost(sum(sizes)),
        name="more",
    )(flags, own, pair, state, *arrays)


def finish_kernel(own_ref, got_ref, out_ref, row_ref):
    scale = 1.4426950408889634 / HD**0.5
    for start in range(0, QROWS, TILE):
        cut = slice(start, start + TILE)
        first, second = own_ref[HD : HD + 1, cut], got_ref[HD : HD + 1, cut]
        best = jnp.maximum(first, second)
        first = jnp.exp2((first - best) * scale)
        second = jnp.exp2((second - best) * scale)
        total = own_ref[HD + 1 : HD + 2, cut] * first + got_ref[HD + 1 : HD + 2, cut] * second
        summed = own_ref[:HD, cut] * first + got_ref[:HD, cut] * second
        row_ref[cut, :] = jnp.transpose(summed / total)
    for head in range(GROUP):
        rows = row_ref[head * BLK : (head + 1) * BLK, :]
        out_ref[:, head * HD : (head + 1) * HD] = rows.astype(jnp.bfloat16)


def finish(own, got):
    return pl.pallas_call(
        finish_kernel,
        out_shape=jax.ShapeDtypeStruct((BLK, GROUP * HD), jnp.bfloat16),
        scratch_shapes=[pltpu.VMEM((QROWS, HD), jnp.float32)],
        compiler_params=params(),
        name="finish",
    )(own, got)


def page_kernel(code_ref, row_ref, odd_ref, *rest):
    arrays, (own_ref, pair_ref, held_ref, sems) = rest[:-4], rest[-4:]
    count = 2 * PAGES

    def start(slot, carry):
        row = pl.multiple_of(row_ref[slot], 2 * PAGE)
        for index, array in enumerate(arrays):

            @pl.when(code_ref[slot] == index)
            def _():
                pltpu.make_async_copy(
                    array.at[pl.ds(row, 2 * PAGE), :], held_ref.at[slot], sems.at[slot]
                ).start()

        return carry

    lax.fori_loop(0, count, start, 0)
    for pair in range(count // 2):
        halves = []
        for slot in (2 * pair, 2 * pair + 1):
            pltpu.make_async_copy(
                arrays[0].at[pl.ds(0, 2 * PAGE), :], held_ref.at[slot], sems.at[slot]
            ).wait()
            rows = held_ref[slot].astype(jnp.float32)
            halves.append(jnp.where(odd_ref[slot] == 1, rows[PAGE:], rows[:PAGE]))
        both = jnp.concatenate(halves, axis=0).astype(jnp.bfloat16)
        out_ref = own_ref if 2 * pair < PAGES else pair_ref
        place = (2 * pair % PAGES) * PAGE
        out_ref[place : place + 2 * PAGE, :] = both


def fetch_pages(code, row, odd, arrays):
    out = jax.ShapeDtypeStruct((PAGES * PAGE, 2 * HD), jnp.bfloat16)
    return pl.pallas_call(
        page_kernel,
        in_specs=[pl.BlockSpec(memory_space=pltpu.SMEM)] * 3
        + [pl.BlockSpec(memory_space=pl.ANY)] * len(arrays),
        out_shape=(out, out),
        scratch_shapes=[
            pltpu.VMEM((2 * PAGES, 2 * PAGE, 2 * HD), jnp.bfloat16),
            pltpu.SemaphoreType.DMA((2 * PAGES,)),
        ],
        compiler_params=params(),
        name="pages",
    )(code, row, odd, *arrays)


def moves(step):
    pairs = []
    for y in range(4):
        for z in range(4):
            for core in range(2):
                to_y, to_z, to_core = step(y, z, core)
                pairs.append(((y * 4 + z) * 2 + core, (to_y * 4 + to_z) * 2 + to_core))
    return pairs


def along_y(value, count):
    return lax.ppermute(value, "seq", moves(lambda y, z, c: ((y + count) % 4, z, c)))


def along_z(value, count):
    return lax.ppermute(value, "seq", moves(lambda y, z, c: (y, (z + count) % 4, c)))


def other_core(value):
    return lax.ppermute(value, "seq", moves(lambda y, z, c: (y, z, 1 - c)))


def pages_of(targets, owner):
    mine = owner * PAGES + jnp.arange(PAGES, dtype=jnp.int32)
    index = jnp.arange(SEQ * PAGES, dtype=jnp.int32)
    return jnp.sum(jnp.where(targets[None, :] == mine[:, None], index[None, :], 0), axis=1)


def attention_and_pages(me, targets, qkv):
    core, z, y = me % 2, (me // 2) % 4, me // 8
    queries, kv = qkv[:, : GROUP * HD], qkv[:, GROUP * HD :]
    pair = other_core(queries)
    by_z = {0: kv}
    for count in (1, 2, 3):
        by_z[count] = along_z(kv, count)
    zero = {count: along_y(kv, count) for count in (1, 3, 2)}
    one = {count: along_y(by_z[1], count) for count in (1, 3, 2)}
    last = jnp.concatenate([by_z[2], by_z[3]], axis=0)
    rest = {count: along_y(last, count) for count in (1, 3, 2)}

    def flag(*conditions):
        return jnp.stack([jnp.asarray(value, jnp.int32) for value in conditions])

    state = attend_first(core, queries, pair, kv)
    state = attend_more(
        flag(z >= 1, z >= 2, z >= 3, y >= 1, y >= 2, y >= 3),
        queries,
        pair,
        state,
        [by_z[1], by_z[2], by_z[3], zero[1], zero[2], zero[3]],
    )
    state = attend_more(
        flag(y >= 1, y >= 2, y >= 3), queries, pair, state, [one[1], one[2], one[3]]
    )
    state = attend_more(
        flag(y >= 1, y >= 1, y >= 3, y >= 3), queries, pair, state, [rest[1], rest[3]]
    )
    own, sent = attend_more(
        flag(y >= 2, y >= 2), queries, pair, state, [rest[2]], split=True
    )
    got = other_core(sent)

    page = jnp.concatenate([pages_of(targets, me), pages_of(targets, me ^ 1)])
    source = page // PAGES
    by_y = (y - source // 8) % 4
    by_zz = (z - (source // 2) % 4) % 4
    held = source % 2 == core
    code = jnp.where(by_y == 0, by_zz, jnp.minimum(by_zz, 2) * 3 + 3 + by_y)
    offset = jnp.where((by_y > 0) & (by_zz == 3), BLK, 0)
    row = offset + (page % PAGES) // 2 * 2 * PAGE
    arrays = [by_z[count] for count in range(4)]
    for group in (zero, one, rest):
        arrays += [group[count] for count in (1, 2, 3)]
    own_pages, sent_pages = fetch_pages(code, row, page % 2, arrays)
    got_pages = other_core(sent_pages)
    attention = finish(own, got)
    keep = held[:PAGES].reshape(PAGES, 1, 1, 1)
    shape = (PAGES, PAGE, 2, HD)
    kv_cache = jnp.where(keep, own_pages.reshape(shape), got_pages.reshape(shape))
    return attention, kv_cache


def on_device(
    features,
    conv_weight,
    conv_bias,
    embed_weight,
    position_table,
    norm_gain,
    qkv_weight,
    page_owner,
    page_slot,
):
    me = lax.axis_index("seq").astype(jnp.int32)
    tensor = lax.axis_index("tensor").astype(jnp.int32)
    tensor_count = lax.axis_size("tensor")
    weight = lax.all_gather(qkv_weight, "seq", axis=0, tiled=True)
    parts = partial_latents(features, conv_weight)
    own = parts[: FRAMES * EXT].reshape(FRAMES, EXT * LAT)
    target = (page_owner * PAGES + page_slot).astype(jnp.float32)
    target = jnp.broadcast_to(target, (FRAMES, PAGES))
    message = jnp.concatenate([own, target], axis=1)
    message = jnp.pad(message, ((0, 0), (0, 512 - message.shape[1])))
    message = jnp.broadcast_to(message[:, None], (FRAMES, SEQ // FRAMES, 512)).reshape(SEQ, 512)
    message = lax.all_to_all(message, "seq", split_axis=0, concat_axis=0, tiled=True)
    targets = message[:, EXT * LAT : EXT * LAT + PAGES].astype(jnp.int32).reshape(-1)
    offset = tensor - me % (SEQ // FRAMES)
    latent = place_latents(message[:, : EXT * LAT].reshape(SEQ * EXT, LAT), offset)
    for bit in (1, 2, 4):
        swap = [(i, i ^ bit) for i in range(tensor_count)]
        latent = latent + lax.ppermute(latent, "tensor", swap)
    normed = normed_hidden(latent, conv_bias, embed_weight, position_table, norm_gain)
    qkv = jnp.dot(normed, weight, preferred_element_type=jnp.float32).astype(jnp.bfloat16)
    return attention_and_pages(me, targets, qkv)


def solution(mesh):
    placed = (
        P(None, "tensor", "seq", None),
        P(),
        P(),
        P(),
        P("seq", None),
        P(),
        P("seq", "tensor"),
        P("seq"),
        P("seq"),
    )
    return jax.shard_map(
        on_device,
        mesh=mesh,
        in_specs=placed,
        out_specs=(P("seq", "tensor"), P("seq", None, None, "tensor")),
        check_vma=False,
    )
```

```python
import functools

import jax
import jax.numpy as jnp
import numpy as np
from jax import lax
from jax.experimental import pallas as pl
from jax.experimental.pallas import tpu as pltpu
from jax.sharding import PartitionSpec as P

HD = 128
PAGE = 8
GROUP = 4
LAT = 16
BLK = 320
PAGES = 40
MOST = 3
SEQ = 32
ROWS = 5
COLS = 2
FRAMES = 4
EXT = (ROWS + 2) * (COLS + 2)
TOK = 384
TILE = 256
QROWS = GROUP * BLK
STATE = HD + 8
VMEM = 24 * 1024 * 1024


def params(**extra):
    return pltpu.CompilerParams(vmem_limit_bytes=VMEM, **extra)


def cost(blocks):
    scores = blocks * 2 * QROWS * BLK
    return pl.CostEstimate(flops=4 * HD * scores, bytes_accessed=3 << 20, transcendentals=scores)


def roll_lanes(value, shift):
    shift = shift % value.shape[1]
    return pltpu.roll(value, shift, 1) if shift else value


def conv_kernel(feat_ref, weight_ref, out_ref, grid_ref):
    grid_ref[...] = jnp.zeros_like(grid_ref)
    for frame in range(FRAMES):
        for row in range(ROWS):
            start = frame * EXT + (row + 1) * (COLS + 2) + 1
            value = feat_ref[frame, row].astype(jnp.float32)
            grid_ref[start : start + COLS, :] = value / (1.0 + jnp.exp(-value))
    active = grid_ref[...].astype(jnp.bfloat16)
    product = lax.dot_general(
        weight_ref[...], active, (((1,), (1,)), ((), ())), preferred_element_type=jnp.float32
    )
    lane = lax.broadcasted_iota(jnp.int32, (LAT, 128), 1)
    total = jnp.zeros((LAT, 128), jnp.float32)
    for time in range(3):
        part = jnp.zeros((LAT, 128), jnp.float32)
        for row in range(3):
            for col in range(3):
                index = (time * 3 + row) * 3 + col
                piece = product[index * LAT : (index + 1) * LAT, :]
                part = part + roll_lanes(piece, -((row - 1) * (COLS + 2) + col - 1))
        delay = (2 - time) * EXT
        if delay:
            part = jnp.where(lane >= delay, roll_lanes(part, delay), 0.0)
        total = total + part
    padded = jnp.concatenate([total, jnp.zeros((128 - LAT, 128), jnp.float32)], axis=0)
    out_ref[...] = jnp.transpose(padded)[:, :LAT]


def partial_latents(features, conv_weight):
    weight = jnp.transpose(conv_weight, (0, 1, 2, 4, 3)).reshape(-1, conv_weight.shape[3])
    return pl.pallas_call(
        conv_kernel,
        out_shape=jax.ShapeDtypeStruct((128, LAT), jnp.float32),
        scratch_shapes=[pltpu.VMEM((128, features.shape[-1]), jnp.float32)],
        compiler_params=params(),
        name="conv",
    )(features, weight)


def split_three(value):
    high = value.astype(jnp.bfloat16)
    rest = value - high.astype(jnp.float32)
    middle = rest.astype(jnp.bfloat16)
    low = (rest - middle.astype(jnp.float32)).astype(jnp.bfloat16)
    return high, middle, low


def place_kernel(parts_ref, token_ref, out_ref):
    count = parts_ref.shape[0]
    token = lax.broadcasted_iota(jnp.int32, (count, TOK), 1)
    pick = jnp.where(token == token_ref[...], 1.0, 0.0).astype(jnp.bfloat16)
    total = jnp.zeros((LAT, TOK), jnp.float32)
    for part in reversed(split_three(parts_ref[...])):
        total = total + lax.dot_general(
            part, pick, (((0,), (0,)), ((), ())), preferred_element_type=jnp.float32
        )
    out_ref[...] = total


def place_table():
    table = np.full((3, SEQ, ROWS + 2, COLS + 2), -1, np.int32)
    for case in range(3):
        for source in range(SEQ):
            for row in range(ROWS + 2):
                for col in range(COLS + 2):
                    height = row - 1 + ROWS * (case - 1)
                    width = source * COLS - 1 + col
                    if 0 <= height < ROWS and 0 <= width < SEQ * COLS:
                        table[case, source, row, col] = height * SEQ * COLS + width
    return table.reshape(3, SEQ * EXT, 1)


def place_latents(parts, offset):
    table = jnp.asarray(place_table())
    token = lax.dynamic_index_in_dim(table, jnp.clip(offset + 1, 0, 2), 0, keepdims=False)
    token = jnp.where(jnp.abs(offset) <= 1, token, -1)
    return pl.pallas_call(
        place_kernel,
        out_shape=jax.ShapeDtypeStruct((LAT, TOK), jnp.float32),
        compiler_params=params(),
        name="place",
    )(parts, token)


def hidden_kernel(latent_ref, bias_ref, embed_ref, table_ref, gain_ref, out_ref, hid_ref, sq_ref):
    step = pl.program_id(0)
    width = table_ref.shape[1]
    latent = latent_ref[...][:, :BLK] + bias_ref[...]
    latent = jnp.concatenate(split_three(latent), axis=0)
    embed = embed_ref[...]
    hidden = lax.dot_general(
        latent,
        jnp.concatenate([embed, embed, embed], axis=0),
        (((0,), (0,)), ((), ())),
        preferred_element_type=jnp.float32,
    ) + table_ref[...].astype(jnp.float32)
    hid_ref[step] = hidden
    squares = jnp.zeros((BLK, 128), jnp.float32)
    for lane in range(0, width, 128):
        piece = hidden[:, lane : lane + 128]
        squares = squares + piece * piece

    @pl.when(step == 0)
    def _():
        sq_ref[...] = squares

    @pl.when(step > 0)
    def _():
        sq_ref[...] += squares

    @pl.when(step == pl.num_programs(0) - 1)
    def _():
        count = hid_ref.shape[0]
        mean = jnp.sum(sq_ref[...], axis=1, keepdims=True) / (count * width)
        factor = lax.rsqrt(mean + 1e-05)
        for tile in range(count):
            cut = slice(tile * width, (tile + 1) * width)
            gain = gain_ref[:, cut].astype(jnp.float32)
            out_ref[:, cut] = (hid_ref[tile] * factor * gain).astype(jnp.bfloat16)


def normed_hidden(latent, conv_bias, embed_weight, position_table, norm_gain):
    depth = position_table.shape[1]
    steps = 8
    width = depth // steps
    return pl.pallas_call(
        hidden_kernel,
        grid=(steps,),
        in_specs=[
            pl.BlockSpec((LAT, TOK), lambda i: (0, 0)),
            pl.BlockSpec((LAT, 1), lambda i: (0, 0)),
            pl.BlockSpec((LAT, width), lambda i: (0, i)),
            pl.BlockSpec((BLK, width), lambda i: (0, i)),
            pl.BlockSpec((1, depth), lambda i: (0, 0)),
        ],
        out_specs=pl.BlockSpec((BLK, depth), lambda i: (0, 0)),
        out_shape=jax.ShapeDtypeStruct((BLK, depth), jnp.bfloat16),
        scratch_shapes=[
            pltpu.VMEM((steps, BLK, width), jnp.float32),
            pltpu.VMEM((BLK, 128), jnp.float32),
        ],
        compiler_params=params(dimension_semantics=("arbitrary",)),
        name="hidden",
    )(latent, conv_bias.reshape(LAT, 1), embed_weight, position_table, norm_gain.reshape(1, depth))


def attend_block(masked, partner_full, keys, values, q_ref, state_ref):
    scale = 1.4426950408889634 / HD**0.5
    tiles = 2 * QROWS // TILE

    def score(tile):
        return lax.dot_general(
            keys,
            q_ref[tile * TILE : (tile + 1) * TILE, :],
            (((1,), (1,)), ((), ())),
            preferred_element_type=jnp.float32,
        )

    upcoming = score(0)
    for tile in range(tiles):
        scores = upcoming
        if tile + 1 < tiles:
            upcoming = score(tile + 1)
        cut = slice(tile * TILE, (tile + 1) * TILE)
        allowed = None
        if masked:
            key = lax.broadcasted_iota(jnp.int32, scores.shape, 0)
            query = tile * TILE + lax.broadcasted_iota(jnp.int32, (1, TILE), 1)
            if tile * TILE >= QROWS:
                query = jnp.where(partner_full, BLK, -1) + 0 * query
            else:
                for head in range(GROUP - 1, 0, -1):
                    query = jnp.where(query >= head * BLK, query - head * BLK, query)
            allowed = key <= query
            scores = jnp.where(allowed, scores, -1e30)
        peak = jnp.max(scores, axis=0, keepdims=True)
        if masked:
            best = peak
        else:
            old = state_ref[HD : HD + 1, cut]
            best = jnp.maximum(old, peak)
            factor = jnp.exp2((old - best) * scale)
        weights = jnp.exp2((scores - best) * scale)
        if masked:
            weights = jnp.where(allowed, weights, 0.0)
        total = jnp.sum(weights, axis=0, keepdims=True)
        summed = lax.dot_general(
            values,
            weights.astype(jnp.bfloat16),
            (((0,), (0,)), ((), ())),
            preferred_element_type=jnp.float32,
        )
        if not masked:
            total = total + state_ref[HD + 1 : HD + 2, cut] * factor
            summed = summed + state_ref[:HD, cut] * factor
        state_ref[HD : HD + 1, cut] = best
        state_ref[HD + 1 : HD + 2, cut] = total
        state_ref[:HD, cut] = summed


def set_queries(own_ref, pair_ref, q_ref):
    for index, ref in enumerate((own_ref, pair_ref)):
        for head in range(GROUP):
            start = (index * GROUP + head) * BLK
            q_ref[start : start + BLK, :] = ref[:, head * HD : (head + 1) * HD]


def first_kernel(core_ref, own_ref, pair_ref, kv_ref, state_ref, q_ref):
    set_queries(own_ref, pair_ref, q_ref)
    state_ref[HD + 2 :, :] = jnp.zeros((STATE - HD - 2, 2 * QROWS), jnp.float32)
    attend_block(True, core_ref[0] == 0, kv_ref[:, :HD], kv_ref[:, HD:], q_ref, state_ref)


def attend_first(core, own, pair, kv):
    return pl.pallas_call(
        first_kernel,
        in_specs=[pl.BlockSpec(memory_space=pltpu.SMEM)]
        + [pl.BlockSpec(memory_space=pltpu.VMEM)] * 3,
        out_shape=jax.ShapeDtypeStruct((STATE, 2 * QROWS), jnp.float32),
        scratch_shapes=[pltpu.VMEM((2 * QROWS, HD), jnp.bfloat16)],
        compiler_params=params(),
        cost_estimate=cost(1),
        name="first",
    )(core.reshape(1), own, pair, kv)


def more_kernel(unit, count, split, flag_ref, own_ref, pair_ref, state_ref, *rest):
    arrays, rest = rest[:count], rest[count:]
    if split:
        own_out_ref, pair_out_ref, q_ref, held_ref, sems, work_ref = rest
    else:
        work_ref, q_ref, held_ref, sems = rest
    copies = []
    for index, array in enumerate(arrays):
        copies.append(pltpu.make_async_copy(array, held_ref.at[index], sems.at[index]))
        copies[-1].start()
    set_queries(own_ref, pair_ref, q_ref)
    work_ref[...] = state_ref[...]
    for copy in copies:
        copy.wait()

    def body(index, carry):
        @pl.when(flag_ref[index] != 0)
        def _():
            keys, values = held_ref[index, :, :HD], held_ref[index, :, HD:]
            attend_block(False, None, keys, values, q_ref, work_ref)

        return carry

    lax.fori_loop(0, count, body, 0)
    if split:
        own_out_ref[...] = work_ref[:, :QROWS]
        pair_out_ref[...] = work_ref[:, QROWS:]


def attend_more(flags, own, pair, state, arrays, split=False):
    unit, count = arrays[0].shape[0], len(arrays)
    half = jax.ShapeDtypeStruct((STATE, QROWS), jnp.float32)
    whole = jax.ShapeDtypeStruct((STATE, 2 * QROWS), jnp.float32)
    scratch = [
        pltpu.VMEM((2 * QROWS, HD), jnp.bfloat16),
        pltpu.VMEM((count, unit, 2 * HD), jnp.bfloat16),
        pltpu.SemaphoreType.DMA((count,)),
    ]
    if split:
        scratch.append(pltpu.VMEM((STATE, 2 * QROWS), jnp.float32))
    return pl.pallas_call(
        functools.partial(more_kernel, unit, count, split),
        in_specs=[pl.BlockSpec(memory_space=pltpu.SMEM)]
        + [pl.BlockSpec(memory_space=pltpu.VMEM)] * 3
        + [pl.BlockSpec(memory_space=pl.ANY)] * count,
        out_shape=(half, half) if split else whole,
        scratch_shapes=scratch,
        compiler_params=params(),
        cost_estimate=cost(count * unit // BLK),
        name="more",
    )(flags, own, pair, state, *arrays)


def finish_kernel(own_ref, got_ref, out_ref, row_ref):
    scale = 1.4426950408889634 / HD**0.5
    for start in range(0, QROWS, TILE):
        cut = slice(start, start + TILE)
        first, second = own_ref[HD : HD + 1, cut], got_ref[HD : HD + 1, cut]
        best = jnp.maximum(first, second)
        first = jnp.exp2((first - best) * scale)
        second = jnp.exp2((second - best) * scale)
        total = own_ref[HD + 1 : HD + 2, cut] * first + got_ref[HD + 1 : HD + 2, cut] * second
        summed = own_ref[:HD, cut] * first + got_ref[:HD, cut] * second
        row_ref[cut, :] = jnp.transpose(summed / total)
    for head in range(GROUP):
        rows = row_ref[head * BLK : (head + 1) * BLK, :]
        out_ref[:, head * HD : (head + 1) * HD] = rows.astype(jnp.bfloat16)


def finish(own, got):
    return pl.pallas_call(
        finish_kernel,
        out_shape=jax.ShapeDtypeStruct((BLK, GROUP * HD), jnp.bfloat16),
        scratch_shapes=[pltpu.VMEM((QROWS, HD), jnp.float32)],
        compiler_params=params(),
        name="finish",
    )(own, got)


def page_kernel(place_ref, code_ref, *rest):
    arrays, (own_ref, pair_ref, held_ref) = rest[:-3], rest[-3:]
    held_ref[...] = jnp.zeros_like(held_ref)
    y, z, core = place_ref[0], place_ref[1], place_ref[2]
    for by_y in range(4):
        for by_z in range(4):
            if by_y == 0:
                array, base = arrays[by_z], 0
            else:
                array, base = arrays[3 + by_y + by_z // 2 * 3], by_z % 2 * BLK
            source = (((y - by_y) & 3) * 4 + ((z - by_z) & 3)) * 2 + core
            for entry in range(2 * MOST):
                code = code_ref[source * 2 * MOST + entry]

                @pl.when(code >= 0)
                def _():
                    page = code >> 6
                    slot = (code & 63) + entry // MOST * PAGES
                    row = pl.multiple_of(base + (page >> 1) * 2 * PAGE, 2 * PAGE)
                    rows = array[pl.ds(row, 2 * PAGE), :].astype(jnp.float32)
                    rows = jnp.where((page & 1) == 1, rows[PAGE:], rows[:PAGE])
                    held_ref[pl.ds(pl.multiple_of(slot * PAGE, PAGE), PAGE), :] = rows

    own_ref[...] = held_ref[: PAGES * PAGE].astype(jnp.bfloat16)
    pair_ref[...] = held_ref[PAGES * PAGE :].astype(jnp.bfloat16)


def fetch_pages(place, codes, arrays):
    out = jax.ShapeDtypeStruct((PAGES * PAGE, 2 * HD), jnp.bfloat16)
    return pl.pallas_call(
        page_kernel,
        in_specs=[pl.BlockSpec(memory_space=pltpu.SMEM)] * 2
        + [pl.BlockSpec(memory_space=pltpu.VMEM)] * len(arrays),
        out_shape=(out, out),
        scratch_shapes=[pltpu.VMEM((2 * PAGES * PAGE, 2 * HD), jnp.float32)],
        compiler_params=params(),
        name="pages",
    )(place, codes, *arrays)


def moves(step):
    pairs = []
    for y in range(4):
        for z in range(4):
            for core in range(2):
                to_y, to_z, to_core = step(y, z, core)
                pairs.append(((y * 4 + z) * 2 + core, (to_y * 4 + to_z) * 2 + to_core))
    return pairs


def along_y(value, count):
    return lax.ppermute(value, "seq", moves(lambda y, z, c: ((y + count) % 4, z, c)))


def along_z(value, count):
    return lax.ppermute(value, "seq", moves(lambda y, z, c: (y, (z + count) % 4, c)))


def other_core(value):
    return lax.ppermute(value, "seq", moves(lambda y, z, c: (y, z, 1 - c)))


def page_codes(targets, me):
    index = jnp.arange(PAGES, dtype=jnp.int32)
    codes = []
    for owner in (me, me ^ 1):
        slot = targets - owner * PAGES
        match = (slot >= 0) & (slot < PAGES)
        before = match[:, None, :] & (index[None, :] < index[:, None])
        rank = jnp.sum(before.astype(jnp.int32), axis=2)
        code = index * 64 + slot + 1
        for entry in range(MOST):
            codes.append(jnp.sum(jnp.where(match & (rank == entry), code, 0), axis=1) - 1)
    return jnp.stack(codes, axis=1).reshape(-1)


def held_here(targets, me):
    mine = me * PAGES + jnp.arange(PAGES, dtype=jnp.int32)
    same_core = (jnp.arange(SEQ, dtype=jnp.int32) % 2 == me % 2)[:, None]
    match = (targets[None] == mine[:, None, None]) & same_core[None]
    return jnp.any(match, axis=(1, 2))


def attention_and_pages(me, targets, qkv):
    core, z, y = me % 2, (me // 2) % 4, me // 8
    queries, kv = qkv[:, : GROUP * HD], qkv[:, GROUP * HD :]
    pair = other_core(queries)
    by_z = {0: kv}
    for count in (1, 2, 3):
        by_z[count] = along_z(kv, count)
    near = jnp.concatenate([kv, by_z[1]], axis=0)
    near = {count: along_y(near, count) for count in (1, 3, 2)}
    far = jnp.concatenate([by_z[2], by_z[3]], axis=0)
    far = {count: along_y(far, count) for count in (1, 3, 2)}

    def flag(*conditions):
        return jnp.stack([jnp.asarray(value, jnp.int32) for value in conditions])

    state = attend_first(core, queries, pair, kv)
    state = attend_more(
        flag(z >= 1, z >= 2, z >= 3), queries, pair, state, [by_z[1], by_z[2], by_z[3]]
    )
    state = attend_more(
        flag(y >= 1, y >= 3, y >= 2), queries, pair, state, [near[1], near[3], near[2]]
    )
    state = attend_more(flag(y >= 1, y >= 3), queries, pair, state, [far[1], far[3]])
    own, sent = attend_more(flag(y >= 2), queries, pair, state, [far[2]], split=True)
    got = other_core(sent)

    arrays = [by_z[count] for count in range(4)]
    arrays += [group[count] for group in (near, far) for count in (1, 2, 3)]
    place = jnp.stack([y, z, core])
    own_pages, sent_pages = fetch_pages(place, page_codes(targets, me), arrays)
    got_pages = other_core(sent_pages)
    attention = finish(own, got)
    keep = held_here(targets, me).reshape(PAGES, 1, 1, 1)
    shape = (PAGES, PAGE, 2, HD)
    kv_cache = jnp.where(keep, own_pages.reshape(shape), got_pages.reshape(shape))
    return attention, kv_cache


def on_device(
    features,
    conv_weight,
    conv_bias,
    embed_weight,
    position_table,
    norm_gain,
    qkv_weight,
    page_owner,
    page_slot,
):
    me = lax.axis_index("seq").astype(jnp.int32)
    tensor = lax.axis_index("tensor").astype(jnp.int32)
    tensor_count = lax.axis_size("tensor")
    weight = lax.all_gather(qkv_weight, "seq", axis=0, tiled=True)
    parts = partial_latents(features, conv_weight)
    own = parts[: FRAMES * EXT].reshape(FRAMES, EXT * LAT)
    target = (page_owner * PAGES + page_slot).astype(jnp.float32)
    target = jnp.broadcast_to(target, (FRAMES, PAGES))
    message = jnp.concatenate([own, target], axis=1)
    message = jnp.pad(message, ((0, 0), (0, 512 - message.shape[1])))
    message = jnp.broadcast_to(message[:, None], (FRAMES, SEQ // FRAMES, 512)).reshape(SEQ, 512)
    message = lax.all_to_all(message, "seq", split_axis=0, concat_axis=0, tiled=True)
    targets = message[:, EXT * LAT : EXT * LAT + PAGES].astype(jnp.int32)
    offset = tensor - me % (SEQ // FRAMES)
    latent = place_latents(message[:, : EXT * LAT].reshape(SEQ * EXT, LAT), offset)
    for bit in (1, 2, 4):
        swap = [(i, i ^ bit) for i in range(tensor_count)]
        latent = latent + lax.ppermute(latent, "tensor", swap)
    normed = normed_hidden(latent, conv_bias, embed_weight, position_table, norm_gain)
    qkv = jnp.dot(normed, weight, preferred_element_type=jnp.float32).astype(jnp.bfloat16)
    return attention_and_pages(me, targets, qkv)


def solution(mesh):
    placed = (
        P(None, "tensor", "seq", None),
        P(),
        P(),
        P(),
        P("seq", None),
        P(),
        P("seq", "tensor"),
        P("seq"),
        P("seq"),
    )
    return jax.shard_map(
        on_device,
        mesh=mesh,
        in_specs=placed,
        out_specs=(P("seq", "tensor"), P("seq", None, None, "tensor")),
        check_vma=False,
    )
```

```python
import functools

import jax
import jax.numpy as jnp
import numpy as np
from jax import lax
from jax.experimental import pallas as pl
from jax.experimental.pallas import tpu as pltpu
from jax.sharding import PartitionSpec as P

HD = 128
PAGE = 8
GROUP = 4
LAT = 16
BLK = 320
PAGES = 40
MOST = 3
SEQ = 32
ROWS = 5
COLS = 2
FRAMES = 4
EXT = (ROWS + 2) * (COLS + 2)
TOK = 384
TILE = 256
QROWS = GROUP * BLK
STATE = HD + 8
RBLK = 320
HALF = 3 * HD
VMEM = 24 * 1024 * 1024


def params(**extra):
    return pltpu.CompilerParams(vmem_limit_bytes=VMEM, **extra)


def cost(blocks):
    scores = blocks * 2 * QROWS * BLK
    return pl.CostEstimate(flops=4 * HD * scores, bytes_accessed=3 << 20, transcendentals=scores)


def roll_lanes(value, shift):
    shift = shift % value.shape[1]
    return pltpu.roll(value, shift, 1) if shift else value


def conv_kernel(feat_ref, weight_ref, out_ref, grid_ref):
    grid_ref[...] = jnp.zeros_like(grid_ref)
    for frame in range(FRAMES):
        for row in range(ROWS):
            start = frame * EXT + (row + 1) * (COLS + 2) + 1
            value = feat_ref[frame, row].astype(jnp.float32)
            grid_ref[start : start + COLS, :] = value / (1.0 + jnp.exp(-value))
    active = grid_ref[...].astype(jnp.bfloat16)
    product = lax.dot_general(
        weight_ref[...], active, (((1,), (1,)), ((), ())), preferred_element_type=jnp.float32
    )
    lane = lax.broadcasted_iota(jnp.int32, (LAT, 128), 1)
    total = jnp.zeros((LAT, 128), jnp.float32)
    for time in range(3):
        part = jnp.zeros((LAT, 128), jnp.float32)
        for row in range(3):
            for col in range(3):
                index = (time * 3 + row) * 3 + col
                piece = product[index * LAT : (index + 1) * LAT, :]
                part = part + roll_lanes(piece, -((row - 1) * (COLS + 2) + col - 1))
        delay = (2 - time) * EXT
        if delay:
            part = jnp.where(lane >= delay, roll_lanes(part, delay), 0.0)
        total = total + part
    padded = jnp.concatenate([total, jnp.zeros((128 - LAT, 128), jnp.float32)], axis=0)
    out_ref[...] = jnp.transpose(padded)[:, :LAT]


def partial_latents(features, conv_weight):
    weight = jnp.transpose(conv_weight, (0, 1, 2, 4, 3)).reshape(-1, conv_weight.shape[3])
    return pl.pallas_call(
        conv_kernel,
        out_shape=jax.ShapeDtypeStruct((128, LAT), jnp.float32),
        scratch_shapes=[pltpu.VMEM((128, features.shape[-1]), jnp.float32)],
        compiler_params=params(),
        name="conv",
    )(features, weight)


def split_three(value):
    high = value.astype(jnp.bfloat16)
    rest = value - high.astype(jnp.float32)
    middle = rest.astype(jnp.bfloat16)
    low = (rest - middle.astype(jnp.float32)).astype(jnp.bfloat16)
    return high, middle, low


def place_kernel(parts_ref, token_ref, out_ref):
    count = parts_ref.shape[0]
    token = lax.broadcasted_iota(jnp.int32, (count, TOK), 1)
    pick = jnp.where(token == token_ref[...], 1.0, 0.0).astype(jnp.bfloat16)
    total = jnp.zeros((LAT, TOK), jnp.float32)
    for part in reversed(split_three(parts_ref[...])):
        total = total + lax.dot_general(
            part, pick, (((0,), (0,)), ((), ())), preferred_element_type=jnp.float32
        )
    out_ref[...] = total


def place_table():
    table = np.full((3, SEQ, ROWS + 2, COLS + 2), -1, np.int32)
    for case in range(3):
        for source in range(SEQ):
            for row in range(ROWS + 2):
                for col in range(COLS + 2):
                    height = row - 1 + ROWS * (case - 1)
                    width = source * COLS - 1 + col
                    if 0 <= height < ROWS and 0 <= width < SEQ * COLS:
                        table[case, source, row, col] = height * SEQ * COLS + width
    return table.reshape(3, SEQ * EXT, 1)


def place_latents(parts, offset):
    table = jnp.asarray(place_table())
    token = lax.dynamic_index_in_dim(table, jnp.clip(offset + 1, 0, 2), 0, keepdims=False)
    token = jnp.where(jnp.abs(offset) <= 1, token, -1)
    return pl.pallas_call(
        place_kernel,
        out_shape=jax.ShapeDtypeStruct((LAT, TOK), jnp.float32),
        compiler_params=params(),
        name="place",
    )(parts, token)


def hidden_kernel(latent_ref, bias_ref, embed_ref, table_ref, gain_ref, out_ref, hid_ref, sq_ref):
    step = pl.program_id(0)
    width = table_ref.shape[1]
    latent = latent_ref[...][:, :BLK] + bias_ref[...]
    latent = jnp.concatenate(split_three(latent), axis=0)
    embed = embed_ref[...]
    hidden = lax.dot_general(
        latent,
        jnp.concatenate([embed, embed, embed], axis=0),
        (((0,), (0,)), ((), ())),
        preferred_element_type=jnp.float32,
    ) + table_ref[...].astype(jnp.float32)
    hid_ref[step] = hidden
    squares = jnp.zeros((BLK, 128), jnp.float32)
    for lane in range(0, width, 128):
        piece = hidden[:, lane : lane + 128]
        squares = squares + piece * piece

    @pl.when(step == 0)
    def _():
        sq_ref[...] = squares

    @pl.when(step > 0)
    def _():
        sq_ref[...] += squares

    @pl.when(step == pl.num_programs(0) - 1)
    def _():
        count = hid_ref.shape[0]
        mean = jnp.sum(sq_ref[...], axis=1, keepdims=True) / (count * width)
        factor = lax.rsqrt(mean + 1e-05)
        for tile in range(count):
            gain = gain_ref[:, tile * width : (tile + 1) * width].astype(jnp.float32)
            normed = hid_ref[tile] * factor * gain
            for part in range(width // RBLK):
                piece = normed[:, part * RBLK : (part + 1) * RBLK]
                out_ref[tile * (width // RBLK) + part] = piece.astype(jnp.bfloat16)


def normed_hidden(latent, conv_bias, embed_weight, position_table, norm_gain):
    depth = position_table.shape[1]
    steps = 8
    width = depth // steps
    return pl.pallas_call(
        hidden_kernel,
        grid=(steps,),
        in_specs=[
            pl.BlockSpec((LAT, TOK), lambda i: (0, 0)),
            pl.BlockSpec((LAT, 1), lambda i: (0, 0)),
            pl.BlockSpec((LAT, width), lambda i: (0, i)),
            pl.BlockSpec((BLK, width), lambda i: (0, i)),
            pl.BlockSpec((1, depth), lambda i: (0, 0)),
        ],
        out_specs=pl.BlockSpec((depth // RBLK, BLK, RBLK), lambda i: (0, 0, 0)),
        out_shape=jax.ShapeDtypeStruct((depth // RBLK, BLK, RBLK), jnp.bfloat16),
        scratch_shapes=[
            pltpu.VMEM((steps, BLK, width), jnp.float32),
            pltpu.VMEM((BLK, 128), jnp.float32),
        ],
        compiler_params=params(dimension_semantics=("arbitrary",)),
        name="hidden",
    )(latent, conv_bias.reshape(LAT, 1), embed_weight, position_table, norm_gain.reshape(1, depth))


def halve_kernel(core_ref, weight_ref, out_ref):
    for core in range(2):

        @pl.when(core_ref[0] == core)
        def _():
            out_ref[:, : 2 * HD] = weight_ref[:, core * 2 * HD : (core + 1) * 2 * HD]
            out_ref[:, 2 * HD :] = weight_ref[:, (GROUP + core) * HD : (GROUP + core + 1) * HD]


def halve(core, weight):
    return pl.pallas_call(
        halve_kernel,
        in_specs=[
            pl.BlockSpec(memory_space=pltpu.SMEM),
            pl.BlockSpec(memory_space=pltpu.VMEM),
        ],
        out_shape=jax.ShapeDtypeStruct((weight.shape[0], HALF), jnp.bfloat16),
        compiler_params=params(),
        name="halve",
    )(core.reshape(1), weight)


def project_kernel(sizes, last, index_ref, own_ref, pair_ref, *rest):
    arrays, rest = rest[: len(sizes)], rest[len(sizes) :]
    if last:
        before_ref, out_ref, held_ref, sems, sum_ref = rest
    else:
        sum_ref, held_ref, sems = rest
    copies = []
    first = 0
    for index, size in enumerate(sizes):
        held = held_ref.at[pl.ds(first * RBLK, size * RBLK), :]
        copies.append(pltpu.make_async_copy(arrays[index], held, sems.at[index]))
        copies[-1].start()
        first += size
    if last:
        sum_ref[...] = before_ref[...]
    else:
        sum_ref[...] = jnp.zeros_like(sum_ref)
    for copy in copies:
        copy.wait()

    def body(block, carry):
        weight = held_ref[pl.ds(pl.multiple_of(block * RBLK, RBLK), RBLK), :]
        for part, ref in enumerate((own_ref, pair_ref)):
            cut = slice(part * BLK, (part + 1) * BLK)
            sum_ref[cut, :] += jnp.dot(
                ref[index_ref[block]], weight, preferred_element_type=jnp.float32
            )
        return carry

    lax.fori_loop(0, sum(sizes), body, 0)
    if last:
        out_ref[...] = sum_ref[...].astype(jnp.bfloat16)


def project(index, own, pair, arrays, before=None):
    sizes = tuple(array.shape[0] // RBLK for array in arrays)
    last = before is not None
    kind = jnp.bfloat16 if last else jnp.float32
    scratch = [
        pltpu.VMEM((sum(sizes) * RBLK, HALF), jnp.bfloat16),
        pltpu.SemaphoreType.DMA((len(sizes),)),
    ]
    if last:
        scratch.append(pltpu.VMEM((2 * BLK, HALF), jnp.float32))
    vmem = pl.BlockSpec(memory_space=pltpu.VMEM)
    return pl.pallas_call(
        functools.partial(project_kernel, sizes, last),
        in_specs=[pl.BlockSpec(memory_space=pltpu.SMEM), vmem, vmem]
        + [pl.BlockSpec(memory_space=pl.ANY)] * len(arrays)
        + [vmem] * last,
        out_shape=jax.ShapeDtypeStruct((2 * BLK, HALF), kind),
        scratch_shapes=scratch,
        compiler_params=params(),
        cost_estimate=pl.CostEstimate(
            flops=4 * BLK * HALF * RBLK * sum(sizes), bytes_accessed=8 << 20, transcendentals=0
        ),
        name="project",
    )(index, own, pair, *arrays, *([before] if last else []))


def attend_block(masked, partner_full, keys, values, q_ref, state_ref):
    scale = 1.4426950408889634 / HD**0.5
    tiles = 2 * QROWS // TILE

    def score(tile):
        return lax.dot_general(
            keys,
            q_ref[tile * TILE : (tile + 1) * TILE, :],
            (((1,), (1,)), ((), ())),
            preferred_element_type=jnp.float32,
        )

    upcoming = score(0)
    for tile in range(tiles):
        scores = upcoming
        if tile + 1 < tiles:
            upcoming = score(tile + 1)
        cut = slice(tile * TILE, (tile + 1) * TILE)
        allowed = None
        if masked:
            key = lax.broadcasted_iota(jnp.int32, scores.shape, 0)
            query = tile * TILE + lax.broadcasted_iota(jnp.int32, (1, TILE), 1)
            if tile * TILE >= QROWS:
                query = jnp.where(partner_full, BLK, -1) + 0 * query
            else:
                for head in range(GROUP - 1, 0, -1):
                    query = jnp.where(query >= head * BLK, query - head * BLK, query)
            allowed = key <= query
            scores = jnp.where(allowed, scores, -1e30)
        peak = jnp.max(scores, axis=0, keepdims=True)
        if masked:
            best = peak
        else:
            old = state_ref[HD : HD + 1, cut]
            best = jnp.maximum(old, peak)
            factor = jnp.exp2((old - best) * scale)
        weights = jnp.exp2((scores - best) * scale)
        if masked:
            weights = jnp.where(allowed, weights, 0.0)
        total = jnp.sum(weights, axis=0, keepdims=True)
        summed = lax.dot_general(
            values,
            weights.astype(jnp.bfloat16),
            (((0,), (0,)), ((), ())),
            preferred_element_type=jnp.float32,
        )
        if not masked:
            total = total + state_ref[HD + 1 : HD + 2, cut] * factor
            summed = summed + state_ref[:HD, cut] * factor
        state_ref[HD : HD + 1, cut] = best
        state_ref[HD + 1 : HD + 2, cut] = total
        state_ref[:HD, cut] = summed


def set_queries(core_ref, mine_ref, theirs_ref, q_ref):
    for core in range(2):

        @pl.when(core_ref[0] == core)
        def _():
            for index in range(2):
                for head in range(GROUP):
                    start = (index * GROUP + head) * BLK
                    lanes = slice(head % 2 * HD, (head % 2 + 1) * HD)
                    if head // 2 == core:
                        rows = mine_ref[index * BLK : (index + 1) * BLK, lanes]
                    else:
                        rows = theirs_ref[(1 - index) * BLK : (2 - index) * BLK, lanes]
                    q_ref[start : start + BLK, :] = rows


def first_kernel(core_ref, mine_ref, theirs_ref, kv_ref, state_ref, q_ref):
    set_queries(core_ref, mine_ref, theirs_ref, q_ref)
    state_ref[HD + 2 :, :] = jnp.zeros((STATE - HD - 2, 2 * QROWS), jnp.float32)
    attend_block(True, core_ref[0] == 0, kv_ref[:, :HD], kv_ref[:, HD:], q_ref, state_ref)


def attend_first(core, mine, theirs, kv):
    return pl.pallas_call(
        first_kernel,
        in_specs=[pl.BlockSpec(memory_space=pltpu.SMEM)]
        + [pl.BlockSpec(memory_space=pltpu.VMEM)] * 3,
        out_shape=(
            jax.ShapeDtypeStruct((STATE, 2 * QROWS), jnp.float32),
            jax.ShapeDtypeStruct((2 * QROWS, HD), jnp.bfloat16),
        ),
        compiler_params=params(),
        cost_estimate=cost(1),
        name="first",
    )(core.reshape(1), mine, theirs, kv)


def more_kernel(count, split, flag_ref, q_ref, state_ref, *rest):
    arrays, rest = rest[:count], rest[count:]
    if split:
        own_out_ref, pair_out_ref, held_ref, sems, work_ref = rest
    else:
        work_ref, held_ref, sems = rest
    copies = []
    for index, array in enumerate(arrays):
        copies.append(pltpu.make_async_copy(array, held_ref.at[index], sems.at[index]))
        copies[-1].start()
    work_ref[...] = state_ref[...]
    for copy in copies:
        copy.wait()

    def body(index, carry):
        @pl.when(flag_ref[index] != 0)
        def _():
            keys, values = held_ref[index, :, :HD], held_ref[index, :, HD:]
            attend_block(False, None, keys, values, q_ref, work_ref)

        return carry

    lax.fori_loop(0, count, body, 0)
    if split:
        own_out_ref[...] = work_ref[:, :QROWS]
        pair_out_ref[...] = work_ref[:, QROWS:]


def attend_more(flags, queries, state, arrays, split=False):
    unit, count = arrays[0].shape[0], len(arrays)
    half = jax.ShapeDtypeStruct((STATE, QROWS), jnp.float32)
    whole = jax.ShapeDtypeStruct((STATE, 2 * QROWS), jnp.float32)
    scratch = [
        pltpu.VMEM((count, unit, 2 * HD), jnp.bfloat16),
        pltpu.SemaphoreType.DMA((count,)),
    ]
    if split:
        scratch.append(pltpu.VMEM((STATE, 2 * QROWS), jnp.float32))
    return pl.pallas_call(
        functools.partial(more_kernel, count, split),
        in_specs=[pl.BlockSpec(memory_space=pltpu.SMEM)]
        + [pl.BlockSpec(memory_space=pltpu.VMEM)] * 2
        + [pl.BlockSpec(memory_space=pl.ANY)] * count,
        out_shape=(half, half) if split else whole,
        scratch_shapes=scratch,
        compiler_params=params(),
        cost_estimate=cost(count * unit // BLK),
        name="more",
    )(flags, queries, state, *arrays)


def finish_kernel(own_ref, got_ref, out_ref, row_ref):
    scale = 1.4426950408889634 / HD**0.5
    for start in range(0, QROWS, TILE):
        cut = slice(start, start + TILE)
        first, second = own_ref[HD : HD + 1, cut], got_ref[HD : HD + 1, cut]
        best = jnp.maximum(first, second)
        first = jnp.exp2((first - best) * scale)
        second = jnp.exp2((second - best) * scale)
        total = own_ref[HD + 1 : HD + 2, cut] * first + got_ref[HD + 1 : HD + 2, cut] * second
        summed = own_ref[:HD, cut] * first + got_ref[:HD, cut] * second
        row_ref[cut, :] = jnp.transpose(summed / total)
    for head in range(GROUP):
        rows = row_ref[head * BLK : (head + 1) * BLK, :]
        out_ref[:, head * HD : (head + 1) * HD] = rows.astype(jnp.bfloat16)


def finish(own, got):
    return pl.pallas_call(
        finish_kernel,
        out_shape=jax.ShapeDtypeStruct((BLK, GROUP * HD), jnp.bfloat16),
        scratch_shapes=[pltpu.VMEM((QROWS, HD), jnp.float32)],
        compiler_params=params(),
        name="finish",
    )(own, got)


def page_kernel(place_ref, code_ref, *rest):
    count = (len(rest) - 4) // 2
    remote, own_ref, pair_ref = rest[:count], rest[count], rest[count + 1]
    held_ref, sems, arrays = rest[count + 2], rest[count + 3], rest[count + 4 :]
    copies = [
        pltpu.make_async_copy(remote[index], arrays[index], sems.at[index])
        for index in range(count)
    ]
    for copy in copies:
        copy.start()
    held_ref[...] = jnp.zeros_like(held_ref)
    for copy in copies:
        copy.wait()
    y, z, core = place_ref[0], place_ref[1], place_ref[2]
    for by_y in range(4):
        for by_z in range(4):
            if by_y == 0:
                array, base = arrays[by_z], 0
            else:
                array, base = arrays[3 + by_y + by_z // 2 * 3], by_z % 2 * BLK
            source = (((y - by_y) & 3) * 4 + ((z - by_z) & 3)) * 2 + core
            for entry in range(2 * MOST):
                code = code_ref[source * 2 * MOST + entry]

                @pl.when(code >= 0)
                def _():
                    page = code >> 6
                    slot = (code & 63) + entry // MOST * PAGES
                    row = pl.multiple_of(base + (page >> 1) * 2 * PAGE, 2 * PAGE)
                    rows = array[pl.ds(row, 2 * PAGE), :].astype(jnp.float32)
                    rows = jnp.where((page & 1) == 1, rows[PAGE:], rows[:PAGE])
                    held_ref[pl.ds(pl.multiple_of(slot * PAGE, PAGE), PAGE), :] = rows

    own_ref[...] = held_ref[: PAGES * PAGE].astype(jnp.bfloat16)
    pair_ref[...] = held_ref[PAGES * PAGE :].astype(jnp.bfloat16)


def fetch_pages(place, codes, arrays):
    out = jax.ShapeDtypeStruct((PAGES * PAGE, 2 * HD), jnp.bfloat16)
    return pl.pallas_call(
        page_kernel,
        in_specs=[pl.BlockSpec(memory_space=pltpu.SMEM)] * 2
        + [pl.BlockSpec(memory_space=pl.ANY)] * len(arrays),
        out_shape=(out, out),
        scratch_shapes=[
            pltpu.VMEM((2 * PAGES * PAGE, 2 * HD), jnp.float32),
            pltpu.SemaphoreType.DMA((len(arrays),)),
        ]
        + [pltpu.VMEM(array.shape, array.dtype) for array in arrays],
        compiler_params=params(),
        name="pages",
    )(place, codes, *arrays)


def moves(step):
    pairs = []
    for y in range(4):
        for z in range(4):
            for core in range(2):
                to_y, to_z, to_core = step(y, z, core)
                pairs.append(((y * 4 + z) * 2 + core, (to_y * 4 + to_z) * 2 + to_core))
    return pairs


def along_y(value, count):
    return lax.ppermute(value, "seq", moves(lambda y, z, c: ((y + count) % 4, z, c)))


def along_z(value, count):
    return lax.ppermute(value, "seq", moves(lambda y, z, c: (y, (z + count) % 4, c)))


def other_core(value):
    return lax.ppermute(value, "seq", moves(lambda y, z, c: (y, z, 1 - c)))


def page_codes(targets, me):
    index = jnp.arange(PAGES, dtype=jnp.int32)
    codes = []
    for owner in (me, me ^ 1):
        slot = targets - owner * PAGES
        match = (slot >= 0) & (slot < PAGES)
        before = match[:, None, :] & (index[None, :] < index[:, None])
        rank = jnp.sum(before.astype(jnp.int32), axis=2)
        code = index * 64 + slot + 1
        for entry in range(MOST):
            codes.append(jnp.sum(jnp.where(match & (rank == entry), code, 0), axis=1) - 1)
    return jnp.stack(codes, axis=1).reshape(-1)


def held_here(targets, me):
    mine = me * PAGES + jnp.arange(PAGES, dtype=jnp.int32)
    same_core = (jnp.arange(SEQ, dtype=jnp.int32) % 2 == me % 2)[:, None]
    match = (targets[None] == mine[:, None, None]) & same_core[None]
    return jnp.any(match, axis=(1, 2))


def spread(value, groups):
    by_z = {0: value}
    for count in (1, 2, 3):
        by_z[count] = along_z(value, count)
    by_y = []
    for group in groups:
        parts = [by_z[count] for count in group]
        parts = jnp.concatenate(parts, axis=0) if len(parts) > 1 else parts[0]
        by_y.append({count: along_y(parts, count) for count in (1, 3, 2)})
    return by_z, by_y


def half_weight(me, weight):
    groups = [[2 * i, 2 * i + 1] for i in range(SEQ // 2)]
    weight = lax.all_gather(weight, "seq", axis=0, tiled=True, axis_index_groups=groups)
    return halve(me % 2, weight)


def project_all(me, weight, own, pair):
    z, y = (me // 2) % 4, me // 8
    by_z, (zero, one, far) = weight

    def index(*blocks):
        return jnp.stack([((y - by_y) & 3) * 4 + ((z - by_zz) & 3) for by_y, by_zz in blocks])

    blocks = [(0, 0), (0, 1), (0, 2), (0, 3)] + [(k, i) for i in (0, 1) for k in (1, 3, 2)]
    arrays = [by_z[count] for count in range(4)]
    arrays += [group[count] for group in (zero, one) for count in (1, 3, 2)]
    before = project(index(*blocks), own, pair, arrays)
    blocks = [(k, i) for k in (1, 3, 2) for i in (2, 3)]
    arrays = [far[count] for count in (1, 3, 2)]
    return project(index(*blocks), own, pair, arrays, before)


def attention_and_pages(me, targets, qkv):
    core, z, y = me % 2, (me // 2) % 4, me // 8
    mine = qkv[:, : 2 * HD]
    keep, sent = qkv[:BLK, 2 * HD :], qkv[BLK:, 2 * HD :]
    got = other_core(sent)
    theirs = other_core(mine)
    low, high = jnp.where(core == 0, keep, got), jnp.where(core == 0, got, keep)
    kv = jnp.concatenate([low, high], axis=1)
    by_z, (near, far) = spread(kv, ((0, 1), (2, 3)))

    def flag(*conditions):
        return jnp.stack([jnp.asarray(value, jnp.int32) for value in conditions])

    state, queries = attend_first(core, mine, theirs, kv)
    state = attend_more(
        flag(z >= 1, z >= 2, z >= 3), queries, state, [by_z[1], by_z[2], by_z[3]]
    )
    state = attend_more(
        flag(y >= 1, y >= 3, y >= 2), queries, state, [near[1], near[3], near[2]]
    )
    state = attend_more(flag(y >= 1, y >= 3), queries, state, [far[1], far[3]])
    own, sent = attend_more(flag(y >= 2), queries, state, [far[2]], split=True)
    got = other_core(sent)

    arrays = [by_z[count] for count in range(4)]
    arrays += [group[count] for group in (near, far) for count in (1, 2, 3)]
    place = jnp.stack([y, z, core])
    own_pages, sent_pages = fetch_pages(place, page_codes(targets, me), arrays)
    got_pages = other_core(sent_pages)
    attention = finish(own, got)
    keep = held_here(targets, me).reshape(PAGES, 1, 1, 1)
    shape = (PAGES, PAGE, 2, HD)
    kv_cache = jnp.where(keep, own_pages.reshape(shape), got_pages.reshape(shape))
    return attention, kv_cache


def on_device(
    features,
    conv_weight,
    conv_bias,
    embed_weight,
    position_table,
    norm_gain,
    qkv_weight,
    page_owner,
    page_slot,
):
    me = lax.axis_index("seq").astype(jnp.int32)
    tensor = lax.axis_index("tensor").astype(jnp.int32)
    tensor_count = lax.axis_size("tensor")
    half = half_weight(me, qkv_weight)
    half, features = lax.optimization_barrier((half, features))
    weight = spread(half, ((0,), (1,), (2, 3)))
    parts = partial_latents(features, conv_weight)
    own = parts[: FRAMES * EXT].reshape(FRAMES, EXT * LAT)
    target = (page_owner * PAGES + page_slot).astype(jnp.float32)
    target = jnp.broadcast_to(target, (FRAMES, PAGES))
    message = jnp.concatenate([own, target], axis=1)
    message = jnp.pad(message, ((0, 0), (0, 512 - message.shape[1])))
    message = jnp.broadcast_to(message[:, None], (FRAMES, SEQ // FRAMES, 512)).reshape(SEQ, 512)
    message = lax.all_to_all(message, "seq", split_axis=0, concat_axis=0, tiled=True)
    targets = message[:, EXT * LAT : EXT * LAT + PAGES].astype(jnp.int32)
    offset = tensor - me % (SEQ // FRAMES)
    latent = place_latents(message[:, : EXT * LAT].reshape(SEQ * EXT, LAT), offset)
    for bit in (1, 2, 4):
        swap = [(i, i ^ bit) for i in range(tensor_count)]
        latent = latent + lax.ppermute(latent, "tensor", swap)
    fixed = (conv_bias, embed_weight)
    own = normed_hidden(latent, *fixed, position_table, norm_gain)
    pair = normed_hidden(other_core(latent), *fixed, other_core(position_table), norm_gain)
    qkv = project_all(me, weight, own, pair)
    return attention_and_pages(me, targets, qkv)


def solution(mesh):
    placed = (
        P(None, "tensor", "seq", None),
        P(),
        P(),
        P(),
        P("seq", None),
        P(),
        P("seq", "tensor"),
        P("seq"),
        P("seq"),
    )
    return jax.shard_map(
        on_device,
        mesh=mesh,
        in_specs=placed,
        out_specs=(P("seq", "tensor"), P("seq", None, None, "tensor")),
        check_vma=False,
    )
```

```python
import functools

import jax
import jax.numpy as jnp
import numpy as np
from jax import lax
from jax.experimental import pallas as pl
from jax.experimental.pallas import tpu as pltpu
from jax.sharding import PartitionSpec as P

HD = 128
PAGE = 8
GROUP = 4
LAT = 16
BLK = 320
PAGES = 40
MOST = 3
SEQ = 32
ROWS = 5
COLS = 2
FRAMES = 4
EXT = (ROWS + 2) * (COLS + 2)
TOK = 384
TILE = 256
QROWS = GROUP * BLK
STATE = HD + 8
RBLK = 160
PIECES = 4
VMEM = 24 * 1024 * 1024


def params(**extra):
    return pltpu.CompilerParams(vmem_limit_bytes=VMEM, **extra)


def cost(blocks):
    scores = blocks * 2 * QROWS * BLK
    return pl.CostEstimate(flops=4 * HD * scores, bytes_accessed=3 << 20, transcendentals=scores)


def roll_lanes(value, shift):
    shift = shift % value.shape[1]
    return pltpu.roll(value, shift, 1) if shift else value


def conv_kernel(feat_ref, weight_ref, out_ref, grid_ref):
    grid_ref[...] = jnp.zeros_like(grid_ref)
    for frame in range(FRAMES):
        for row in range(ROWS):
            start = frame * EXT + (row + 1) * (COLS + 2) + 1
            value = feat_ref[frame, row].astype(jnp.float32)
            grid_ref[start : start + COLS, :] = value / (1.0 + jnp.exp(-value))
    active = grid_ref[...].astype(jnp.bfloat16)
    product = lax.dot_general(
        weight_ref[...], active, (((1,), (1,)), ((), ())), preferred_element_type=jnp.float32
    )
    lane = lax.broadcasted_iota(jnp.int32, (LAT, 128), 1)
    total = jnp.zeros((LAT, 128), jnp.float32)
    for time in range(3):
        part = jnp.zeros((LAT, 128), jnp.float32)
        for row in range(3):
            for col in range(3):
                index = (time * 3 + row) * 3 + col
                piece = product[index * LAT : (index + 1) * LAT, :]
                part = part + roll_lanes(piece, -((row - 1) * (COLS + 2) + col - 1))
        delay = (2 - time) * EXT
        if delay:
            part = jnp.where(lane >= delay, roll_lanes(part, delay), 0.0)
        total = total + part
    padded = jnp.concatenate([total, jnp.zeros((128 - LAT, 128), jnp.float32)], axis=0)
    out_ref[...] = jnp.transpose(padded)[:, :LAT]


def partial_latents(features, conv_weight):
    weight = jnp.transpose(conv_weight, (0, 1, 2, 4, 3)).reshape(-1, conv_weight.shape[3])
    return pl.pallas_call(
        conv_kernel,
        out_shape=jax.ShapeDtypeStruct((128, LAT), jnp.float32),
        scratch_shapes=[pltpu.VMEM((128, features.shape[-1]), jnp.float32)],
        compiler_params=params(),
        name="conv",
    )(features, weight)


def split_three(value):
    high = value.astype(jnp.bfloat16)
    rest = value - high.astype(jnp.float32)
    middle = rest.astype(jnp.bfloat16)
    low = (rest - middle.astype(jnp.float32)).astype(jnp.bfloat16)
    return high, middle, low


def place_kernel(parts_ref, token_ref, out_ref):
    count = parts_ref.shape[0]
    token = lax.broadcasted_iota(jnp.int32, (count, TOK), 1)
    pick = jnp.where(token == token_ref[...], 1.0, 0.0).astype(jnp.bfloat16)
    total = jnp.zeros((LAT, TOK), jnp.float32)
    for part in reversed(split_three(parts_ref[...])):
        total = total + lax.dot_general(
            part, pick, (((0,), (0,)), ((), ())), preferred_element_type=jnp.float32
        )
    out_ref[...] = total


def place_table():
    table = np.full((3, SEQ, ROWS + 2, COLS + 2), -1, np.int32)
    for case in range(3):
        for source in range(SEQ):
            for row in range(ROWS + 2):
                for col in range(COLS + 2):
                    height = row - 1 + ROWS * (case - 1)
                    width = source * COLS - 1 + col
                    if 0 <= height < ROWS and 0 <= width < SEQ * COLS:
                        table[case, source, row, col] = height * SEQ * COLS + width
    return table.reshape(3, SEQ * EXT, 1)


def place_latents(parts, offset):
    table = jnp.asarray(place_table())
    token = lax.dynamic_index_in_dim(table, jnp.clip(offset + 1, 0, 2), 0, keepdims=False)
    token = jnp.where(jnp.abs(offset) <= 1, token, -1)
    return pl.pallas_call(
        place_kernel,
        out_shape=jax.ShapeDtypeStruct((LAT, TOK), jnp.float32),
        compiler_params=params(),
        name="place",
    )(parts, token)


def hidden_kernel(latent_ref, bias_ref, embed_ref, table_ref, gain_ref, out_ref, hid_ref, sq_ref):
    step = pl.program_id(0)
    width = table_ref.shape[1]
    latent = latent_ref[...][:, :BLK] + bias_ref[...]
    latent = jnp.concatenate(split_three(latent), axis=0)
    embed = embed_ref[...]
    hidden = lax.dot_general(
        latent,
        jnp.concatenate([embed, embed, embed], axis=0),
        (((0,), (0,)), ((), ())),
        preferred_element_type=jnp.float32,
    ) + table_ref[...].astype(jnp.float32)
    hid_ref[step] = hidden
    squares = jnp.zeros((BLK, 128), jnp.float32)
    for lane in range(0, width, 128):
        piece = hidden[:, lane : lane + 128]
        squares = squares + piece * piece

    @pl.when(step == 0)
    def _():
        sq_ref[...] = squares

    @pl.when(step > 0)
    def _():
        sq_ref[...] += squares

    @pl.when(step == pl.num_programs(0) - 1)
    def _():
        count = hid_ref.shape[0]
        mean = jnp.sum(sq_ref[...], axis=1, keepdims=True) / (count * width)
        factor = lax.rsqrt(mean + 1e-05)
        for tile in range(count):
            gain = gain_ref[:, tile * width : (tile + 1) * width].astype(jnp.float32)
            normed = hid_ref[tile] * factor * gain
            for part in range(width // RBLK):
                piece = normed[:, part * RBLK : (part + 1) * RBLK]
                out_ref[tile * (width // RBLK) + part] = piece.astype(jnp.bfloat16)


def normed_hidden(latent, conv_bias, embed_weight, position_table, norm_gain):
    depth = position_table.shape[1]
    steps = 8
    width = depth // steps
    return pl.pallas_call(
        hidden_kernel,
        grid=(steps,),
        in_specs=[
            pl.BlockSpec((LAT, TOK), lambda i: (0, 0)),
            pl.BlockSpec((LAT, 1), lambda i: (0, 0)),
            pl.BlockSpec((LAT, width), lambda i: (0, i)),
            pl.BlockSpec((BLK, width), lambda i: (0, i)),
            pl.BlockSpec((1, depth), lambda i: (0, 0)),
        ],
        out_specs=pl.BlockSpec((depth // RBLK, BLK, RBLK), lambda i: (0, 0, 0)),
        out_shape=jax.ShapeDtypeStruct((depth // RBLK, BLK, RBLK), jnp.bfloat16),
        scratch_shapes=[
            pltpu.VMEM((steps, BLK, width), jnp.float32),
            pltpu.VMEM((BLK, 128), jnp.float32),
        ],
        compiler_params=params(dimension_semantics=("arbitrary",)),
        name="hidden",
    )(latent, conv_bias.reshape(LAT, 1), embed_weight, position_table, norm_gain.reshape(1, depth))


def project_kernel(index_ref, normed_ref, weight_ref, out_ref, held_ref, sum_ref, sems):
    rows = weight_ref.shape[0] // PIECES
    copies = []
    for piece in range(PIECES):
        cut = pl.ds(piece * rows, rows)
        copies.append(
            pltpu.make_async_copy(weight_ref.at[cut, :], held_ref.at[cut, :], sems.at[piece])
        )
        copies[-1].start()
    sum_ref[...] = jnp.zeros_like(sum_ref)
    for piece in range(PIECES):
        copies[piece].wait()

        def body(step, carry, first=piece * rows // RBLK):
            block = first + step
            weight = held_ref[pl.ds(pl.multiple_of(block * RBLK, RBLK), RBLK), :]
            sum_ref[...] += jnp.dot(
                normed_ref[index_ref[block]], weight, preferred_element_type=jnp.float32
            )
            return carry

        lax.fori_loop(0, rows // RBLK, body, 0)
    out_ref[...] = sum_ref[...].astype(jnp.bfloat16)


def project(index, normed, weight):
    depth, width = weight.shape
    return pl.pallas_call(
        project_kernel,
        in_specs=[
            pl.BlockSpec(memory_space=pltpu.SMEM),
            pl.BlockSpec(memory_space=pltpu.VMEM),
            pl.BlockSpec(memory_space=pl.ANY),
        ],
        out_shape=jax.ShapeDtypeStruct((BLK, width), jnp.bfloat16),
        scratch_shapes=[
            pltpu.VMEM((depth, width), jnp.bfloat16),
            pltpu.VMEM((BLK, width), jnp.float32),
            pltpu.SemaphoreType.DMA((PIECES,)),
        ],
        compiler_params=params(),
        cost_estimate=pl.CostEstimate(
            flops=2 * BLK * depth * width, bytes_accessed=2 * depth * width, transcendentals=0
        ),
        name="project",
    )(index, normed, weight)


def attend_block(masked, partner_full, keys, values, q_ref, state_ref):
    scale = 1.4426950408889634 / HD**0.5
    tiles = 2 * QROWS // TILE

    def score(tile):
        return lax.dot_general(
            keys,
            q_ref[tile * TILE : (tile + 1) * TILE, :],
            (((1,), (1,)), ((), ())),
            preferred_element_type=jnp.float32,
        )

    upcoming = score(0)
    for tile in range(tiles):
        scores = upcoming
        if tile + 1 < tiles:
            upcoming = score(tile + 1)
        cut = slice(tile * TILE, (tile + 1) * TILE)
        allowed = None
        if masked:
            key = lax.broadcasted_iota(jnp.int32, scores.shape, 0)
            query = tile * TILE + lax.broadcasted_iota(jnp.int32, (1, TILE), 1)
            if tile * TILE >= QROWS:
                query = jnp.where(partner_full, BLK, -1) + 0 * query
            else:
                for head in range(GROUP - 1, 0, -1):
                    query = jnp.where(query >= head * BLK, query - head * BLK, query)
            allowed = key <= query
            scores = jnp.where(allowed, scores, -1e30)
        peak = jnp.max(scores, axis=0, keepdims=True)
        if masked:
            best = peak
        else:
            old = state_ref[HD : HD + 1, cut]
            best = jnp.maximum(old, peak)
            factor = jnp.exp2((old - best) * scale)
        weights = jnp.exp2((scores - best) * scale)
        if masked:
            weights = jnp.where(allowed, weights, 0.0)
        total = jnp.sum(weights, axis=0, keepdims=True)
        summed = lax.dot_general(
            values,
            weights.astype(jnp.bfloat16),
            (((0,), (0,)), ((), ())),
            preferred_element_type=jnp.float32,
        )
        if not masked:
            total = total + state_ref[HD + 1 : HD + 2, cut] * factor
            summed = summed + state_ref[:HD, cut] * factor
        state_ref[HD : HD + 1, cut] = best
        state_ref[HD + 1 : HD + 2, cut] = total
        state_ref[:HD, cut] = summed


def first_kernel(core_ref, own_ref, pair_ref, kv_ref, state_ref, q_ref):
    for index, ref in enumerate((own_ref, pair_ref)):
        for head in range(GROUP):
            start = (index * GROUP + head) * BLK
            q_ref[start : start + BLK, :] = ref[:, head * HD : (head + 1) * HD]
    state_ref[HD + 2 :, :] = jnp.zeros((STATE - HD - 2, 2 * QROWS), jnp.float32)
    attend_block(True, core_ref[0] == 0, kv_ref[:, :HD], kv_ref[:, HD:], q_ref, state_ref)


def attend_first(core, own, pair, kv):
    return pl.pallas_call(
        first_kernel,
        in_specs=[pl.BlockSpec(memory_space=pltpu.SMEM)]
        + [pl.BlockSpec(memory_space=pltpu.VMEM)] * 3,
        out_shape=(
            jax.ShapeDtypeStruct((STATE, 2 * QROWS), jnp.float32),
            jax.ShapeDtypeStruct((2 * QROWS, HD), jnp.bfloat16),
        ),
        compiler_params=params(),
        cost_estimate=cost(1),
        name="first",
    )(core.reshape(1), own, pair, kv)


def more_kernel(count, split, flag_ref, q_ref, state_ref, *rest):
    arrays, rest = rest[:count], rest[count:]
    if split:
        own_out_ref, pair_out_ref, held_ref, sems, work_ref = rest
    else:
        work_ref, held_ref, sems = rest
    copies = []
    for index, array in enumerate(arrays):
        copies.append(pltpu.make_async_copy(array, held_ref.at[index], sems.at[index]))
        copies[-1].start()
    work_ref[...] = state_ref[...]
    for copy in copies:
        copy.wait()

    def body(index, carry):
        @pl.when(flag_ref[index] != 0)
        def _():
            keys, values = held_ref[index, :, :HD], held_ref[index, :, HD:]
            attend_block(False, None, keys, values, q_ref, work_ref)

        return carry

    lax.fori_loop(0, count, body, 0)
    if split:
        own_out_ref[...] = work_ref[:, :QROWS]
        pair_out_ref[...] = work_ref[:, QROWS:]


def attend_more(flags, queries, state, arrays, split=False):
    unit, count = arrays[0].shape[0], len(arrays)
    half = jax.ShapeDtypeStruct((STATE, QROWS), jnp.float32)
    whole = jax.ShapeDtypeStruct((STATE, 2 * QROWS), jnp.float32)
    scratch = [
        pltpu.VMEM((count, unit, 2 * HD), jnp.bfloat16),
        pltpu.SemaphoreType.DMA((count,)),
    ]
    if split:
        scratch.append(pltpu.VMEM((STATE, 2 * QROWS), jnp.float32))
    return pl.pallas_call(
        functools.partial(more_kernel, count, split),
        in_specs=[pl.BlockSpec(memory_space=pltpu.SMEM)]
        + [pl.BlockSpec(memory_space=pltpu.VMEM)] * 2
        + [pl.BlockSpec(memory_space=pl.ANY)] * count,
        out_shape=(half, half) if split else whole,
        scratch_shapes=scratch,
        compiler_params=params(),
        cost_estimate=cost(count * unit // BLK),
        name="more",
    )(flags, queries, state, *arrays)


def finish_kernel(own_ref, got_ref, out_ref, row_ref):
    scale = 1.4426950408889634 / HD**0.5
    for start in range(0, QROWS, TILE):
        cut = slice(start, start + TILE)
        first, second = own_ref[HD : HD + 1, cut], got_ref[HD : HD + 1, cut]
        best = jnp.maximum(first, second)
        first = jnp.exp2((first - best) * scale)
        second = jnp.exp2((second - best) * scale)
        total = own_ref[HD + 1 : HD + 2, cut] * first + got_ref[HD + 1 : HD + 2, cut] * second
        summed = own_ref[:HD, cut] * first + got_ref[:HD, cut] * second
        row_ref[cut, :] = jnp.transpose(summed / total)
    for head in range(GROUP):
        rows = row_ref[head * BLK : (head + 1) * BLK, :]
        out_ref[:, head * HD : (head + 1) * HD] = rows.astype(jnp.bfloat16)


def finish(own, got):
    return pl.pallas_call(
        finish_kernel,
        out_shape=jax.ShapeDtypeStruct((BLK, GROUP * HD), jnp.bfloat16),
        scratch_shapes=[pltpu.VMEM((QROWS, HD), jnp.float32)],
        compiler_params=params(),
        name="finish",
    )(own, got)


def page_kernel(place_ref, code_ref, *rest):
    count = (len(rest) - 4) // 2
    remote, own_ref, pair_ref = rest[:count], rest[count], rest[count + 1]
    held_ref, sems, arrays = rest[count + 2], rest[count + 3], rest[count + 4 :]
    copies = [
        pltpu.make_async_copy(remote[index], arrays[index], sems.at[index])
        for index in range(count)
    ]
    for copy in copies:
        copy.start()
    held_ref[...] = jnp.zeros_like(held_ref)
    for copy in copies:
        copy.wait()
    y, z, core = place_ref[0], place_ref[1], place_ref[2]
    for by_y in range(4):
        for by_z in range(4):
            if by_y == 0:
                array, base = arrays[by_z], 0
            else:
                array, base = arrays[3 + by_y + by_z // 2 * 3], by_z % 2 * BLK
            source = (((y - by_y) & 3) * 4 + ((z - by_z) & 3)) * 2 + core
            for entry in range(2 * MOST):
                code = code_ref[source * 2 * MOST + entry]

                @pl.when(code >= 0)
                def _():
                    page = code >> 6
                    slot = (code & 63) + entry // MOST * PAGES
                    row = pl.multiple_of(base + (page >> 1) * 2 * PAGE, 2 * PAGE)
                    rows = array[pl.ds(row, 2 * PAGE), :].astype(jnp.float32)
                    rows = jnp.where((page & 1) == 1, rows[PAGE:], rows[:PAGE])
                    held_ref[pl.ds(pl.multiple_of(slot * PAGE, PAGE), PAGE), :] = rows

    own_ref[...] = held_ref[: PAGES * PAGE].astype(jnp.bfloat16)
    pair_ref[...] = held_ref[PAGES * PAGE :].astype(jnp.bfloat16)


def fetch_pages(place, codes, arrays):
    out = jax.ShapeDtypeStruct((PAGES * PAGE, 2 * HD), jnp.bfloat16)
    return pl.pallas_call(
        page_kernel,
        in_specs=[pl.BlockSpec(memory_space=pltpu.SMEM)] * 2
        + [pl.BlockSpec(memory_space=pl.ANY)] * len(arrays),
        out_shape=(out, out),
        scratch_shapes=[
            pltpu.VMEM((2 * PAGES * PAGE, 2 * HD), jnp.float32),
            pltpu.SemaphoreType.DMA((len(arrays),)),
        ]
        + [pltpu.VMEM(array.shape, array.dtype) for array in arrays],
        compiler_params=params(),
        name="pages",
    )(place, codes, *arrays)


def moves(step):
    pairs = []
    for y in range(4):
        for z in range(4):
            for core in range(2):
                to_y, to_z, to_core = step(y, z, core)
                pairs.append(((y * 4 + z) * 2 + core, (to_y * 4 + to_z) * 2 + to_core))
    return pairs


def along_y(value, count):
    return lax.ppermute(value, "seq", moves(lambda y, z, c: ((y + count) % 4, z, c)))


def along_z(value, count):
    return lax.ppermute(value, "seq", moves(lambda y, z, c: (y, (z + count) % 4, c)))


def other_core(value):
    return lax.ppermute(value, "seq", moves(lambda y, z, c: (y, z, 1 - c)))


def page_codes(targets, me):
    index = jnp.arange(PAGES, dtype=jnp.int32)
    codes = []
    for owner in (me, me ^ 1):
        slot = targets - owner * PAGES
        match = (slot >= 0) & (slot < PAGES)
        before = match[:, None, :] & (index[None, :] < index[:, None])
        rank = jnp.sum(before.astype(jnp.int32), axis=2)
        code = index * 64 + slot + 1
        for entry in range(MOST):
            codes.append(jnp.sum(jnp.where(match & (rank == entry), code, 0), axis=1) - 1)
    return jnp.stack(codes, axis=1).reshape(-1)


def held_here(targets, me):
    mine = me * PAGES + jnp.arange(PAGES, dtype=jnp.int32)
    same_core = (jnp.arange(SEQ, dtype=jnp.int32) % 2 == me % 2)[:, None]
    match = (targets[None] == mine[:, None, None]) & same_core[None]
    return jnp.any(match, axis=(1, 2))


def spread(value, groups):
    by_z = {0: value}
    for count in (1, 2, 3):
        by_z[count] = along_z(value, count)
    by_y = []
    for group in groups:
        parts = [by_z[count] for count in group]
        parts = jnp.concatenate(parts, axis=0) if len(parts) > 1 else parts[0]
        by_y.append({count: along_y(parts, count) for count in (1, 3, 2)})
    return by_z, by_y


def gather_rows(stacked):
    groups = [[(y * 4 + z) * 2 + c for y in range(4) for c in range(2)] for z in range(4)]
    return lax.all_gather(stacked, "seq", axis=0, tiled=True, axis_index_groups=groups)


def stack_z(value):
    parts = [value] + [along_z(value, count) for count in (1, 2, 3)]
    return jnp.concatenate(parts, axis=0)


def row_order(me):
    z = (me // 2) % 4
    order = [(y * 4 + ((z - k) & 3)) * 2 + c for y in range(4) for c in range(2) for k in range(4)]
    return jnp.stack(order)


def attention_and_pages(me, targets, normed, kv_weight, query_weight):
    core, z, y = me % 2, (me // 2) % 4, me // 8
    order = row_order(me)
    kv = project(order, normed, kv_weight)
    by_z, (near, far) = spread(kv, ((0, 1), (2, 3)))
    order, near[1], near[2], near[3] = lax.optimization_barrier(
        (order, near[1], near[2], near[3])
    )
    own_queries = project(order, normed, query_weight)
    pair_queries = other_core(own_queries)

    def flag(*conditions):
        return jnp.stack([jnp.asarray(value, jnp.int32) for value in conditions])

    state, queries = attend_first(core, own_queries, pair_queries, kv)
    state = attend_more(
        flag(z >= 1, z >= 2, z >= 3), queries, state, [by_z[1], by_z[2], by_z[3]]
    )
    state = attend_more(
        flag(y >= 1, y >= 3, y >= 2), queries, state, [near[1], near[3], near[2]]
    )
    state = attend_more(flag(y >= 1, y >= 3), queries, state, [far[1], far[3]])
    own, sent = attend_more(flag(y >= 2), queries, state, [far[2]], split=True)
    got = other_core(sent)

    arrays = [by_z[count] for count in range(4)]
    arrays += [group[count] for group in (near, far) for count in (1, 2, 3)]
    place = jnp.stack([y, z, core])
    own_pages, sent_pages = fetch_pages(place, page_codes(targets, me), arrays)
    got_pages = other_core(sent_pages)
    attention = finish(own, got)
    keep = held_here(targets, me).reshape(PAGES, 1, 1, 1)
    shape = (PAGES, PAGE, 2, HD)
    kv_cache = jnp.where(keep, own_pages.reshape(shape), got_pages.reshape(shape))
    return attention, kv_cache


def on_device(
    features,
    conv_weight,
    conv_bias,
    embed_weight,
    position_table,
    norm_gain,
    qkv_weight,
    page_owner,
    page_slot,
):
    me = lax.axis_index("seq").astype(jnp.int32)
    tensor = lax.axis_index("tensor").astype(jnp.int32)
    tensor_count = lax.axis_size("tensor")
    kv_weight = stack_z(qkv_weight[:, GROUP * HD :])
    query_weight = stack_z(qkv_weight[:, : GROUP * HD])
    parts = partial_latents(features, conv_weight)
    parts, kv_weight = lax.optimization_barrier((parts, kv_weight))
    kv_weight = gather_rows(kv_weight)
    own = parts[: FRAMES * EXT].reshape(FRAMES, EXT * LAT)
    target = (page_owner * PAGES + page_slot).astype(jnp.float32)
    target = jnp.broadcast_to(target, (FRAMES, PAGES))
    message = jnp.concatenate([own, target], axis=1)
    message = jnp.pad(message, ((0, 0), (0, 512 - message.shape[1])))
    message = jnp.broadcast_to(message[:, None], (FRAMES, SEQ // FRAMES, 512)).reshape(SEQ, 512)
    message = lax.all_to_all(message, "seq", split_axis=0, concat_axis=0, tiled=True)
    message, query_weight = lax.optimization_barrier((message, query_weight))
    query_weight = gather_rows(query_weight)
    targets = message[:, EXT * LAT : EXT * LAT + PAGES].astype(jnp.int32)
    offset = tensor - me % (SEQ // FRAMES)
    latent = place_latents(message[:, : EXT * LAT].reshape(SEQ * EXT, LAT), offset)
    for bit in (1, 2, 4):
        swap = [(i, i ^ bit) for i in range(tensor_count)]
        latent = latent + lax.ppermute(latent, "tensor", swap)
    normed = normed_hidden(latent, conv_bias, embed_weight, position_table, norm_gain)
    return attention_and_pages(me, targets, normed, kv_weight, query_weight)


def solution(mesh):
    placed = (
        P(None, "tensor", "seq", None),
        P(),
        P(),
        P(),
        P("seq", None),
        P(),
        P("seq", "tensor"),
        P("seq"),
        P("seq"),
    )
    return jax.shard_map(
        on_device,
        mesh=mesh,
        in_specs=placed,
        out_specs=(P("seq", "tensor"), P("seq", None, None, "tensor")),
        check_vma=False,
    )
```

```python
import functools

import jax
import jax.numpy as jnp
import numpy as np
from jax import lax
from jax.experimental import pallas as pl
from jax.experimental.pallas import tpu as pltpu
from jax.sharding import PartitionSpec as P

HD = 128
PAGE = 8
GROUP = 4
LAT = 16
BLK = 320
PAGES = 40
MOST = 3
SEQ = 32
ROWS = 5
COLS = 2
FRAMES = 4
EXT = (ROWS + 2) * (COLS + 2)
TOK = 384
TILE = 256
QROWS = GROUP * BLK
STATE = HD + 8
RBLK = 160
VMEM = 24 * 1024 * 1024


def params(**extra):
    return pltpu.CompilerParams(vmem_limit_bytes=VMEM, **extra)


def cost(blocks):
    scores = blocks * 2 * QROWS * BLK
    return pl.CostEstimate(flops=4 * HD * scores, bytes_accessed=3 << 20, transcendentals=scores)


def roll_lanes(value, shift):
    shift = shift % value.shape[1]
    return pltpu.roll(value, shift, 1) if shift else value


def conv_kernel(feat_ref, weight_ref, out_ref, grid_ref):
    grid_ref[...] = jnp.zeros_like(grid_ref)
    for frame in range(FRAMES):
        for row in range(ROWS):
            start = frame * EXT + (row + 1) * (COLS + 2) + 1
            value = feat_ref[frame, row].astype(jnp.float32)
            grid_ref[start : start + COLS, :] = value / (1.0 + jnp.exp(-value))
    active = grid_ref[...].astype(jnp.bfloat16)
    product = lax.dot_general(
        weight_ref[...], active, (((1,), (1,)), ((), ())), preferred_element_type=jnp.float32
    )
    lane = lax.broadcasted_iota(jnp.int32, (LAT, 128), 1)
    total = jnp.zeros((LAT, 128), jnp.float32)
    for time in range(3):
        part = jnp.zeros((LAT, 128), jnp.float32)
        for row in range(3):
            for col in range(3):
                index = (time * 3 + row) * 3 + col
                piece = product[index * LAT : (index + 1) * LAT, :]
                part = part + roll_lanes(piece, -((row - 1) * (COLS + 2) + col - 1))
        delay = (2 - time) * EXT
        if delay:
            part = jnp.where(lane >= delay, roll_lanes(part, delay), 0.0)
        total = total + part
    padded = jnp.concatenate([total, jnp.zeros((128 - LAT, 128), jnp.float32)], axis=0)
    out_ref[...] = jnp.transpose(padded)[:, :LAT]


def partial_latents(features, conv_weight):
    weight = jnp.transpose(conv_weight, (0, 1, 2, 4, 3)).reshape(-1, conv_weight.shape[3])
    return pl.pallas_call(
        conv_kernel,
        out_shape=jax.ShapeDtypeStruct((128, LAT), jnp.float32),
        scratch_shapes=[pltpu.VMEM((128, features.shape[-1]), jnp.float32)],
        compiler_params=params(),
        name="conv",
    )(features, weight)


def split_three(value):
    high = value.astype(jnp.bfloat16)
    rest = value - high.astype(jnp.float32)
    middle = rest.astype(jnp.bfloat16)
    low = (rest - middle.astype(jnp.float32)).astype(jnp.bfloat16)
    return high, middle, low


def place_kernel(offset_ref, parts_ref, token_ref, out_ref):
    count = parts_ref.shape[0]
    token = lax.broadcasted_iota(jnp.int32, (count, TOK), 1) - offset_ref[0] * BLK
    pick = jnp.where(token == token_ref[...], 1.0, 0.0).astype(jnp.bfloat16)
    total = jnp.zeros((LAT, TOK), jnp.float32)
    for part in reversed(split_three(parts_ref[...])):
        total = total + lax.dot_general(
            part, pick, (((0,), (0,)), ((), ())), preferred_element_type=jnp.float32
        )
    out_ref[...] = total


def place_table():
    row = np.arange(ROWS + 2).reshape(1, -1, 1) - 1
    col = np.arange(COLS + 2).reshape(1, 1, -1) - 1
    width = np.arange(SEQ).reshape(-1, 1, 1) * COLS + col
    inside = (width >= 0) & (width < SEQ * COLS)
    token = np.where(inside, row * SEQ * COLS + width, -(1 << 20))
    return token.astype(np.int32).reshape(SEQ * EXT, 1)


def place_latents(parts, offset):
    return pl.pallas_call(
        place_kernel,
        in_specs=[pl.BlockSpec(memory_space=pltpu.SMEM)]
        + [pl.BlockSpec(memory_space=pltpu.VMEM)] * 2,
        out_shape=jax.ShapeDtypeStruct((LAT, TOK), jnp.float32),
        compiler_params=params(),
        name="place",
    )(offset.reshape(1), parts, jnp.asarray(place_table()))


def hidden_kernel(latent_ref, bias_ref, embed_ref, table_ref, gain_ref, out_ref, hid_ref, sq_ref):
    step = pl.program_id(0)
    width = table_ref.shape[1]
    latent = latent_ref[...][:, :BLK] + bias_ref[...]
    latent = jnp.concatenate(split_three(latent), axis=0)
    embed = embed_ref[...]
    hidden = lax.dot_general(
        latent,
        jnp.concatenate([embed, embed, embed], axis=0),
        (((0,), (0,)), ((), ())),
        preferred_element_type=jnp.float32,
    ) + table_ref[...].astype(jnp.float32)
    hid_ref[step] = hidden
    squares = jnp.zeros((BLK, 128), jnp.float32)
    for lane in range(0, width, 128):
        piece = hidden[:, lane : lane + 128]
        squares = squares + piece * piece

    @pl.when(step == 0)
    def _():
        sq_ref[...] = squares

    @pl.when(step > 0)
    def _():
        sq_ref[...] += squares

    @pl.when(step == pl.num_programs(0) - 1)
    def _():
        count = hid_ref.shape[0]
        mean = jnp.sum(sq_ref[...], axis=1, keepdims=True) / (count * width)
        factor = lax.rsqrt(mean + 1e-05)
        for tile in range(count):
            gain = gain_ref[:, tile * width : (tile + 1) * width].astype(jnp.float32)
            normed = hid_ref[tile] * factor * gain
            for part in range(width // RBLK):
                piece = normed[:, part * RBLK : (part + 1) * RBLK]
                block = tile * (width // RBLK) + part
                y, z, core = block // 8, block // 2 % 4, block % 2
                start = ((y * 2 + core) * 4 + z) * RBLK
                out_ref[:, start : start + RBLK] = piece.astype(jnp.bfloat16)


def normed_hidden(latent, conv_bias, embed_weight, position_table, norm_gain):
    depth = position_table.shape[1]
    steps = 8
    width = depth // steps
    return pl.pallas_call(
        hidden_kernel,
        grid=(steps,),
        in_specs=[
            pl.BlockSpec((LAT, TOK), lambda i: (0, 0)),
            pl.BlockSpec((LAT, 1), lambda i: (0, 0)),
            pl.BlockSpec((LAT, width), lambda i: (0, i)),
            pl.BlockSpec((BLK, width), lambda i: (0, i)),
            pl.BlockSpec((1, depth), lambda i: (0, 0)),
        ],
        out_specs=pl.BlockSpec((BLK, depth), lambda i: (0, 0)),
        out_shape=jax.ShapeDtypeStruct((BLK, depth), jnp.bfloat16),
        scratch_shapes=[
            pltpu.VMEM((steps, BLK, width), jnp.float32),
            pltpu.VMEM((BLK, 128), jnp.float32),
        ],
        compiler_params=params(dimension_semantics=("arbitrary",)),
        name="hidden",
    )(latent, conv_bias.reshape(LAT, 1), embed_weight, position_table, norm_gain.reshape(1, depth))


def attend_block(masked, partner_full, keys, values, q_ref, state_ref):
    scale = 1.4426950408889634 / HD**0.5
    tiles = 2 * QROWS // TILE

    def score(tile):
        return lax.dot_general(
            keys,
            q_ref[tile * TILE : (tile + 1) * TILE, :],
            (((1,), (1,)), ((), ())),
            preferred_element_type=jnp.float32,
        )

    upcoming = score(0)
    for tile in range(tiles):
        scores = upcoming
        if tile + 1 < tiles:
            upcoming = score(tile + 1)
        cut = slice(tile * TILE, (tile + 1) * TILE)
        allowed = None
        if masked:
            key = lax.broadcasted_iota(jnp.int32, scores.shape, 0)
            query = tile * TILE + lax.broadcasted_iota(jnp.int32, (1, TILE), 1)
            if tile * TILE >= QROWS:
                query = jnp.where(partner_full, BLK, -1) + 0 * query
            else:
                for head in range(GROUP - 1, 0, -1):
                    query = jnp.where(query >= head * BLK, query - head * BLK, query)
            allowed = key <= query
            scores = jnp.where(allowed, scores, -1e30)
        peak = jnp.max(scores, axis=0, keepdims=True)
        if masked:
            best = peak
        else:
            old = state_ref[HD : HD + 1, cut]
            best = jnp.maximum(old, peak)
            factor = jnp.exp2((old - best) * scale)
        weights = jnp.exp2((scores - best) * scale)
        if masked:
            weights = jnp.where(allowed, weights, 0.0)
        total = jnp.sum(weights, axis=0, keepdims=True)
        summed = lax.dot_general(
            values,
            weights.astype(jnp.bfloat16),
            (((0,), (0,)), ((), ())),
            preferred_element_type=jnp.float32,
        )
        if not masked:
            total = total + state_ref[HD + 1 : HD + 2, cut] * factor
            summed = summed + state_ref[:HD, cut] * factor
        state_ref[HD : HD + 1, cut] = best
        state_ref[HD + 1 : HD + 2, cut] = total
        state_ref[:HD, cut] = summed


def first_kernel(core_ref, own_ref, pair_ref, kv_ref, state_ref, q_ref):
    for index, ref in enumerate((own_ref, pair_ref)):
        for head in range(GROUP):
            start = (index * GROUP + head) * BLK
            q_ref[start : start + BLK, :] = ref[:, head * HD : (head + 1) * HD]
    state_ref[HD + 2 :, :] = jnp.zeros((STATE - HD - 2, 2 * QROWS), jnp.float32)
    attend_block(True, core_ref[0] == 0, kv_ref[:, :HD], kv_ref[:, HD:], q_ref, state_ref)


def attend_first(core, own, pair, kv):
    return pl.pallas_call(
        first_kernel,
        in_specs=[pl.BlockSpec(memory_space=pltpu.SMEM)]
        + [pl.BlockSpec(memory_space=pltpu.VMEM)] * 3,
        out_shape=(
            jax.ShapeDtypeStruct((STATE, 2 * QROWS), jnp.float32),
            jax.ShapeDtypeStruct((2 * QROWS, HD), jnp.bfloat16),
        ),
        compiler_params=params(),
        cost_estimate=cost(1),
        name="first",
    )(core.reshape(1), own, pair, kv)


def more_kernel(count, split, flag_ref, q_ref, state_ref, *rest):
    arrays, rest = rest[:count], rest[count:]
    if split:
        own_out_ref, pair_out_ref, held_ref, sems, work_ref = rest
    else:
        work_ref, held_ref, sems = rest
    copies = []
    for index, array in enumerate(arrays):
        copies.append(pltpu.make_async_copy(array, held_ref.at[index], sems.at[index]))
        copies[-1].start()
    work_ref[...] = state_ref[...]
    for copy in copies:
        copy.wait()

    def body(index, carry):
        @pl.when(flag_ref[index] != 0)
        def _():
            keys, values = held_ref[index, :, :HD], held_ref[index, :, HD:]
            attend_block(False, None, keys, values, q_ref, work_ref)

        return carry

    lax.fori_loop(0, count, body, 0)
    if split:
        own_out_ref[...] = work_ref[:, :QROWS]
        pair_out_ref[...] = work_ref[:, QROWS:]


def attend_more(flags, queries, state, arrays, split=False):
    unit, count = arrays[0].shape[0], len(arrays)
    half = jax.ShapeDtypeStruct((STATE, QROWS), jnp.float32)
    whole = jax.ShapeDtypeStruct((STATE, 2 * QROWS), jnp.float32)
    scratch = [
        pltpu.VMEM((count, unit, 2 * HD), jnp.bfloat16),
        pltpu.SemaphoreType.DMA((count,)),
    ]
    if split:
        scratch.append(pltpu.VMEM((STATE, 2 * QROWS), jnp.float32))
    return pl.pallas_call(
        functools.partial(more_kernel, count, split),
        in_specs=[pl.BlockSpec(memory_space=pltpu.SMEM)]
        + [pl.BlockSpec(memory_space=pltpu.VMEM)] * 2
        + [pl.BlockSpec(memory_space=pl.ANY)] * count,
        out_shape=(half, half) if split else whole,
        scratch_shapes=scratch,
        compiler_params=params(),
        cost_estimate=cost(count * unit // BLK),
        name="more",
    )(flags, queries, state, *arrays)


def finish_kernel(own_ref, got_ref, out_ref, row_ref):
    scale = 1.4426950408889634 / HD**0.5
    for start in range(0, QROWS, TILE):
        cut = slice(start, start + TILE)
        first, second = own_ref[HD : HD + 1, cut], got_ref[HD : HD + 1, cut]
        best = jnp.maximum(first, second)
        first = jnp.exp2((first - best) * scale)
        second = jnp.exp2((second - best) * scale)
        total = own_ref[HD + 1 : HD + 2, cut] * first + got_ref[HD + 1 : HD + 2, cut] * second
        summed = own_ref[:HD, cut] * first + got_ref[:HD, cut] * second
        row_ref[cut, :] = jnp.transpose(summed / total)
    for head in range(GROUP):
        rows = row_ref[head * BLK : (head + 1) * BLK, :]
        out_ref[:, head * HD : (head + 1) * HD] = rows.astype(jnp.bfloat16)


def finish(own, got):
    return pl.pallas_call(
        finish_kernel,
        out_shape=jax.ShapeDtypeStruct((BLK, GROUP * HD), jnp.bfloat16),
        scratch_shapes=[pltpu.VMEM((QROWS, HD), jnp.float32)],
        compiler_params=params(),
        name="finish",
    )(own, got)


def page_kernel(place_ref, code_ref, *rest):
    count = (len(rest) - 4) // 2
    remote, own_ref, pair_ref = rest[:count], rest[count], rest[count + 1]
    held_ref, sems, arrays = rest[count + 2], rest[count + 3], rest[count + 4 :]
    copies = [
        pltpu.make_async_copy(remote[index], arrays[index], sems.at[index])
        for index in range(count)
    ]
    for copy in copies:
        copy.start()
    held_ref[...] = jnp.zeros_like(held_ref)
    for copy in copies:
        copy.wait()
    y, z, core = place_ref[0], place_ref[1], place_ref[2]
    for by_y in range(4):
        for by_z in range(4):
            if by_y == 0:
                array, base = arrays[by_z], 0
            else:
                array, base = arrays[3 + by_y + by_z // 3 * 3], by_z % 3 * BLK
            source = (((y - by_y) & 3) * 4 + ((z - by_z) & 3)) * 2 + core
            for entry in range(2 * MOST):
                code = code_ref[source * 2 * MOST + entry]

                @pl.when(code >= 0)
                def _():
                    page = code >> 6
                    slot = (code & 63) + entry // MOST * PAGES
                    row = pl.multiple_of(base + (page >> 1) * 2 * PAGE, 2 * PAGE)
                    rows = array[pl.ds(row, 2 * PAGE), :].astype(jnp.float32)
                    rows = jnp.where((page & 1) == 1, rows[PAGE:], rows[:PAGE])
                    held_ref[pl.ds(pl.multiple_of(slot * PAGE, PAGE), PAGE), :] = rows

    own_ref[...] = held_ref[: PAGES * PAGE].astype(jnp.bfloat16)
    pair_ref[...] = held_ref[PAGES * PAGE :].astype(jnp.bfloat16)


def fetch_pages(place, codes, arrays):
    out = jax.ShapeDtypeStruct((PAGES * PAGE, 2 * HD), jnp.bfloat16)
    return pl.pallas_call(
        page_kernel,
        in_specs=[pl.BlockSpec(memory_space=pltpu.SMEM)] * 2
        + [pl.BlockSpec(memory_space=pl.ANY)] * len(arrays),
        out_shape=(out, out),
        scratch_shapes=[
            pltpu.VMEM((2 * PAGES * PAGE, 2 * HD), jnp.float32),
            pltpu.SemaphoreType.DMA((len(arrays),)),
        ]
        + [pltpu.VMEM(array.shape, array.dtype) for array in arrays],
        compiler_params=params(),
        name="pages",
    )(place, codes, *arrays)


def moves(step):
    pairs = []
    for y in range(4):
        for z in range(4):
            for core in range(2):
                to_y, to_z, to_core = step(y, z, core)
                pairs.append(((y * 4 + z) * 2 + core, (to_y * 4 + to_z) * 2 + to_core))
    return pairs


def along_y(value, count):
    return lax.ppermute(value, "seq", moves(lambda y, z, c: ((y + count) % 4, z, c)))


def along_z(value, count):
    return lax.ppermute(value, "seq", moves(lambda y, z, c: (y, (z + count) % 4, c)))


def other_core(value):
    return lax.ppermute(value, "seq", moves(lambda y, z, c: (y, z, 1 - c)))


def page_codes(targets, me):
    index = jnp.arange(PAGES, dtype=jnp.int32)
    codes = []
    for owner in (me, me ^ 1):
        slot = targets - owner * PAGES
        match = (slot >= 0) & (slot < PAGES)
        before = match[:, None, :] & (index[None, :] < index[:, None])
        rank = jnp.sum(before.astype(jnp.int32), axis=2)
        code = index * 64 + slot + 1
        for entry in range(MOST):
            codes.append(jnp.sum(jnp.where(match & (rank == entry), code, 0), axis=1) - 1)
    return jnp.stack(codes, axis=1).reshape(-1)


def held_here(targets, me):
    mine = me * PAGES + jnp.arange(PAGES, dtype=jnp.int32)
    same_core = (jnp.arange(SEQ, dtype=jnp.int32) % 2 == me % 2)[:, None]
    match = (targets[None] == mine[:, None, None]) & same_core[None]
    return jnp.any(match, axis=(1, 2))


def spread(value, groups):
    by_z = {0: value}
    for count in (1, 2, 3):
        by_z[count] = along_z(value, count)
    by_y = []
    for group in groups:
        parts = [by_z[count] for count in group]
        parts = jnp.concatenate(parts, axis=0) if len(parts) > 1 else parts[0]
        by_y.append({count: along_y(parts, count) for count in (1, 3, 2)})
    return by_z, by_y


def gather_rows(stacked):
    groups = [[(y * 4 + z) * 2 + c for y in range(4) for c in range(2)] for z in range(4)]
    return lax.all_gather(stacked, "seq", axis=0, tiled=True, axis_index_groups=groups)


def stack_z(value, me):
    z = (me // 2) % 4
    by_z = [value] + [along_z(value, count) for count in (1, 2, 3)]
    orders = [jnp.concatenate([by_z[(own - i) % 4] for i in range(4)], axis=0) for own in range(4)]
    low = jnp.where(z == 0, orders[0], orders[1])
    high = jnp.where(z == 2, orders[2], orders[3])
    return jnp.where(z < 2, low, high)


def project(normed, weight):
    return jnp.dot(normed, weight, preferred_element_type=jnp.float32).astype(jnp.bfloat16)


def attention_and_pages(me, targets, normed, kv_weight, query_weight):
    core, z, y = me % 2, (me // 2) % 4, me // 8
    kv = project(normed, kv_weight)
    by_z, (near, far) = spread(kv, ((0, 1, 2), (3,)))
    normed, unused = lax.optimization_barrier((normed, near[1]))
    own_queries = project(normed, query_weight)
    pair_queries = other_core(own_queries)

    def flag(*conditions):
        return jnp.stack([jnp.asarray(value, jnp.int32) for value in conditions])

    state, queries = attend_first(core, own_queries, pair_queries, kv)
    state = attend_more(
        flag(z >= 1, z >= 2, z >= 3), queries, state, [by_z[1], by_z[2], by_z[3]]
    )
    state = attend_more(
        flag(y >= 1, y >= 3, y >= 2), queries, state, [near[1], near[3], near[2]]
    )
    own, sent = attend_more(
        flag(y >= 1, y >= 3, y >= 2), queries, state, [far[1], far[3], far[2]], split=True
    )
    got = other_core(sent)

    arrays = [by_z[count] for count in range(4)]
    arrays += [group[count] for group in (near, far) for count in (1, 2, 3)]
    place = jnp.stack([y, z, core])
    own_pages, sent_pages = fetch_pages(place, page_codes(targets, me), arrays)
    got_pages = other_core(sent_pages)
    attention = finish(own, got)
    keep = held_here(targets, me).reshape(PAGES, 1, 1, 1)
    shape = (PAGES, PAGE, 2, HD)
    kv_cache = jnp.where(keep, own_pages.reshape(shape), got_pages.reshape(shape))
    return attention, kv_cache


def on_device(
    features,
    conv_weight,
    conv_bias,
    embed_weight,
    position_table,
    norm_gain,
    qkv_weight,
    page_owner,
    page_slot,
):
    me = lax.axis_index("seq").astype(jnp.int32)
    tensor = lax.axis_index("tensor").astype(jnp.int32)
    tensor_count = lax.axis_size("tensor")
    kv_weight = stack_z(qkv_weight[:, GROUP * HD :], me)
    query_weight = stack_z(qkv_weight[:, : GROUP * HD], me)
    parts = partial_latents(features, conv_weight)
    parts, kv_weight = lax.optimization_barrier((parts, kv_weight))
    kv_weight = gather_rows(kv_weight)
    own = parts[: FRAMES * EXT].reshape(FRAMES, EXT * LAT)
    target = (page_owner * PAGES + page_slot).astype(jnp.float32)
    target = jnp.broadcast_to(target, (FRAMES, PAGES))
    message = jnp.concatenate([own, target], axis=1)
    message = jnp.pad(message, ((0, 0), (0, 512 - message.shape[1])))
    message = jnp.broadcast_to(message[:, None], (FRAMES, SEQ // FRAMES, 512)).reshape(SEQ, 512)
    message = lax.all_to_all(message, "seq", split_axis=0, concat_axis=0, tiled=True)
    targets = message[:, EXT * LAT : EXT * LAT + PAGES].astype(jnp.int32)
    offset = tensor - me % (SEQ // FRAMES)
    latent = place_latents(message[:, : EXT * LAT].reshape(SEQ * EXT, LAT), offset)
    for bit in (1, 2, 4):
        swap = [(i, i ^ bit) for i in range(tensor_count)]
        latent = latent + lax.ppermute(latent, "tensor", swap)
        if bit == 1:
            latent, query_weight = lax.optimization_barrier((latent, query_weight))
    query_weight = gather_rows(query_weight)
    normed = normed_hidden(latent, conv_bias, embed_weight, position_table, norm_gain)
    return attention_and_pages(me, targets, normed, kv_weight, query_weight)


def solution(mesh):
    placed = (
        P(None, "tensor", "seq", None),
        P(),
        P(),
        P(),
        P("seq", None),
        P(),
        P("seq", "tensor"),
        P("seq"),
        P("seq"),
    )
    return jax.shard_map(
        on_device,
        mesh=mesh,
        in_specs=placed,
        out_specs=(P("seq", "tensor"), P("seq", None, None, "tensor")),
        check_vma=False,
    )
```

```python
import functools

import jax
import jax.numpy as jnp
import numpy as np
from jax import lax
from jax.experimental import pallas as pl
from jax.experimental.pallas import tpu as pltpu
from jax.sharding import PartitionSpec as P

HD = 128
PAGE = 8
GROUP = 4
LAT = 16
BLK = 320
PAGES = 40
MOST = 3
SEQ = 32
ROWS = 5
COLS = 2
FRAMES = 4
EXT = (ROWS + 2) * (COLS + 2)
TOK = 384
TILE = 256
QROWS = GROUP * BLK
STATE = HD + 8
RBLK = 160
VMEM = 24 * 1024 * 1024


def params(**extra):
    return pltpu.CompilerParams(vmem_limit_bytes=VMEM, **extra)


def cost(blocks):
    scores = blocks * 2 * QROWS * BLK
    return pl.CostEstimate(flops=4 * HD * scores, bytes_accessed=3 << 20, transcendentals=scores)


def roll_lanes(value, shift):
    shift = shift % value.shape[1]
    return pltpu.roll(value, shift, 1) if shift else value


def conv_kernel(feat_ref, weight_ref, out_ref, grid_ref):
    grid_ref[...] = jnp.zeros_like(grid_ref)
    for frame in range(FRAMES):
        for row in range(ROWS):
            start = frame * EXT + (row + 1) * (COLS + 2) + 1
            value = feat_ref[frame, row].astype(jnp.float32)
            grid_ref[start : start + COLS, :] = value / (1.0 + jnp.exp(-value))
    active = grid_ref[...].astype(jnp.bfloat16)
    product = lax.dot_general(
        weight_ref[...], active, (((1,), (1,)), ((), ())), preferred_element_type=jnp.float32
    )
    lane = lax.broadcasted_iota(jnp.int32, (LAT, 128), 1)
    total = jnp.zeros((LAT, 128), jnp.float32)
    for time in range(3):
        part = jnp.zeros((LAT, 128), jnp.float32)
        for row in range(3):
            for col in range(3):
                index = (time * 3 + row) * 3 + col
                piece = product[index * LAT : (index + 1) * LAT, :]
                part = part + roll_lanes(piece, -((row - 1) * (COLS + 2) + col - 1))
        delay = (2 - time) * EXT
        if delay:
            part = jnp.where(lane >= delay, roll_lanes(part, delay), 0.0)
        total = total + part
    padded = jnp.concatenate([total, jnp.zeros((128 - LAT, 128), jnp.float32)], axis=0)
    out_ref[...] = jnp.transpose(padded)[:, :LAT]


def partial_latents(features, conv_weight):
    weight = jnp.transpose(conv_weight, (0, 1, 2, 4, 3)).reshape(-1, conv_weight.shape[3])
    return pl.pallas_call(
        conv_kernel,
        out_shape=jax.ShapeDtypeStruct((128, LAT), jnp.float32),
        scratch_shapes=[pltpu.VMEM((128, features.shape[-1]), jnp.float32)],
        compiler_params=params(),
        name="conv",
    )(features, weight)


def split_three(value):
    high = value.astype(jnp.bfloat16)
    rest = value - high.astype(jnp.float32)
    middle = rest.astype(jnp.bfloat16)
    low = (rest - middle.astype(jnp.float32)).astype(jnp.bfloat16)
    return high, middle, low


def place_kernel(offset_ref, parts_ref, token_ref, out_ref):
    count = parts_ref.shape[0]
    token = lax.broadcasted_iota(jnp.int32, (TOK, count), 0) - offset_ref[0] * BLK
    pick = jnp.where(token == token_ref[...], 1.0, 0.0).astype(jnp.bfloat16)
    total = jnp.zeros((LAT, TOK), jnp.float32)
    for part in reversed(split_three(parts_ref[...])):
        total = total + lax.dot_general(
            part, pick, (((0,), (1,)), ((), ())), preferred_element_type=jnp.float32
        )
    out_ref[...] = total


def place_table():
    row = np.arange(ROWS + 2).reshape(1, -1, 1) - 1
    col = np.arange(COLS + 2).reshape(1, 1, -1) - 1
    width = np.arange(SEQ).reshape(-1, 1, 1) * COLS + col
    inside = (width >= 0) & (width < SEQ * COLS)
    token = np.where(inside, row * SEQ * COLS + width, -(1 << 20))
    return token.astype(np.int32).reshape(1, SEQ * EXT)


def place_latents(parts, offset):
    return pl.pallas_call(
        place_kernel,
        in_specs=[pl.BlockSpec(memory_space=pltpu.SMEM)]
        + [pl.BlockSpec(memory_space=pltpu.VMEM)] * 2,
        out_shape=jax.ShapeDtypeStruct((LAT, TOK), jnp.float32),
        compiler_params=params(),
        name="place",
    )(offset.reshape(1), parts, jnp.asarray(place_table()))


def hidden_kernel(latent_ref, embed_ref, table_ref, gain_ref, out_ref, hid_ref, sq_ref):
    step = pl.program_id(0)
    width = table_ref.shape[1]
    latent = latent_ref[...][:, :BLK]
    latent = jnp.concatenate(split_three(latent), axis=0)
    embed = embed_ref[...]
    hidden = lax.dot_general(
        latent,
        jnp.concatenate([embed, embed, embed], axis=0),
        (((0,), (0,)), ((), ())),
        preferred_element_type=jnp.float32,
    ) + table_ref[...].astype(jnp.float32)
    hid_ref[step] = hidden
    squares = jnp.zeros((BLK, 128), jnp.float32)
    for lane in range(0, width, 128):
        piece = hidden[:, lane : lane + 128]
        squares = squares + piece * piece

    @pl.when(step == 0)
    def _():
        sq_ref[...] = squares

    @pl.when(step > 0)
    def _():
        sq_ref[...] += squares

    @pl.when(step == pl.num_programs(0) - 1)
    def _():
        count = hid_ref.shape[0]
        mean = jnp.sum(sq_ref[...], axis=1, keepdims=True) / (count * width)
        factor = lax.rsqrt(mean + 1e-05)
        for tile in range(count):
            gain = gain_ref[:, tile * width : (tile + 1) * width].astype(jnp.float32)
            normed = hid_ref[tile] * factor * gain
            for part in range(width // RBLK):
                piece = normed[:, part * RBLK : (part + 1) * RBLK]
                block = tile * (width // RBLK) + part
                y, z, core = block // 8, block // 2 % 4, block % 2
                start = ((y * 2 + core) * 4 + z) * RBLK
                out_ref[:, start : start + RBLK] = piece.astype(jnp.bfloat16)


def normed_hidden(latent, embed_weight, position_table, gain):
    depth = position_table.shape[1]
    steps = 8
    width = depth // steps
    return pl.pallas_call(
        hidden_kernel,
        grid=(steps,),
        in_specs=[
            pl.BlockSpec((LAT, TOK), lambda i: (0, 0)),
            pl.BlockSpec((LAT, width), lambda i: (0, i)),
            pl.BlockSpec((BLK, width), lambda i: (0, i)),
            pl.BlockSpec((1, depth), lambda i: (0, 0)),
        ],
        out_specs=pl.BlockSpec((BLK, depth), lambda i: (0, 0)),
        out_shape=jax.ShapeDtypeStruct((BLK, depth), jnp.bfloat16),
        scratch_shapes=[
            pltpu.VMEM((steps, BLK, width), jnp.float32),
            pltpu.VMEM((BLK, 128), jnp.float32),
        ],
        compiler_params=params(dimension_semantics=("arbitrary",)),
        name="hidden",
    )(latent, embed_weight, position_table, gain)


def attend_block(masked, partner_full, keys, values, q_ref, state_ref):
    scale = 1.4426950408889634 / HD**0.5
    tiles = 2 * QROWS // TILE

    def score(tile):
        return lax.dot_general(
            keys,
            q_ref[tile * TILE : (tile + 1) * TILE, :],
            (((1,), (1,)), ((), ())),
            preferred_element_type=jnp.float32,
        )

    upcoming = score(0)
    for tile in range(tiles):
        scores = upcoming
        if tile + 1 < tiles:
            upcoming = score(tile + 1)
        cut = slice(tile * TILE, (tile + 1) * TILE)
        allowed = None
        if masked:
            key = lax.broadcasted_iota(jnp.int32, scores.shape, 0)
            query = tile * TILE + lax.broadcasted_iota(jnp.int32, (1, TILE), 1)
            if tile * TILE >= QROWS:
                query = jnp.where(partner_full, BLK, -1) + 0 * query
            else:
                for head in range(GROUP - 1, 0, -1):
                    query = jnp.where(query >= head * BLK, query - head * BLK, query)
            allowed = key <= query
            scores = jnp.where(allowed, scores, -1e30)
        peak = jnp.max(scores, axis=0, keepdims=True)
        if masked:
            best = peak
        else:
            old = state_ref[HD : HD + 1, cut]
            best = jnp.maximum(old, peak)
            factor = jnp.exp2((old - best) * scale)
        weights = jnp.exp2((scores - best) * scale)
        if masked:
            weights = jnp.where(allowed, weights, 0.0)
        total = jnp.sum(weights, axis=0, keepdims=True)
        summed = lax.dot_general(
            values,
            weights.astype(jnp.bfloat16),
            (((0,), (0,)), ((), ())),
            preferred_element_type=jnp.float32,
        )
        if not masked:
            total = total + state_ref[HD + 1 : HD + 2, cut] * factor
            summed = summed + state_ref[:HD, cut] * factor
        state_ref[HD : HD + 1, cut] = best
        state_ref[HD + 1 : HD + 2, cut] = total
        state_ref[:HD, cut] = summed


def first_kernel(core_ref, own_ref, pair_ref, kv_ref, state_ref, q_ref):
    for index, ref in enumerate((own_ref, pair_ref)):
        for head in range(GROUP):
            start = (index * GROUP + head) * BLK
            q_ref[start : start + BLK, :] = ref[:, head * HD : (head + 1) * HD]
    state_ref[HD + 2 :, :] = jnp.zeros((STATE - HD - 2, 2 * QROWS), jnp.float32)
    attend_block(True, core_ref[0] == 0, kv_ref[:, :HD], kv_ref[:, HD:], q_ref, state_ref)


def attend_first(core, own, pair, kv):
    return pl.pallas_call(
        first_kernel,
        in_specs=[pl.BlockSpec(memory_space=pltpu.SMEM)]
        + [pl.BlockSpec(memory_space=pltpu.VMEM)] * 3,
        out_shape=(
            jax.ShapeDtypeStruct((STATE, 2 * QROWS), jnp.float32),
            jax.ShapeDtypeStruct((2 * QROWS, HD), jnp.bfloat16),
        ),
        compiler_params=params(),
        cost_estimate=cost(1),
        name="first",
    )(core.reshape(1), own, pair, kv)


def more_kernel(count, split, flag_ref, q_ref, state_ref, *rest):
    arrays, rest = rest[:count], rest[count:]
    if split:
        own_out_ref, pair_out_ref, held_ref, sems, work_ref = rest
    else:
        work_ref, held_ref, sems = rest
    copies = []
    for index, array in enumerate(arrays):
        copies.append(pltpu.make_async_copy(array, held_ref.at[index], sems.at[index]))
        copies[-1].start()
    work_ref[...] = state_ref[...]
    for copy in copies:
        copy.wait()

    def body(index, carry):
        @pl.when(flag_ref[index] != 0)
        def _():
            keys, values = held_ref[index, :, :HD], held_ref[index, :, HD:]
            attend_block(False, None, keys, values, q_ref, work_ref)

        return carry

    lax.fori_loop(0, count, body, 0)
    if split:
        own_out_ref[...] = work_ref[:, :QROWS]
        pair_out_ref[...] = work_ref[:, QROWS:]


def attend_more(flags, queries, state, arrays, split=False):
    unit, count = arrays[0].shape[0], len(arrays)
    half = jax.ShapeDtypeStruct((STATE, QROWS), jnp.float32)
    whole = jax.ShapeDtypeStruct((STATE, 2 * QROWS), jnp.float32)
    scratch = [
        pltpu.VMEM((count, unit, 2 * HD), jnp.bfloat16),
        pltpu.SemaphoreType.DMA((count,)),
    ]
    if split:
        scratch.append(pltpu.VMEM((STATE, 2 * QROWS), jnp.float32))
    return pl.pallas_call(
        functools.partial(more_kernel, count, split),
        in_specs=[pl.BlockSpec(memory_space=pltpu.SMEM)]
        + [pl.BlockSpec(memory_space=pltpu.VMEM)] * 2
        + [pl.BlockSpec(memory_space=pl.ANY)] * count,
        out_shape=(half, half) if split else whole,
        scratch_shapes=scratch,
        compiler_params=params(),
        cost_estimate=cost(count * unit // BLK),
        name="more",
    )(flags, queries, state, *arrays)


def finish_kernel(own_ref, got_ref, out_ref, row_ref):
    scale = 1.4426950408889634 / HD**0.5
    for start in range(0, QROWS, TILE):
        cut = slice(start, start + TILE)
        first, second = own_ref[HD : HD + 1, cut], got_ref[HD : HD + 1, cut]
        best = jnp.maximum(first, second)
        first = jnp.exp2((first - best) * scale)
        second = jnp.exp2((second - best) * scale)
        total = own_ref[HD + 1 : HD + 2, cut] * first + got_ref[HD + 1 : HD + 2, cut] * second
        summed = own_ref[:HD, cut] * first + got_ref[:HD, cut] * second
        row_ref[cut, :] = jnp.transpose(summed / total)
    for head in range(GROUP):
        rows = row_ref[head * BLK : (head + 1) * BLK, :]
        out_ref[:, head * HD : (head + 1) * HD] = rows.astype(jnp.bfloat16)


def finish(own, got):
    return pl.pallas_call(
        finish_kernel,
        out_shape=jax.ShapeDtypeStruct((BLK, GROUP * HD), jnp.bfloat16),
        scratch_shapes=[pltpu.VMEM((QROWS, HD), jnp.float32)],
        compiler_params=params(),
        name="finish",
    )(own, got)


def page_kernel(place_ref, code_ref, *rest):
    count = (len(rest) - 4) // 2
    remote, own_ref, pair_ref = rest[:count], rest[count], rest[count + 1]
    held_ref, sems, arrays = rest[count + 2], rest[count + 3], rest[count + 4 :]
    copies = [
        pltpu.make_async_copy(remote[index], arrays[index], sems.at[index])
        for index in range(count)
    ]
    for copy in copies:
        copy.start()
    held_ref[...] = jnp.zeros_like(held_ref)
    for copy in copies:
        copy.wait()
    y, z, core = place_ref[0], place_ref[1], place_ref[2]
    for by_y in range(4):
        for by_z in range(4):
            if by_y == 0:
                array, base = arrays[by_z], 0
            else:
                array, base = arrays[3 + by_y + by_z // 3 * 3], by_z % 3 * BLK
            source = (((y - by_y) & 3) * 4 + ((z - by_z) & 3)) * 2 + core
            for entry in range(2 * MOST):
                code = code_ref[source * 2 * MOST + entry]

                @pl.when(code >= 0)
                def _():
                    page = code >> 6
                    slot = (code & 63) + entry // MOST * PAGES
                    row = pl.multiple_of(base + (page >> 1) * 2 * PAGE, 2 * PAGE)
                    rows = array[pl.ds(row, 2 * PAGE), :].astype(jnp.float32)
                    rows = jnp.where((page & 1) == 1, rows[PAGE:], rows[:PAGE])
                    held_ref[pl.ds(pl.multiple_of(slot * PAGE, PAGE), PAGE), :] = rows

    own_ref[...] = held_ref[: PAGES * PAGE].astype(jnp.bfloat16)
    pair_ref[...] = held_ref[PAGES * PAGE :].astype(jnp.bfloat16)


def fetch_pages(place, codes, arrays):
    out = jax.ShapeDtypeStruct((PAGES * PAGE, 2 * HD), jnp.bfloat16)
    return pl.pallas_call(
        page_kernel,
        in_specs=[pl.BlockSpec(memory_space=pltpu.SMEM)] * 2
        + [pl.BlockSpec(memory_space=pl.ANY)] * len(arrays),
        out_shape=(out, out),
        scratch_shapes=[
            pltpu.VMEM((2 * PAGES * PAGE, 2 * HD), jnp.float32),
            pltpu.SemaphoreType.DMA((len(arrays),)),
        ]
        + [pltpu.VMEM(array.shape, array.dtype) for array in arrays],
        compiler_params=params(),
        name="pages",
    )(place, codes, *arrays)


def moves(step):
    pairs = []
    for y in range(4):
        for z in range(4):
            for core in range(2):
                to_y, to_z, to_core = step(y, z, core)
                pairs.append(((y * 4 + z) * 2 + core, (to_y * 4 + to_z) * 2 + to_core))
    return pairs


def along_y(value, count):
    return lax.ppermute(value, "seq", moves(lambda y, z, c: ((y + count) % 4, z, c)))


def along_z(value, count):
    return lax.ppermute(value, "seq", moves(lambda y, z, c: (y, (z + count) % 4, c)))


def other_core(value):
    return lax.ppermute(value, "seq", moves(lambda y, z, c: (y, z, 1 - c)))


def page_codes(targets, me):
    index = jnp.arange(PAGES, dtype=jnp.int32)
    codes = []
    for owner in (me, me ^ 1):
        slot = targets - owner * PAGES
        match = (slot >= 0) & (slot < PAGES)
        before = match[:, None, :] & (index[None, :] < index[:, None])
        rank = jnp.sum(before.astype(jnp.int32), axis=2)
        code = index * 64 + slot + 1
        for entry in range(MOST):
            codes.append(jnp.sum(jnp.where(match & (rank == entry), code, 0), axis=1) - 1)
    return jnp.stack(codes, axis=1).reshape(-1)


def held_here(targets, me):
    mine = me * PAGES + jnp.arange(PAGES, dtype=jnp.int32)
    same_core = (jnp.arange(SEQ, dtype=jnp.int32) % 2 == me % 2)[:, None]
    match = (targets[None] == mine[:, None, None]) & same_core[None]
    return jnp.any(match, axis=(1, 2))


def spread(value, groups):
    by_z = {0: value}
    for count in (1, 2, 3):
        by_z[count] = along_z(value, count)
    by_y = []
    for group in groups:
        parts = [by_z[count] for count in group]
        parts = jnp.concatenate(parts, axis=0) if len(parts) > 1 else parts[0]
        by_y.append({count: along_y(parts, count) for count in (1, 3, 2)})
    return by_z, by_y


def gather_rows(stacked):
    groups = [[(y * 4 + z) * 2 + c for y in range(4) for c in range(2)] for z in range(4)]
    return lax.all_gather(stacked, "seq", axis=0, tiled=True, axis_index_groups=groups)


def stack_z(value, me):
    z = (me // 2) % 4
    by_z = [value] + [along_z(value, count) for count in (1, 2, 3)]
    orders = [jnp.concatenate([by_z[(own - i) % 4] for i in range(4)], axis=0) for own in range(4)]
    low = jnp.where(z == 0, orders[0], orders[1])
    high = jnp.where(z == 2, orders[2], orders[3])
    return jnp.where(z < 2, low, high)


def project(normed, weight):
    return jnp.dot(normed, weight, preferred_element_type=jnp.float32).astype(jnp.bfloat16)


def attention_and_pages(me, codes, keep, normed, kv_weight, query_weight):
    core, z, y = me % 2, (me // 2) % 4, me // 8
    kv = project(normed, kv_weight)
    by_z, (near, far) = spread(kv, ((0, 1, 2), (3,)))
    normed, unused, unused = lax.optimization_barrier((normed, near[1], by_z[3]))
    own_queries = project(normed, query_weight)
    pair_queries = other_core(own_queries)

    def flag(*conditions):
        return jnp.stack([jnp.asarray(value, jnp.int32) for value in conditions])

    state, queries = attend_first(core, own_queries, pair_queries, kv)
    state = attend_more(
        flag(z >= 1, z >= 2, z >= 3), queries, state, [by_z[1], by_z[2], by_z[3]]
    )
    state, near[3], near[2] = lax.optimization_barrier((state, near[3], near[2]))
    state = attend_more(
        flag(y >= 1, y >= 3, y >= 2), queries, state, [near[1], near[3], near[2]]
    )
    state, far[1], far[3], far[2] = lax.optimization_barrier((state, far[1], far[3], far[2]))
    own, sent = attend_more(
        flag(y >= 1, y >= 3, y >= 2), queries, state, [far[1], far[3], far[2]], split=True
    )
    got = other_core(sent)

    arrays = [by_z[count] for count in range(4)]
    arrays += [group[count] for group in (near, far) for count in (1, 2, 3)]
    place = jnp.stack([y, z, core])
    own_pages, sent_pages = fetch_pages(place, codes, arrays)
    got_pages = other_core(sent_pages)
    attention = finish(own, got)
    keep = keep.reshape(PAGES, 1, 1, 1)
    shape = (PAGES, PAGE, 2, HD)
    kv_cache = jnp.where(keep, own_pages.reshape(shape), got_pages.reshape(shape))
    return attention, kv_cache


def on_device(
    features,
    conv_weight,
    conv_bias,
    embed_weight,
    position_table,
    norm_gain,
    qkv_weight,
    page_owner,
    page_slot,
):
    me = lax.axis_index("seq").astype(jnp.int32)
    tensor = lax.axis_index("tensor").astype(jnp.int32)
    tensor_count = lax.axis_size("tensor")
    kv_weight = stack_z(qkv_weight[:, GROUP * HD :], me)
    query_weight = stack_z(qkv_weight[:, : GROUP * HD], me)
    parts = partial_latents(features, conv_weight)
    own = parts[: FRAMES * EXT].reshape(FRAMES, EXT * LAT)
    target = (page_owner * PAGES + page_slot).astype(jnp.float32)
    target = jnp.broadcast_to(target, (FRAMES, PAGES))
    message = jnp.concatenate([own, target], axis=1)
    message = jnp.pad(message, ((0, 0), (0, 512 - message.shape[1])))
    message = jnp.broadcast_to(message[:, None], (FRAMES, SEQ // FRAMES, 512)).reshape(SEQ, 512)
    message = lax.all_to_all(message, "seq", split_axis=0, concat_axis=0, tiled=True)
    gain = norm_gain.reshape(1, -1)
    message, kv_weight, gain = lax.optimization_barrier((message, kv_weight, gain))
    kv_weight = gather_rows(kv_weight)
    targets = message[:, EXT * LAT : EXT * LAT + PAGES].astype(jnp.int32)
    offset = tensor - me % (SEQ // FRAMES)
    latent = place_latents(message[:, : EXT * LAT].reshape(SEQ * EXT, LAT), offset)
    for bit in (1, 2, 4):
        swap = [(i, i ^ bit) for i in range(tensor_count)]
        latent = latent + lax.ppermute(latent, "tensor", swap)
        if bit == 1:
            latent, query_weight = lax.optimization_barrier((latent, query_weight))
    query_weight = gather_rows(query_weight)
    latent = latent + conv_bias[:, None]
    normed = normed_hidden(latent, embed_weight, position_table, gain)
    codes, keep = page_codes(targets, me), held_here(targets, me)
    normed, codes, keep = lax.optimization_barrier((normed, codes, keep))
    return attention_and_pages(me, codes, keep, normed, kv_weight, query_weight)


def solution(mesh):
    placed = (
        P(None, "tensor", "seq", None),
        P(),
        P(),
        P(),
        P("seq", None),
        P(),
        P("seq", "tensor"),
        P("seq"),
        P("seq"),
    )
    return jax.shard_map(
        on_device,
        mesh=mesh,
        in_specs=placed,
        out_specs=(P("seq", "tensor"), P("seq", None, None, "tensor")),
        check_vma=False,
    )
```

```python
import functools

import jax
import jax.numpy as jnp
import numpy as np
from jax import lax
from jax.experimental import pallas as pl
from jax.experimental.pallas import tpu as pltpu
from jax.sharding import PartitionSpec as P

HD = 128
PAGE = 8
GROUP = 4
LAT = 16
BLK = 320
PAGES = 40
MOST = 3
SEQ = 32
ROWS = 5
COLS = 2
FRAMES = 4
EXT = (ROWS + 2) * (COLS + 2)
TOK = 384
TILE = 256
QROWS = GROUP * BLK
STATE = HD + 8
VMEM = 24 * 1024 * 1024


def params(**extra):
    return pltpu.CompilerParams(vmem_limit_bytes=VMEM, **extra)


def cost(blocks):
    scores = blocks * 2 * QROWS * BLK
    return pl.CostEstimate(flops=4 * HD * scores, bytes_accessed=3 << 20, transcendentals=scores)


def roll_lanes(value, shift):
    shift = shift % value.shape[1]
    return pltpu.roll(value, shift, 1) if shift else value


def conv_kernel(feat_ref, weight_ref, out_ref, grid_ref):
    grid_ref[...] = jnp.zeros_like(grid_ref)
    for frame in range(FRAMES):
        for row in range(ROWS):
            start = frame * EXT + (row + 1) * (COLS + 2) + 1
            value = feat_ref[frame, row].astype(jnp.float32)
            grid_ref[start : start + COLS, :] = value / (1.0 + jnp.exp(-value))
    active = grid_ref[...].astype(jnp.bfloat16)
    product = lax.dot_general(
        weight_ref[...], active, (((1,), (1,)), ((), ())), preferred_element_type=jnp.float32
    )
    lane = lax.broadcasted_iota(jnp.int32, (LAT, 128), 1)
    total = jnp.zeros((LAT, 128), jnp.float32)
    for time in range(3):
        part = jnp.zeros((LAT, 128), jnp.float32)
        for row in range(3):
            for col in range(3):
                index = (time * 3 + row) * 3 + col
                piece = product[index * LAT : (index + 1) * LAT, :]
                part = part + roll_lanes(piece, -((row - 1) * (COLS + 2) + col - 1))
        delay = (2 - time) * EXT
        if delay:
            part = jnp.where(lane >= delay, roll_lanes(part, delay), 0.0)
        total = total + part
    padded = jnp.concatenate([total, jnp.zeros((128 - LAT, 128), jnp.float32)], axis=0)
    out_ref[...] = jnp.transpose(padded)[:, :LAT]


def partial_latents(features, conv_weight):
    weight = jnp.transpose(conv_weight, (0, 1, 2, 4, 3)).reshape(-1, conv_weight.shape[3])
    return pl.pallas_call(
        conv_kernel,
        out_shape=jax.ShapeDtypeStruct((128, LAT), jnp.float32),
        scratch_shapes=[pltpu.VMEM((128, features.shape[-1]), jnp.float32)],
        compiler_params=params(),
        name="conv",
    )(features, weight)


def split_three(value):
    high = value.astype(jnp.bfloat16)
    rest = value - high.astype(jnp.float32)
    middle = rest.astype(jnp.bfloat16)
    low = (rest - middle.astype(jnp.float32)).astype(jnp.bfloat16)
    return high, middle, low


def place_kernel(offset_ref, parts_ref, token_ref, out_ref):
    count = parts_ref.shape[0]
    token = lax.broadcasted_iota(jnp.int32, (TOK, count), 0) - offset_ref[0] * BLK
    pick = jnp.where(token == token_ref[...], 1.0, 0.0).astype(jnp.bfloat16)
    total = jnp.zeros((LAT, TOK), jnp.float32)
    for part in reversed(split_three(parts_ref[...])):
        total = total + lax.dot_general(
            part, pick, (((0,), (1,)), ((), ())), preferred_element_type=jnp.float32
        )
    out_ref[...] = total


def place_table():
    row = np.arange(ROWS + 2).reshape(1, -1, 1) - 1
    col = np.arange(COLS + 2).reshape(1, 1, -1) - 1
    width = np.arange(SEQ).reshape(-1, 1, 1) * COLS + col
    inside = (width >= 0) & (width < SEQ * COLS)
    token = np.where(inside, row * SEQ * COLS + width, -(1 << 20))
    return token.astype(np.int32).reshape(1, SEQ * EXT)


def place_latents(parts, offset):
    return pl.pallas_call(
        place_kernel,
        in_specs=[pl.BlockSpec(memory_space=pltpu.SMEM)]
        + [pl.BlockSpec(memory_space=pltpu.VMEM)] * 2,
        out_shape=jax.ShapeDtypeStruct((LAT, TOK), jnp.float32),
        compiler_params=params(),
        name="place",
    )(offset.reshape(1), parts, jnp.asarray(place_table()))


def hidden_kernel(latent_ref, embed_ref, table_ref, gain_ref, out_ref, hid_ref, sq_ref):
    step = pl.program_id(0)
    width = table_ref.shape[1]
    latent = latent_ref[...][:, :BLK]
    latent = jnp.concatenate(split_three(latent), axis=0)
    embed = embed_ref[...]
    hidden = lax.dot_general(
        latent,
        jnp.concatenate([embed, embed, embed], axis=0),
        (((0,), (0,)), ((), ())),
        preferred_element_type=jnp.float32,
    ) + table_ref[...].astype(jnp.float32)
    hid_ref[step] = hidden
    squares = jnp.zeros((BLK, 128), jnp.float32)
    for lane in range(0, width, 128):
        piece = hidden[:, lane : lane + 128]
        squares = squares + piece * piece

    @pl.when(step == 0)
    def _():
        sq_ref[...] = squares

    @pl.when(step > 0)
    def _():
        sq_ref[...] += squares

    @pl.when(step == pl.num_programs(0) - 1)
    def _():
        count = hid_ref.shape[0]
        mean = jnp.sum(sq_ref[...], axis=1, keepdims=True) / (count * width)
        factor = lax.rsqrt(mean + 1e-05)
        for tile in range(count):
            gain = gain_ref[:, tile * width : (tile + 1) * width].astype(jnp.float32)
            normed = hid_ref[tile] * factor * gain
            out_ref[:, tile * width : (tile + 1) * width] = normed.astype(jnp.bfloat16)


def normed_hidden(latent, embed_weight, position_table, gain):
    depth = position_table.shape[1]
    steps = 8
    width = depth // steps
    return pl.pallas_call(
        hidden_kernel,
        grid=(steps,),
        in_specs=[
            pl.BlockSpec((LAT, TOK), lambda i: (0, 0)),
            pl.BlockSpec((LAT, width), lambda i: (0, i)),
            pl.BlockSpec((BLK, width), lambda i: (0, i)),
            pl.BlockSpec((1, depth), lambda i: (0, 0)),
        ],
        out_specs=pl.BlockSpec((BLK, depth), lambda i: (0, 0)),
        out_shape=jax.ShapeDtypeStruct((BLK, depth), jnp.bfloat16),
        scratch_shapes=[
            pltpu.VMEM((steps, BLK, width), jnp.float32),
            pltpu.VMEM((BLK, 128), jnp.float32),
        ],
        compiler_params=params(dimension_semantics=("arbitrary",)),
        name="hidden",
    )(latent, embed_weight, position_table, gain)


def attend_block(masked, partner_full, keys, values, q_ref, state_ref):
    scale = 1.4426950408889634 / HD**0.5
    tiles = 2 * QROWS // TILE

    def score(tile):
        return lax.dot_general(
            keys,
            q_ref[tile * TILE : (tile + 1) * TILE, :],
            (((1,), (1,)), ((), ())),
            preferred_element_type=jnp.float32,
        )

    upcoming = score(0)
    for tile in range(tiles):
        scores = upcoming
        if tile + 1 < tiles:
            upcoming = score(tile + 1)
        cut = slice(tile * TILE, (tile + 1) * TILE)
        allowed = None
        if masked:
            key = lax.broadcasted_iota(jnp.int32, scores.shape, 0)
            query = tile * TILE + lax.broadcasted_iota(jnp.int32, (1, TILE), 1)
            if tile * TILE >= QROWS:
                query = jnp.where(partner_full, BLK, -1) + 0 * query
            else:
                for head in range(GROUP - 1, 0, -1):
                    query = jnp.where(query >= head * BLK, query - head * BLK, query)
            allowed = key <= query
            scores = jnp.where(allowed, scores, -1e30)
        peak = jnp.max(scores, axis=0, keepdims=True)
        if masked:
            best = peak
        else:
            old = state_ref[HD : HD + 1, cut]
            best = jnp.maximum(old, peak)
            factor = jnp.exp2((old - best) * scale)
        weights = jnp.exp2((scores - best) * scale)
        if masked:
            weights = jnp.where(allowed, weights, 0.0)
        total = jnp.sum(weights, axis=0, keepdims=True)
        summed = lax.dot_general(
            values,
            weights.astype(jnp.bfloat16),
            (((0,), (0,)), ((), ())),
            preferred_element_type=jnp.float32,
        )
        if not masked:
            total = total + state_ref[HD + 1 : HD + 2, cut] * factor
            summed = summed + state_ref[:HD, cut] * factor
        state_ref[HD : HD + 1, cut] = best
        state_ref[HD + 1 : HD + 2, cut] = total
        state_ref[:HD, cut] = summed


def first_kernel(core_ref, own_ref, pair_ref, kv_ref, state_ref, q_ref):
    for index, ref in enumerate((own_ref, pair_ref)):
        for head in range(GROUP):
            start = (index * GROUP + head) * BLK
            q_ref[start : start + BLK, :] = ref[:, head * HD : (head + 1) * HD]
    state_ref[HD + 2 :, :] = jnp.zeros((STATE - HD - 2, 2 * QROWS), jnp.float32)
    attend_block(True, core_ref[0] == 0, kv_ref[:, :HD], kv_ref[:, HD:], q_ref, state_ref)


def attend_first(core, own, pair, kv):
    return pl.pallas_call(
        first_kernel,
        in_specs=[pl.BlockSpec(memory_space=pltpu.SMEM)]
        + [pl.BlockSpec(memory_space=pltpu.VMEM)] * 3,
        out_shape=(
            jax.ShapeDtypeStruct((STATE, 2 * QROWS), jnp.float32),
            jax.ShapeDtypeStruct((2 * QROWS, HD), jnp.bfloat16),
        ),
        compiler_params=params(),
        cost_estimate=cost(1),
        name="first",
    )(core.reshape(1), own, pair, kv)


def more_kernel(count, split, flag_ref, q_ref, state_ref, *rest):
    arrays, rest = rest[:count], rest[count:]
    if split:
        own_out_ref, pair_out_ref, held_ref, sems, work_ref = rest
    else:
        work_ref, held_ref, sems = rest
    copies = []
    for index, array in enumerate(arrays):
        copies.append(pltpu.make_async_copy(array, held_ref.at[index], sems.at[index]))
        copies[-1].start()
    work_ref[...] = state_ref[...]
    for copy in copies:
        copy.wait()

    def body(index, carry):
        @pl.when(flag_ref[index] != 0)
        def _():
            keys, values = held_ref[index, :, :HD], held_ref[index, :, HD:]
            attend_block(False, None, keys, values, q_ref, work_ref)

        return carry

    lax.fori_loop(0, count, body, 0)
    if split:
        own_out_ref[...] = work_ref[:, :QROWS]
        pair_out_ref[...] = work_ref[:, QROWS:]


def attend_more(flags, queries, state, arrays, split=False):
    unit, count = arrays[0].shape[0], len(arrays)
    half = jax.ShapeDtypeStruct((STATE, QROWS), jnp.float32)
    whole = jax.ShapeDtypeStruct((STATE, 2 * QROWS), jnp.float32)
    scratch = [
        pltpu.VMEM((count, unit, 2 * HD), jnp.bfloat16),
        pltpu.SemaphoreType.DMA((count,)),
    ]
    if split:
        scratch.append(pltpu.VMEM((STATE, 2 * QROWS), jnp.float32))
    return pl.pallas_call(
        functools.partial(more_kernel, count, split),
        in_specs=[pl.BlockSpec(memory_space=pltpu.SMEM)]
        + [pl.BlockSpec(memory_space=pltpu.VMEM)] * 2
        + [pl.BlockSpec(memory_space=pl.ANY)] * count,
        out_shape=(half, half) if split else whole,
        scratch_shapes=scratch,
        compiler_params=params(),
        cost_estimate=cost(count * unit // BLK),
        name="more",
    )(flags, queries, state, *arrays)


def finish_kernel(own_ref, got_ref, out_ref, row_ref):
    scale = 1.4426950408889634 / HD**0.5
    for start in range(0, QROWS, TILE):
        cut = slice(start, start + TILE)
        first, second = own_ref[HD : HD + 1, cut], got_ref[HD : HD + 1, cut]
        best = jnp.maximum(first, second)
        first = jnp.exp2((first - best) * scale)
        second = jnp.exp2((second - best) * scale)
        total = own_ref[HD + 1 : HD + 2, cut] * first + got_ref[HD + 1 : HD + 2, cut] * second
        summed = own_ref[:HD, cut] * first + got_ref[:HD, cut] * second
        row_ref[cut, :] = jnp.transpose(summed / total)
    for head in range(GROUP):
        rows = row_ref[head * BLK : (head + 1) * BLK, :]
        out_ref[:, head * HD : (head + 1) * HD] = rows.astype(jnp.bfloat16)


def finish(own, got):
    return pl.pallas_call(
        finish_kernel,
        out_shape=jax.ShapeDtypeStruct((BLK, GROUP * HD), jnp.bfloat16),
        scratch_shapes=[pltpu.VMEM((QROWS, HD), jnp.float32)],
        compiler_params=params(),
        name="finish",
    )(own, got)


def page_kernel(place_ref, code_ref, *rest):
    count = (len(rest) - 4) // 2
    remote, own_ref, pair_ref = rest[:count], rest[count], rest[count + 1]
    held_ref, sems, arrays = rest[count + 2], rest[count + 3], rest[count + 4 :]
    copies = [
        pltpu.make_async_copy(remote[index], arrays[index], sems.at[index])
        for index in range(count)
    ]
    for copy in copies:
        copy.start()
    held_ref[...] = jnp.zeros_like(held_ref)
    for copy in copies:
        copy.wait()
    y, z, core = place_ref[0], place_ref[1], place_ref[2]
    for by_y in range(4):
        for by_z in range(4):
            if by_y == 0:
                array, base = arrays[by_z], 0
            else:
                array, base = arrays[3 + by_y + by_z // 2 * 3], by_z % 2 * BLK
            source = (((y - by_y) & 3) * 4 + ((z - by_z) & 3)) * 2 + core
            for entry in range(2 * MOST):
                code = code_ref[source * 2 * MOST + entry]

                @pl.when(code >= 0)
                def _():
                    page = code >> 6
                    slot = (code & 63) + entry // MOST * PAGES
                    row = pl.multiple_of(base + (page >> 1) * 2 * PAGE, 2 * PAGE)
                    rows = array[pl.ds(row, 2 * PAGE), :].astype(jnp.float32)
                    rows = jnp.where((page & 1) == 1, rows[PAGE:], rows[:PAGE])
                    held_ref[pl.ds(pl.multiple_of(slot * PAGE, PAGE), PAGE), :] = rows

    own_ref[...] = held_ref[: PAGES * PAGE].astype(jnp.bfloat16)
    pair_ref[...] = held_ref[PAGES * PAGE :].astype(jnp.bfloat16)


def fetch_pages(place, codes, arrays):
    out = jax.ShapeDtypeStruct((PAGES * PAGE, 2 * HD), jnp.bfloat16)
    return pl.pallas_call(
        page_kernel,
        in_specs=[pl.BlockSpec(memory_space=pltpu.SMEM)] * 2
        + [pl.BlockSpec(memory_space=pl.ANY)] * len(arrays),
        out_shape=(out, out),
        scratch_shapes=[
            pltpu.VMEM((2 * PAGES * PAGE, 2 * HD), jnp.float32),
            pltpu.SemaphoreType.DMA((len(arrays),)),
        ]
        + [pltpu.VMEM(array.shape, array.dtype) for array in arrays],
        compiler_params=params(),
        name="pages",
    )(place, codes, *arrays)


def moves(step):
    pairs = []
    for y in range(4):
        for z in range(4):
            for core in range(2):
                to_y, to_z, to_core = step(y, z, core)
                pairs.append(((y * 4 + z) * 2 + core, (to_y * 4 + to_z) * 2 + to_core))
    return pairs


def along_y(value, count):
    return lax.ppermute(value, "seq", moves(lambda y, z, c: ((y + count) % 4, z, c)))


def along_z(value, count):
    return lax.ppermute(value, "seq", moves(lambda y, z, c: (y, (z + count) % 4, c)))


def other_core(value):
    return lax.ppermute(value, "seq", moves(lambda y, z, c: (y, z, 1 - c)))


def page_codes(targets, me):
    index = jnp.arange(PAGES, dtype=jnp.int32)
    codes = []
    for owner in (me, me ^ 1):
        slot = targets - owner * PAGES
        match = (slot >= 0) & (slot < PAGES)
        before = match[:, None, :] & (index[None, :] < index[:, None])
        rank = jnp.sum(before.astype(jnp.int32), axis=2)
        code = index * 64 + slot + 1
        for entry in range(MOST):
            codes.append(jnp.sum(jnp.where(match & (rank == entry), code, 0), axis=1) - 1)
    return jnp.stack(codes, axis=1).reshape(-1)


def held_here(targets, me):
    mine = me * PAGES + jnp.arange(PAGES, dtype=jnp.int32)
    same_core = (jnp.arange(SEQ, dtype=jnp.int32) % 2 == me % 2)[:, None]
    match = (targets[None] == mine[:, None, None]) & same_core[None]
    return jnp.any(match, axis=(1, 2))


def spread(value, groups):
    by_z = {0: value}
    for count in (1, 2, 3):
        by_z[count] = along_z(value, count)
    by_y = []
    for group in groups:
        parts = [by_z[count] for count in group]
        parts = jnp.concatenate(parts, axis=0) if len(parts) > 1 else parts[0]
        by_y.append({count: along_y(parts, count) for count in (1, 3, 2)})
    return by_z, by_y


def project(normed, weight):
    return jnp.dot(normed, weight, preferred_element_type=jnp.float32).astype(jnp.bfloat16)


def attention_and_pages(me, codes, keep, normed, weight):
    core, z, y = me % 2, (me // 2) % 4, me // 8
    kv = project(normed, weight[:, GROUP * HD :])
    normed, kv = lax.optimization_barrier((normed, kv))
    by_z, (near, far) = spread(kv, ((0, 1), (2, 3)))
    own_queries = project(normed, weight[:, : GROUP * HD])
    pair_queries = other_core(own_queries)

    def flag(*conditions):
        return jnp.stack([jnp.asarray(value, jnp.int32) for value in conditions])

    state, queries = attend_first(core, own_queries, pair_queries, kv)
    state = attend_more(
        flag(z >= 1, z >= 2, z >= 3), queries, state, [by_z[1], by_z[2], by_z[3]]
    )
    state, near[3], near[2] = lax.optimization_barrier((state, near[3], near[2]))
    state = attend_more(
        flag(y >= 1, y >= 3, y >= 2), queries, state, [near[1], near[3], near[2]]
    )
    state, far[1], far[3] = lax.optimization_barrier((state, far[1], far[3]))
    state = attend_more(flag(y >= 1, y >= 3), queries, state, [far[1], far[3]])
    state, far[2] = lax.optimization_barrier((state, far[2]))
    own, sent = attend_more(flag(y >= 2), queries, state, [far[2]], split=True)
    got = other_core(sent)

    arrays = [by_z[count] for count in range(4)]
    arrays += [group[count] for group in (near, far) for count in (1, 2, 3)]
    place = jnp.stack([y, z, core])
    own_pages, sent_pages = fetch_pages(place, codes, arrays)
    got_pages = other_core(sent_pages)
    attention = finish(own, got)
    keep = keep.reshape(PAGES, 1, 1, 1)
    shape = (PAGES, PAGE, 2, HD)
    kv_cache = jnp.where(keep, own_pages.reshape(shape), got_pages.reshape(shape))
    return attention, kv_cache


def on_device(
    features,
    conv_weight,
    conv_bias,
    embed_weight,
    position_table,
    norm_gain,
    qkv_weight,
    page_owner,
    page_slot,
):
    me = lax.axis_index("seq").astype(jnp.int32)
    tensor = lax.axis_index("tensor").astype(jnp.int32)
    tensor_count = lax.axis_size("tensor")
    weight = lax.all_gather(qkv_weight, "seq", axis=0, tiled=True)
    parts = partial_latents(features, conv_weight)
    own = parts[: FRAMES * EXT].reshape(FRAMES, EXT * LAT)
    target = (page_owner * PAGES + page_slot).astype(jnp.float32)
    target = jnp.broadcast_to(target, (FRAMES, PAGES))
    message = jnp.concatenate([own, target], axis=1)
    message = jnp.pad(message, ((0, 0), (0, 512 - message.shape[1])))
    message = jnp.broadcast_to(message[:, None], (FRAMES, SEQ // FRAMES, 512)).reshape(SEQ, 512)
    message = lax.all_to_all(message, "seq", split_axis=0, concat_axis=0, tiled=True)
    gain = norm_gain.reshape(1, -1)
    message, gain = lax.optimization_barrier((message, gain))
    targets = message[:, EXT * LAT : EXT * LAT + PAGES].astype(jnp.int32)
    offset = tensor - me % (SEQ // FRAMES)
    latent = place_latents(message[:, : EXT * LAT].reshape(SEQ * EXT, LAT), offset)
    for bit in (1, 2, 4):
        swap = [(i, i ^ bit) for i in range(tensor_count)]
        latent = latent + lax.ppermute(latent, "tensor", swap)
    latent = latent + conv_bias[:, None]
    normed = normed_hidden(latent, embed_weight, position_table, gain)
    codes, keep = page_codes(targets, me), held_here(targets, me)
    normed, codes, keep = lax.optimization_barrier((normed, codes, keep))
    return attention_and_pages(me, codes, keep, normed, weight)


def solution(mesh):
    placed = (
        P(None, "tensor", "seq", None),
        P(),
        P(),
        P(),
        P("seq", None),
        P(),
        P("seq", "tensor"),
        P("seq"),
        P("seq"),
    )
    return jax.shard_map(
        on_device,
        mesh=mesh,
        in_specs=placed,
        out_specs=(P("seq", "tensor"), P("seq", None, None, "tensor")),
        check_vma=False,
    )
```

```python
import functools

import jax
import jax.numpy as jnp
import numpy as np
from jax import lax
from jax.experimental import pallas as pl
from jax.experimental.pallas import tpu as pltpu
from jax.sharding import PartitionSpec as P

HD = 128
PAGE = 8
GROUP = 4
LAT = 16
BLK = 320
PAGES = 40
MOST = 3
SEQ = 32
ROWS = 5
COLS = 2
FRAMES = 4
EXT = (ROWS + 2) * (COLS + 2)
TOK = 384
TILE = 256
QROWS = GROUP * BLK
STATE = HD + 8
VMEM = 24 * 1024 * 1024


def params(**extra):
    return pltpu.CompilerParams(vmem_limit_bytes=VMEM, **extra)


def cost(blocks):
    scores = blocks * 2 * QROWS * BLK
    return pl.CostEstimate(flops=4 * HD * scores, bytes_accessed=3 << 20, transcendentals=scores)


def roll_lanes(value, shift):
    shift = shift % value.shape[1]
    return pltpu.roll(value, shift, 1) if shift else value


def conv_kernel(feat_ref, weight_ref, out_ref, grid_ref):
    grid_ref[...] = jnp.zeros_like(grid_ref)
    for frame in range(FRAMES):
        for row in range(ROWS):
            start = frame * EXT + (row + 1) * (COLS + 2) + 1
            value = feat_ref[frame, row].astype(jnp.float32)
            grid_ref[start : start + COLS, :] = value / (1.0 + jnp.exp(-value))
    active = grid_ref[...].astype(jnp.bfloat16)
    product = lax.dot_general(
        weight_ref[...], active, (((1,), (1,)), ((), ())), preferred_element_type=jnp.float32
    )
    lane = lax.broadcasted_iota(jnp.int32, (LAT, 128), 1)
    total = jnp.zeros((LAT, 128), jnp.float32)
    for time in range(3):
        part = jnp.zeros((LAT, 128), jnp.float32)
        for row in range(3):
            for col in range(3):
                index = (time * 3 + row) * 3 + col
                piece = product[index * LAT : (index + 1) * LAT, :]
                part = part + roll_lanes(piece, -((row - 1) * (COLS + 2) + col - 1))
        delay = (2 - time) * EXT
        if delay:
            part = jnp.where(lane >= delay, roll_lanes(part, delay), 0.0)
        total = total + part
    padded = jnp.concatenate([total, jnp.zeros((128 - LAT, 128), jnp.float32)], axis=0)
    out_ref[...] = jnp.transpose(padded)[:, :LAT]


def partial_latents(features, conv_weight):
    weight = jnp.transpose(conv_weight, (0, 1, 2, 4, 3)).reshape(-1, conv_weight.shape[3])
    return pl.pallas_call(
        conv_kernel,
        out_shape=jax.ShapeDtypeStruct((128, LAT), jnp.float32),
        scratch_shapes=[pltpu.VMEM((128, features.shape[-1]), jnp.float32)],
        compiler_params=params(),
        name="conv",
    )(features, weight)


def split_three(value):
    high = value.astype(jnp.bfloat16)
    rest = value - high.astype(jnp.float32)
    middle = rest.astype(jnp.bfloat16)
    low = (rest - middle.astype(jnp.float32)).astype(jnp.bfloat16)
    return high, middle, low


def place_kernel(offset_ref, parts_ref, token_ref, out_ref):
    count = parts_ref.shape[0]
    token = lax.broadcasted_iota(jnp.int32, (TOK, count), 0) - offset_ref[0] * BLK
    pick = jnp.where(token == token_ref[...], 1.0, 0.0).astype(jnp.bfloat16)
    total = jnp.zeros((LAT, TOK), jnp.float32)
    for part in reversed(split_three(parts_ref[...])):
        total = total + lax.dot_general(
            part, pick, (((0,), (1,)), ((), ())), preferred_element_type=jnp.float32
        )
    out_ref[...] = total


def place_table():
    row = np.arange(ROWS + 2).reshape(1, -1, 1) - 1
    col = np.arange(COLS + 2).reshape(1, 1, -1) - 1
    width = np.arange(SEQ).reshape(-1, 1, 1) * COLS + col
    inside = (width >= 0) & (width < SEQ * COLS)
    token = np.where(inside, row * SEQ * COLS + width, -(1 << 20))
    return token.astype(np.int32).reshape(1, SEQ * EXT)


def place_latents(parts, offset):
    return pl.pallas_call(
        place_kernel,
        in_specs=[pl.BlockSpec(memory_space=pltpu.SMEM)]
        + [pl.BlockSpec(memory_space=pltpu.VMEM)] * 2,
        out_shape=jax.ShapeDtypeStruct((LAT, TOK), jnp.float32),
        compiler_params=params(),
        name="place",
    )(offset.reshape(1), parts, jnp.asarray(place_table()))


def hidden_kernel(latent_ref, embed_ref, table_ref, gain_ref, out_ref, hid_ref, sq_ref):
    step = pl.program_id(0)
    width = table_ref.shape[1]
    latent = latent_ref[...][:, :BLK]
    latent = jnp.concatenate(split_three(latent), axis=0)
    embed = embed_ref[...]
    hidden = lax.dot_general(
        latent,
        jnp.concatenate([embed, embed, embed], axis=0),
        (((0,), (0,)), ((), ())),
        preferred_element_type=jnp.float32,
    ) + table_ref[...].astype(jnp.float32)
    hid_ref[step] = hidden
    squares = jnp.zeros((BLK, 128), jnp.float32)
    for lane in range(0, width, 128):
        piece = hidden[:, lane : lane + 128]
        squares = squares + piece * piece

    @pl.when(step == 0)
    def _():
        sq_ref[...] = squares

    @pl.when(step > 0)
    def _():
        sq_ref[...] += squares

    @pl.when(step == pl.num_programs(0) - 1)
    def _():
        count = hid_ref.shape[0]
        mean = jnp.sum(sq_ref[...], axis=1, keepdims=True) / (count * width)
        factor = lax.rsqrt(mean + 1e-05)
        for tile in range(count):
            gain = gain_ref[:, tile * width : (tile + 1) * width].astype(jnp.float32)
            normed = hid_ref[tile] * factor * gain
            out_ref[:, tile * width : (tile + 1) * width] = normed.astype(jnp.bfloat16)


def normed_hidden(latent, embed_weight, position_table, gain):
    depth = position_table.shape[1]
    steps = 8
    width = depth // steps
    return pl.pallas_call(
        hidden_kernel,
        grid=(steps,),
        in_specs=[
            pl.BlockSpec((LAT, TOK), lambda i: (0, 0)),
            pl.BlockSpec((LAT, width), lambda i: (0, i)),
            pl.BlockSpec((BLK, width), lambda i: (0, i)),
            pl.BlockSpec((1, depth), lambda i: (0, 0)),
        ],
        out_specs=pl.BlockSpec((BLK, depth), lambda i: (0, 0)),
        out_shape=jax.ShapeDtypeStruct((BLK, depth), jnp.bfloat16),
        scratch_shapes=[
            pltpu.VMEM((steps, BLK, width), jnp.float32),
            pltpu.VMEM((BLK, 128), jnp.float32),
        ],
        compiler_params=params(dimension_semantics=("arbitrary",)),
        name="hidden",
    )(latent, embed_weight, position_table, gain)


def attend_block(masked, partner_full, keys, values, q_ref, state_ref):
    scale = 1.4426950408889634 / HD**0.5
    tiles = 2 * QROWS // TILE

    def score(tile):
        return lax.dot_general(
            keys,
            q_ref[tile * TILE : (tile + 1) * TILE, :],
            (((1,), (1,)), ((), ())),
            preferred_element_type=jnp.float32,
        )

    upcoming = score(0)
    for tile in range(tiles):
        scores = upcoming
        if tile + 1 < tiles:
            upcoming = score(tile + 1)
        cut = slice(tile * TILE, (tile + 1) * TILE)
        allowed = None
        if masked:
            key = lax.broadcasted_iota(jnp.int32, scores.shape, 0)
            query = tile * TILE + lax.broadcasted_iota(jnp.int32, (1, TILE), 1)
            if tile * TILE >= QROWS:
                query = jnp.where(partner_full, BLK, -1) + 0 * query
            else:
                for head in range(GROUP - 1, 0, -1):
                    query = jnp.where(query >= head * BLK, query - head * BLK, query)
            allowed = key <= query
            scores = jnp.where(allowed, scores, -1e30)
        peak = jnp.max(scores, axis=0, keepdims=True)
        if masked:
            best = peak
        else:
            old = state_ref[HD : HD + 1, cut]
            best = jnp.maximum(old, peak)
            factor = jnp.exp2((old - best) * scale)
        weights = jnp.exp2((scores - best) * scale)
        if masked:
            weights = jnp.where(allowed, weights, 0.0)
        total = jnp.sum(weights, axis=0, keepdims=True)
        summed = lax.dot_general(
            values,
            weights.astype(jnp.bfloat16),
            (((0,), (0,)), ((), ())),
            preferred_element_type=jnp.float32,
        )
        if not masked:
            total = total + state_ref[HD + 1 : HD + 2, cut] * factor
            summed = summed + state_ref[:HD, cut] * factor
        state_ref[HD : HD + 1, cut] = best
        state_ref[HD + 1 : HD + 2, cut] = total
        state_ref[:HD, cut] = summed


def first_kernel(core_ref, own_ref, pair_ref, kv_ref, state_ref, q_ref):
    for index, ref in enumerate((own_ref, pair_ref)):
        for head in range(GROUP):
            start = (index * GROUP + head) * BLK
            q_ref[start : start + BLK, :] = ref[:, head * HD : (head + 1) * HD]
    state_ref[HD + 2 :, :] = jnp.zeros((STATE - HD - 2, 2 * QROWS), jnp.float32)
    attend_block(True, core_ref[0] == 0, kv_ref[:, :HD], kv_ref[:, HD:], q_ref, state_ref)


def attend_first(core, own, pair, kv):
    return pl.pallas_call(
        first_kernel,
        in_specs=[pl.BlockSpec(memory_space=pltpu.SMEM)]
        + [pl.BlockSpec(memory_space=pltpu.VMEM)] * 3,
        out_shape=(
            jax.ShapeDtypeStruct((STATE, 2 * QROWS), jnp.float32),
            jax.ShapeDtypeStruct((2 * QROWS, HD), jnp.bfloat16),
        ),
        compiler_params=params(),
        cost_estimate=cost(1),
        name="first",
    )(core.reshape(1), own, pair, kv)


def more_kernel(count, split, flag_ref, q_ref, state_ref, *rest):
    arrays, rest = rest[:count], rest[count:]
    if split:
        own_out_ref, pair_out_ref, held_ref, sems, work_ref = rest
    else:
        work_ref, held_ref, sems = rest
    copies = []
    for index, array in enumerate(arrays):
        copies.append(pltpu.make_async_copy(array, held_ref.at[index], sems.at[index]))
        copies[-1].start()
    work_ref[...] = state_ref[...]
    for copy in copies:
        copy.wait()

    def body(index, carry):
        @pl.when(flag_ref[index] != 0)
        def _():
            keys, values = held_ref[index, :, :HD], held_ref[index, :, HD:]
            attend_block(False, None, keys, values, q_ref, work_ref)

        return carry

    lax.fori_loop(0, count, body, 0)
    if split:
        own_out_ref[...] = work_ref[:, :QROWS]
        pair_out_ref[...] = work_ref[:, QROWS:]


def attend_more(flags, queries, state, arrays, split=False):
    unit, count = arrays[0].shape[0], len(arrays)
    half = jax.ShapeDtypeStruct((STATE, QROWS), jnp.float32)
    whole = jax.ShapeDtypeStruct((STATE, 2 * QROWS), jnp.float32)
    scratch = [
        pltpu.VMEM((count, unit, 2 * HD), jnp.bfloat16),
        pltpu.SemaphoreType.DMA((count,)),
    ]
    if split:
        scratch.append(pltpu.VMEM((STATE, 2 * QROWS), jnp.float32))
    return pl.pallas_call(
        functools.partial(more_kernel, count, split),
        in_specs=[pl.BlockSpec(memory_space=pltpu.SMEM)]
        + [pl.BlockSpec(memory_space=pltpu.VMEM)] * 2
        + [pl.BlockSpec(memory_space=pl.ANY)] * count,
        out_shape=(half, half) if split else whole,
        scratch_shapes=scratch,
        compiler_params=params(),
        cost_estimate=cost(count * unit // BLK),
        name="more",
    )(flags, queries, state, *arrays)


def finish_kernel(own_ref, got_ref, out_ref, row_ref):
    scale = 1.4426950408889634 / HD**0.5
    for start in range(0, QROWS, TILE):
        cut = slice(start, start + TILE)
        first, second = own_ref[HD : HD + 1, cut], got_ref[HD : HD + 1, cut]
        best = jnp.maximum(first, second)
        first = jnp.exp2((first - best) * scale)
        second = jnp.exp2((second - best) * scale)
        total = own_ref[HD + 1 : HD + 2, cut] * first + got_ref[HD + 1 : HD + 2, cut] * second
        summed = own_ref[:HD, cut] * first + got_ref[:HD, cut] * second
        row_ref[cut, :] = jnp.transpose(summed / total)
    for head in range(GROUP):
        rows = row_ref[head * BLK : (head + 1) * BLK, :]
        out_ref[:, head * HD : (head + 1) * HD] = rows.astype(jnp.bfloat16)


def finish(own, got):
    return pl.pallas_call(
        finish_kernel,
        out_shape=jax.ShapeDtypeStruct((BLK, GROUP * HD), jnp.bfloat16),
        scratch_shapes=[pltpu.VMEM((QROWS, HD), jnp.float32)],
        compiler_params=params(),
        name="finish",
    )(own, got)


def page_kernel(place_ref, code_ref, *rest):
    count = (len(rest) - 4) // 2
    remote, own_ref, pair_ref = rest[:count], rest[count], rest[count + 1]
    held_ref, sems, arrays = rest[count + 2], rest[count + 3], rest[count + 4 :]
    copies = [
        pltpu.make_async_copy(remote[index], arrays[index], sems.at[index])
        for index in range(count)
    ]
    for copy in copies:
        copy.start()
    held_ref[...] = jnp.zeros_like(held_ref)
    for copy in copies:
        copy.wait()
    y, z, core = place_ref[0], place_ref[1], place_ref[2]
    for by_y in range(4):
        for by_z in range(4):
            if by_y == 0:
                array, base = arrays[by_z], 0
            else:
                array, base = arrays[3 + by_y + (0, 3, 6, 3)[by_z]], by_z // 3 * BLK
            source = (((y - by_y) & 3) * 4 + ((z - by_z) & 3)) * 2 + core
            for entry in range(2 * MOST):
                code = code_ref[source * 2 * MOST + entry]

                @pl.when(code >= 0)
                def _():
                    page = code >> 6
                    slot = (code & 63) + entry // MOST * PAGES
                    row = pl.multiple_of(base + (page >> 1) * 2 * PAGE, 2 * PAGE)
                    rows = array[pl.ds(row, 2 * PAGE), :].astype(jnp.float32)
                    rows = jnp.where((page & 1) == 1, rows[PAGE:], rows[:PAGE])
                    held_ref[pl.ds(pl.multiple_of(slot * PAGE, PAGE), PAGE), :] = rows

    own_ref[...] = held_ref[: PAGES * PAGE].astype(jnp.bfloat16)
    pair_ref[...] = held_ref[PAGES * PAGE :].astype(jnp.bfloat16)


def fetch_pages(place, codes, arrays):
    out = jax.ShapeDtypeStruct((PAGES * PAGE, 2 * HD), jnp.bfloat16)
    return pl.pallas_call(
        page_kernel,
        in_specs=[pl.BlockSpec(memory_space=pltpu.SMEM)] * 2
        + [pl.BlockSpec(memory_space=pl.ANY)] * len(arrays),
        out_shape=(out, out),
        scratch_shapes=[
            pltpu.VMEM((2 * PAGES * PAGE, 2 * HD), jnp.float32),
            pltpu.SemaphoreType.DMA((len(arrays),)),
        ]
        + [pltpu.VMEM(array.shape, array.dtype) for array in arrays],
        compiler_params=params(),
        name="pages",
    )(place, codes, *arrays)


def moves(step):
    pairs = []
    for y in range(4):
        for z in range(4):
            for core in range(2):
                to_y, to_z, to_core = step(y, z, core)
                pairs.append(((y * 4 + z) * 2 + core, (to_y * 4 + to_z) * 2 + to_core))
    return pairs


def along_y(value, count):
    return lax.ppermute(value, "seq", moves(lambda y, z, c: ((y + count) % 4, z, c)))


def along_z(value, count):
    return lax.ppermute(value, "seq", moves(lambda y, z, c: (y, (z + count) % 4, c)))


def other_core(value):
    return lax.ppermute(value, "seq", moves(lambda y, z, c: (y, z, 1 - c)))


def page_codes(targets, me):
    index = jnp.arange(PAGES, dtype=jnp.int32)
    codes = []
    for owner in (me, me ^ 1):
        slot = targets - owner * PAGES
        match = (slot >= 0) & (slot < PAGES)
        before = match[:, None, :] & (index[None, :] < index[:, None])
        rank = jnp.sum(before.astype(jnp.int32), axis=2)
        code = index * 64 + slot + 1
        for entry in range(MOST):
            codes.append(jnp.sum(jnp.where(match & (rank == entry), code, 0), axis=1) - 1)
    return jnp.stack(codes, axis=1).reshape(-1)


def held_here(targets, me):
    mine = me * PAGES + jnp.arange(PAGES, dtype=jnp.int32)
    same_core = (jnp.arange(SEQ, dtype=jnp.int32) % 2 == me % 2)[:, None]
    match = (targets[None] == mine[:, None, None]) & same_core[None]
    return jnp.any(match, axis=(1, 2))


def project(normed, weight):
    return jnp.dot(normed, weight, preferred_element_type=jnp.float32).astype(jnp.bfloat16)


def attention_and_pages(me, codes, keep, normed, weight):
    core, z, y = me % 2, (me // 2) % 4, me // 8
    kv = project(normed, weight[:, GROUP * HD :])
    normed, kv = lax.optimization_barrier((normed, kv))
    by_z = {0: kv, 1: along_z(kv, 1), 3: along_z(kv, 3)}
    none = {count: along_y(kv, count) for count in (1, 3, 2)}
    own_queries = project(normed, weight[:, : GROUP * HD])
    pair_queries = other_core(own_queries)

    def flag(*conditions):
        return jnp.stack([jnp.asarray(value, jnp.int32) for value in conditions])

    state, queries = attend_first(core, own_queries, pair_queries, kv)
    state, by_z[1], by_z[3] = lax.optimization_barrier((state, by_z[1], by_z[3]))
    kv, odd = lax.optimization_barrier((kv, jnp.concatenate([by_z[1], by_z[3]], axis=0)))
    by_z[2] = along_z(kv, 2)
    odd = {count: along_y(odd, count) for count in (1, 3, 2)}
    state = attend_more(
        flag(y >= 1, y >= 3, y >= 2), queries, state, [none[1], none[3], none[2]]
    )
    state, by_z[2] = lax.optimization_barrier((state, by_z[2]))
    two = {count: along_y(by_z[2], count) for count in (1, 3, 2)}
    state = attend_more(
        flag(z >= 1, z >= 3, z >= 2), queries, state, [by_z[1], by_z[3], by_z[2]]
    )
    state, odd[1], odd[3], odd[2] = lax.optimization_barrier((state, odd[1], odd[3], odd[2]))
    state = attend_more(flag(y >= 1, y >= 3, y >= 2), queries, state, [odd[1], odd[3], odd[2]])
    state, two[1], two[3], two[2] = lax.optimization_barrier((state, two[1], two[3], two[2]))
    own, sent = attend_more(
        flag(y >= 1, y >= 3, y >= 2), queries, state, [two[1], two[3], two[2]], split=True
    )
    got = other_core(sent)

    arrays = [by_z[count] for count in range(4)]
    arrays += [group[count] for group in (none, odd, two) for count in (1, 2, 3)]
    place = jnp.stack([y, z, core])
    own_pages, sent_pages = fetch_pages(place, codes, arrays)
    got_pages = other_core(sent_pages)
    attention = finish(own, got)
    keep = keep.reshape(PAGES, 1, 1, 1)
    shape = (PAGES, PAGE, 2, HD)
    kv_cache = jnp.where(keep, own_pages.reshape(shape), got_pages.reshape(shape))
    return attention, kv_cache


def on_device(
    features,
    conv_weight,
    conv_bias,
    embed_weight,
    position_table,
    norm_gain,
    qkv_weight,
    page_owner,
    page_slot,
):
    me = lax.axis_index("seq").astype(jnp.int32)
    tensor = lax.axis_index("tensor").astype(jnp.int32)
    tensor_count = lax.axis_size("tensor")
    weight = lax.all_gather(qkv_weight, "seq", axis=0, tiled=True)
    parts = partial_latents(features, conv_weight)
    own = parts[: FRAMES * EXT].reshape(FRAMES, EXT * LAT)
    target = (page_owner * PAGES + page_slot).astype(jnp.float32)
    target = jnp.broadcast_to(target, (FRAMES, PAGES))
    message = jnp.concatenate([own, target], axis=1)
    message = jnp.pad(message, ((0, 0), (0, 512 - message.shape[1])))
    message = jnp.broadcast_to(message[:, None], (FRAMES, SEQ // FRAMES, 512)).reshape(SEQ, 512)
    message = lax.all_to_all(message, "seq", split_axis=0, concat_axis=0, tiled=True)
    gain = norm_gain.reshape(1, -1)
    message, gain = lax.optimization_barrier((message, gain))
    targets = message[:, EXT * LAT : EXT * LAT + PAGES].astype(jnp.int32)
    offset = tensor - me % (SEQ // FRAMES)
    latent = place_latents(message[:, : EXT * LAT].reshape(SEQ * EXT, LAT), offset)
    for bit in (1, 2, 4):
        swap = [(i, i ^ bit) for i in range(tensor_count)]
        latent = latent + lax.ppermute(latent, "tensor", swap)
    latent = latent + conv_bias[:, None]
    normed = normed_hidden(latent, embed_weight, position_table, gain)
    codes, keep = page_codes(targets, me), held_here(targets, me)
    normed, codes, keep = lax.optimization_barrier((normed, codes, keep))
    return attention_and_pages(me, codes, keep, normed, weight)


def solution(mesh):
    placed = (
        P(None, "tensor", "seq", None),
        P(),
        P(),
        P(),
        P("seq", None),
        P(),
        P("seq", "tensor"),
        P("seq"),
        P("seq"),
    )
    return jax.shard_map(
        on_device,
        mesh=mesh,
        in_specs=placed,
        out_specs=(P("seq", "tensor"), P("seq", None, None, "tensor")),
        check_vma=False,
    )
```

```python
import functools

import jax
import jax.numpy as jnp
import numpy as np
from jax import lax
from jax.experimental import pallas as pl
from jax.experimental.pallas import tpu as pltpu
from jax.sharding import PartitionSpec as P

HD = 128
PAGE = 8
GROUP = 4
LAT = 16
BLK = 320
PAGES = 40
MOST = 3
SEQ = 32
ROWS = 5
COLS = 2
FRAMES = 4
EXT = (ROWS + 2) * (COLS + 2)
TOK = 384
TILE = 256
QROWS = GROUP * BLK
STATE = HD + 8
VMEM = 24 * 1024 * 1024


def params(**extra):
    return pltpu.CompilerParams(vmem_limit_bytes=VMEM, **extra)


def cost(blocks):
    scores = blocks * 2 * QROWS * BLK
    return pl.CostEstimate(flops=4 * HD * scores, bytes_accessed=3 << 20, transcendentals=scores)


def roll_lanes(value, shift):
    shift = shift % value.shape[1]
    return pltpu.roll(value, shift, 1) if shift else value


def conv_kernel(feat_ref, weight_ref, out_ref, grid_ref):
    grid_ref[...] = jnp.zeros_like(grid_ref)
    for frame in range(FRAMES):
        for row in range(ROWS):
            start = frame * EXT + (row + 1) * (COLS + 2) + 1
            value = feat_ref[frame, row].astype(jnp.float32)
            grid_ref[start : start + COLS, :] = value / (1.0 + jnp.exp(-value))
    active = grid_ref[...].astype(jnp.bfloat16)
    product = lax.dot_general(
        weight_ref[...], active, (((1,), (1,)), ((), ())), preferred_element_type=jnp.float32
    )
    lane = lax.broadcasted_iota(jnp.int32, (LAT, 128), 1)
    total = jnp.zeros((LAT, 128), jnp.float32)
    for time in range(3):
        part = jnp.zeros((LAT, 128), jnp.float32)
        for row in range(3):
            for col in range(3):
                index = (time * 3 + row) * 3 + col
                piece = product[index * LAT : (index + 1) * LAT, :]
                part = part + roll_lanes(piece, -((row - 1) * (COLS + 2) + col - 1))
        delay = (2 - time) * EXT
        if delay:
            part = jnp.where(lane >= delay, roll_lanes(part, delay), 0.0)
        total = total + part
    padded = jnp.concatenate([total, jnp.zeros((128 - LAT, 128), jnp.float32)], axis=0)
    out_ref[...] = jnp.transpose(padded)[:, :LAT]


def partial_latents(features, conv_weight):
    weight = jnp.transpose(conv_weight, (0, 1, 2, 4, 3)).reshape(-1, conv_weight.shape[3])
    return pl.pallas_call(
        conv_kernel,
        out_shape=jax.ShapeDtypeStruct((128, LAT), jnp.float32),
        scratch_shapes=[pltpu.VMEM((128, features.shape[-1]), jnp.float32)],
        compiler_params=params(),
        name="conv",
    )(features, weight)


def split_three(value):
    high = value.astype(jnp.bfloat16)
    rest = value - high.astype(jnp.float32)
    middle = rest.astype(jnp.bfloat16)
    low = (rest - middle.astype(jnp.float32)).astype(jnp.bfloat16)
    return high, middle, low


def place_kernel(offset_ref, parts_ref, token_ref, out_ref):
    count = parts_ref.shape[0]
    token = lax.broadcasted_iota(jnp.int32, (TOK, count), 0) - offset_ref[0] * BLK
    pick = jnp.where(token == token_ref[...], 1.0, 0.0).astype(jnp.bfloat16)
    total = jnp.zeros((LAT, TOK), jnp.float32)
    for part in reversed(split_three(parts_ref[...])):
        total = total + lax.dot_general(
            part, pick, (((0,), (1,)), ((), ())), preferred_element_type=jnp.float32
        )
    out_ref[...] = total


def place_table():
    row = np.arange(ROWS + 2).reshape(1, -1, 1) - 1
    col = np.arange(COLS + 2).reshape(1, 1, -1) - 1
    width = np.arange(SEQ).reshape(-1, 1, 1) * COLS + col
    inside = (width >= 0) & (width < SEQ * COLS)
    token = np.where(inside, row * SEQ * COLS + width, -(1 << 20))
    return token.astype(np.int32).reshape(1, SEQ * EXT)


def place_latents(parts, offset):
    return pl.pallas_call(
        place_kernel,
        in_specs=[pl.BlockSpec(memory_space=pltpu.SMEM)]
        + [pl.BlockSpec(memory_space=pltpu.VMEM)] * 2,
        out_shape=jax.ShapeDtypeStruct((LAT, TOK), jnp.float32),
        compiler_params=params(),
        name="place",
    )(offset.reshape(1), parts, jnp.asarray(place_table()))


def hidden_kernel(latent_ref, embed_ref, table_ref, gain_ref, out_ref, hid_ref, sq_ref):
    step = pl.program_id(0)
    width = table_ref.shape[1]
    latent = latent_ref[...][:, :BLK]
    latent = jnp.concatenate(split_three(latent), axis=0)
    embed = embed_ref[...]
    hidden = lax.dot_general(
        latent,
        jnp.concatenate([embed, embed, embed], axis=0),
        (((0,), (0,)), ((), ())),
        preferred_element_type=jnp.float32,
    ) + table_ref[...].astype(jnp.float32)
    hid_ref[step] = hidden
    squares = jnp.zeros((BLK, 128), jnp.float32)
    for lane in range(0, width, 128):
        piece = hidden[:, lane : lane + 128]
        squares = squares + piece * piece

    @pl.when(step == 0)
    def _():
        sq_ref[...] = squares

    @pl.when(step > 0)
    def _():
        sq_ref[...] += squares

    @pl.when(step == pl.num_programs(0) - 1)
    def _():
        count = hid_ref.shape[0]
        mean = jnp.sum(sq_ref[...], axis=1, keepdims=True) / (count * width)
        factor = lax.rsqrt(mean + 1e-05)
        for tile in range(count):
            gain = gain_ref[:, tile * width : (tile + 1) * width].astype(jnp.float32)
            normed = hid_ref[tile] * factor * gain
            out_ref[:, tile * width : (tile + 1) * width] = normed.astype(jnp.bfloat16)


def normed_hidden(latent, embed_weight, position_table, gain):
    depth = position_table.shape[1]
    steps = 8
    width = depth // steps
    return pl.pallas_call(
        hidden_kernel,
        grid=(steps,),
        in_specs=[
            pl.BlockSpec((LAT, TOK), lambda i: (0, 0)),
            pl.BlockSpec((LAT, width), lambda i: (0, i)),
            pl.BlockSpec((BLK, width), lambda i: (0, i)),
            pl.BlockSpec((1, depth), lambda i: (0, 0)),
        ],
        out_specs=pl.BlockSpec((BLK, depth), lambda i: (0, 0)),
        out_shape=jax.ShapeDtypeStruct((BLK, depth), jnp.bfloat16),
        scratch_shapes=[
            pltpu.VMEM((steps, BLK, width), jnp.float32),
            pltpu.VMEM((BLK, 128), jnp.float32),
        ],
        compiler_params=params(dimension_semantics=("arbitrary",)),
        name="hidden",
    )(latent, embed_weight, position_table, gain)


def attend_block(masked, partner_full, keys, values, q_ref, state_ref):
    scale = 1.4426950408889634 / HD**0.5
    tiles = 2 * QROWS // TILE

    def score(tile):
        return lax.dot_general(
            keys,
            q_ref[tile * TILE : (tile + 1) * TILE, :],
            (((1,), (1,)), ((), ())),
            preferred_element_type=jnp.float32,
        )

    upcoming = score(0)
    for tile in range(tiles):
        scores = upcoming
        if tile + 1 < tiles:
            upcoming = score(tile + 1)
        cut = slice(tile * TILE, (tile + 1) * TILE)
        allowed = None
        if masked:
            key = lax.broadcasted_iota(jnp.int32, scores.shape, 0)
            query = tile * TILE + lax.broadcasted_iota(jnp.int32, (1, TILE), 1)
            if tile * TILE >= QROWS:
                query = jnp.where(partner_full, BLK, -1) + 0 * query
            else:
                for head in range(GROUP - 1, 0, -1):
                    query = jnp.where(query >= head * BLK, query - head * BLK, query)
            allowed = key <= query
            scores = jnp.where(allowed, scores, -1e30)
        peak = jnp.max(scores, axis=0, keepdims=True)
        if masked:
            best = peak
        else:
            old = state_ref[HD : HD + 1, cut]
            best = jnp.maximum(old, peak)
            factor = jnp.exp2((old - best) * scale)
        weights = jnp.exp2((scores - best) * scale)
        if masked:
            weights = jnp.where(allowed, weights, 0.0)
        total = jnp.sum(weights, axis=0, keepdims=True)
        summed = lax.dot_general(
            values,
            weights.astype(jnp.bfloat16),
            (((0,), (0,)), ((), ())),
            preferred_element_type=jnp.float32,
        )
        if not masked:
            total = total + state_ref[HD + 1 : HD + 2, cut] * factor
            summed = summed + state_ref[:HD, cut] * factor
        state_ref[HD : HD + 1, cut] = best
        state_ref[HD + 1 : HD + 2, cut] = total
        state_ref[:HD, cut] = summed


def first_kernel(core_ref, own_ref, pair_ref, kv_ref, state_ref, q_ref):
    for index, ref in enumerate((own_ref, pair_ref)):
        for head in range(GROUP):
            start = (index * GROUP + head) * BLK
            q_ref[start : start + BLK, :] = ref[:, head * HD : (head + 1) * HD]
    state_ref[HD + 2 :, :] = jnp.zeros((STATE - HD - 2, 2 * QROWS), jnp.float32)
    attend_block(True, core_ref[0] == 0, kv_ref[:, :HD], kv_ref[:, HD:], q_ref, state_ref)


def attend_first(core, own, pair, kv):
    return pl.pallas_call(
        first_kernel,
        in_specs=[pl.BlockSpec(memory_space=pltpu.SMEM)]
        + [pl.BlockSpec(memory_space=pltpu.VMEM)] * 3,
        out_shape=(
            jax.ShapeDtypeStruct((STATE, 2 * QROWS), jnp.float32),
            jax.ShapeDtypeStruct((2 * QROWS, HD), jnp.bfloat16),
        ),
        compiler_params=params(),
        cost_estimate=cost(1),
        name="first",
    )(core.reshape(1), own, pair, kv)


def more_kernel(count, split, flag_ref, q_ref, state_ref, *rest):
    arrays, rest = rest[:count], rest[count:]
    if split:
        own_out_ref, pair_out_ref, held_ref, sems, work_ref = rest
    else:
        work_ref, held_ref, sems = rest
    copies = []
    for index, array in enumerate(arrays):
        unit = array.shape[0]
        held = held_ref.at[pl.ds(index * unit, unit), :]
        copies.append(pltpu.make_async_copy(array, held, sems.at[index]))
        copies[-1].start()
    work_ref[...] = state_ref[...]
    for copy in copies:
        copy.wait()

    every = jnp.int32(unit == BLK)
    for index in range(count):
        every = every * flag_ref[index]

    if unit == BLK:

        @pl.when(every != 0)
        def _():
            attend_block(False, None, held_ref[:, :HD], held_ref[:, HD:], q_ref, work_ref)

    def body(index, carry):
        @pl.when(flag_ref[index] != 0)
        def _():
            rows = pl.ds(pl.multiple_of(index * unit, unit), unit)
            attend_block(False, None, held_ref[rows, :HD], held_ref[rows, HD:], q_ref, work_ref)

        return carry

    @pl.when(every == 0)
    def _():
        lax.fori_loop(0, count, body, 0)

    if split:
        own_out_ref[...] = work_ref[:, :QROWS]
        pair_out_ref[...] = work_ref[:, QROWS:]


def attend_more(flags, queries, state, arrays, split=False):
    unit, count = arrays[0].shape[0], len(arrays)
    half = jax.ShapeDtypeStruct((STATE, QROWS), jnp.float32)
    whole = jax.ShapeDtypeStruct((STATE, 2 * QROWS), jnp.float32)
    scratch = [
        pltpu.VMEM((count * unit, 2 * HD), jnp.bfloat16),
        pltpu.SemaphoreType.DMA((count,)),
    ]
    if split:
        scratch.append(pltpu.VMEM((STATE, 2 * QROWS), jnp.float32))
    return pl.pallas_call(
        functools.partial(more_kernel, count, split),
        in_specs=[pl.BlockSpec(memory_space=pltpu.SMEM)]
        + [pl.BlockSpec(memory_space=pltpu.VMEM)] * 2
        + [pl.BlockSpec(memory_space=pl.ANY)] * count,
        out_shape=(half, half) if split else whole,
        scratch_shapes=scratch,
        compiler_params=params(),
        cost_estimate=cost(count * unit // BLK),
        name="more",
    )(flags, queries, state, *arrays)


def finish_kernel(own_ref, got_ref, out_ref, row_ref):
    scale = 1.4426950408889634 / HD**0.5
    for start in range(0, QROWS, TILE):
        cut = slice(start, start + TILE)
        first, second = own_ref[HD : HD + 1, cut], got_ref[HD : HD + 1, cut]
        best = jnp.maximum(first, second)
        first = jnp.exp2((first - best) * scale)
        second = jnp.exp2((second - best) * scale)
        total = own_ref[HD + 1 : HD + 2, cut] * first + got_ref[HD + 1 : HD + 2, cut] * second
        summed = own_ref[:HD, cut] * first + got_ref[:HD, cut] * second
        row_ref[cut, :] = jnp.transpose(summed / total)
    for head in range(GROUP):
        rows = row_ref[head * BLK : (head + 1) * BLK, :]
        out_ref[:, head * HD : (head + 1) * HD] = rows.astype(jnp.bfloat16)


def finish(own, got):
    return pl.pallas_call(
        finish_kernel,
        out_shape=jax.ShapeDtypeStruct((BLK, GROUP * HD), jnp.bfloat16),
        scratch_shapes=[pltpu.VMEM((QROWS, HD), jnp.float32)],
        compiler_params=params(),
        name="finish",
    )(own, got)


def page_kernel(place_ref, code_ref, *rest):
    count = (len(rest) - 4) // 2
    remote, own_ref, pair_ref = rest[:count], rest[count], rest[count + 1]
    held_ref, sems, arrays = rest[count + 2], rest[count + 3], rest[count + 4 :]
    copies = [
        pltpu.make_async_copy(remote[index], arrays[index], sems.at[index])
        for index in range(count)
    ]
    for copy in copies:
        copy.start()
    held_ref[...] = jnp.zeros_like(held_ref)
    y, z, core = place_ref[0], place_ref[1], place_ref[2]
    waited = set()
    for by_y in range(4):
        for by_z in range(4):
            if by_y == 0:
                index, base = by_z, 0
            else:
                index, base = 3 + by_y + (0, 3, 6, 3)[by_z], by_z // 3 * BLK
            if index not in waited:
                copies[index].wait()
                waited.add(index)
            array = arrays[index]
            source = (((y - by_y) & 3) * 4 + ((z - by_z) & 3)) * 2 + core
            for entry in range(2 * MOST):
                code = code_ref[source * 2 * MOST + entry]

                @pl.when(code >= 0)
                def _():
                    page = code >> 6
                    slot = (code & 63) + entry // MOST * PAGES
                    row = pl.multiple_of(base + (page >> 1) * 2 * PAGE, 2 * PAGE)
                    rows = array[pl.ds(row, 2 * PAGE), :].astype(jnp.float32)
                    rows = jnp.where((page & 1) == 1, rows[PAGE:], rows[:PAGE])
                    held_ref[pl.ds(pl.multiple_of(slot * PAGE, PAGE), PAGE), :] = rows

    own_ref[...] = held_ref[: PAGES * PAGE].astype(jnp.bfloat16)
    pair_ref[...] = held_ref[PAGES * PAGE :].astype(jnp.bfloat16)


def fetch_pages(place, codes, arrays):
    out = jax.ShapeDtypeStruct((PAGES * PAGE, 2 * HD), jnp.bfloat16)
    return pl.pallas_call(
        page_kernel,
        in_specs=[pl.BlockSpec(memory_space=pltpu.SMEM)] * 2
        + [pl.BlockSpec(memory_space=pl.ANY)] * len(arrays),
        out_shape=(out, out),
        scratch_shapes=[
            pltpu.VMEM((2 * PAGES * PAGE, 2 * HD), jnp.float32),
            pltpu.SemaphoreType.DMA((len(arrays),)),
        ]
        + [pltpu.VMEM(array.shape, array.dtype) for array in arrays],
        compiler_params=params(),
        name="pages",
    )(place, codes, *arrays)


def moves(step):
    pairs = []
    for y in range(4):
        for z in range(4):
            for core in range(2):
                to_y, to_z, to_core = step(y, z, core)
                pairs.append(((y * 4 + z) * 2 + core, (to_y * 4 + to_z) * 2 + to_core))
    return pairs


def along_y(value, count):
    return lax.ppermute(value, "seq", moves(lambda y, z, c: ((y + count) % 4, z, c)))


def along_z(value, count):
    return lax.ppermute(value, "seq", moves(lambda y, z, c: (y, (z + count) % 4, c)))


def other_core(value):
    return lax.ppermute(value, "seq", moves(lambda y, z, c: (y, z, 1 - c)))


def page_codes(targets, me):
    index = jnp.arange(PAGES, dtype=jnp.int32)
    codes = []
    for owner in (me, me ^ 1):
        slot = targets - owner * PAGES
        match = (slot >= 0) & (slot < PAGES)
        before = match[:, None, :] & (index[None, :] < index[:, None])
        rank = jnp.sum(before.astype(jnp.int32), axis=2)
        code = index * 64 + slot + 1
        for entry in range(MOST):
            codes.append(jnp.sum(jnp.where(match & (rank == entry), code, 0), axis=1) - 1)
    return jnp.stack(codes, axis=1).reshape(-1)


def held_here(targets, me):
    mine = me * PAGES + jnp.arange(PAGES, dtype=jnp.int32)
    same_core = (jnp.arange(SEQ, dtype=jnp.int32) % 2 == me % 2)[:, None]
    match = (targets[None] == mine[:, None, None]) & same_core[None]
    return jnp.any(match, axis=(1, 2))


def project(normed, weight):
    return jnp.dot(normed, weight, preferred_element_type=jnp.float32).astype(jnp.bfloat16)


def attention_and_pages(me, codes, keep, normed, weight):
    core, z, y = me % 2, (me // 2) % 4, me // 8
    kv = project(normed, weight[:, GROUP * HD :])
    normed, kv = lax.optimization_barrier((normed, kv))
    by_z = {0: kv, 1: along_z(kv, 1), 3: along_z(kv, 3)}
    none = {count: along_y(kv, count) for count in (1, 3, 2)}
    own_queries = project(normed, weight[:, : GROUP * HD])
    pair_queries = other_core(own_queries)

    def flag(*conditions):
        return jnp.stack([jnp.asarray(value, jnp.int32) for value in conditions])

    state, queries = attend_first(core, own_queries, pair_queries, kv)
    state, by_z[1], by_z[3] = lax.optimization_barrier((state, by_z[1], by_z[3]))
    kv, odd = lax.optimization_barrier((kv, jnp.concatenate([by_z[1], by_z[3]], axis=0)))
    by_z[2] = along_z(kv, 2)
    odd = {count: along_y(odd, count) for count in (1, 3, 2)}
    state = attend_more(
        flag(y >= 1, y >= 3, y >= 2), queries, state, [none[1], none[3], none[2]]
    )
    state, by_z[2] = lax.optimization_barrier((state, by_z[2]))
    two = {count: along_y(by_z[2], count) for count in (1, 3, 2)}
    state = attend_more(
        flag(z >= 1, z >= 3, z >= 2), queries, state, [by_z[1], by_z[3], by_z[2]]
    )
    state, odd[1], odd[3], odd[2] = lax.optimization_barrier((state, odd[1], odd[3], odd[2]))
    state = attend_more(flag(y >= 1, y >= 3, y >= 2), queries, state, [odd[1], odd[3], odd[2]])
    state, two[1], two[3], two[2] = lax.optimization_barrier((state, two[1], two[3], two[2]))
    own, sent = attend_more(
        flag(y >= 1, y >= 3, y >= 2), queries, state, [two[1], two[3], two[2]], split=True
    )
    got = other_core(sent)

    arrays = [by_z[count] for count in range(4)]
    arrays += [group[count] for group in (none, odd, two) for count in (1, 2, 3)]
    place = jnp.stack([y, z, core])
    own_pages, sent_pages = fetch_pages(place, codes, arrays)
    got_pages = other_core(sent_pages)
    attention = finish(own, got)
    keep = keep.reshape(PAGES, 1, 1, 1)
    shape = (PAGES, PAGE, 2, HD)
    kv_cache = jnp.where(keep, own_pages.reshape(shape), got_pages.reshape(shape))
    return attention, kv_cache


def on_device(
    features,
    conv_weight,
    conv_bias,
    embed_weight,
    position_table,
    norm_gain,
    qkv_weight,
    page_owner,
    page_slot,
):
    me = lax.axis_index("seq").astype(jnp.int32)
    tensor = lax.axis_index("tensor").astype(jnp.int32)
    tensor_count = lax.axis_size("tensor")
    weight = lax.all_gather(qkv_weight, "seq", axis=0, tiled=True)
    parts = partial_latents(features, conv_weight)
    own = parts[: FRAMES * EXT].reshape(FRAMES, EXT * LAT)
    target = (page_owner * PAGES + page_slot).astype(jnp.float32)
    target = jnp.broadcast_to(target, (FRAMES, PAGES))
    message = jnp.concatenate([own, target], axis=1)
    message = jnp.pad(message, ((0, 0), (0, 512 - message.shape[1])))
    message = jnp.broadcast_to(message[:, None], (FRAMES, SEQ // FRAMES, 512)).reshape(SEQ, 512)
    message = lax.all_to_all(message, "seq", split_axis=0, concat_axis=0, tiled=True)
    gain = norm_gain.reshape(1, -1)
    message, gain = lax.optimization_barrier((message, gain))
    targets = message[:, EXT * LAT : EXT * LAT + PAGES].astype(jnp.int32)
    offset = tensor - me % (SEQ // FRAMES)
    latent = place_latents(message[:, : EXT * LAT].reshape(SEQ * EXT, LAT), offset)
    for bit in (1, 2, 4):
        swap = [(i, i ^ bit) for i in range(tensor_count)]
        latent = latent + lax.ppermute(latent, "tensor", swap)
    latent = latent + conv_bias[:, None]
    normed = normed_hidden(latent, embed_weight, position_table, gain)
    codes, keep = page_codes(targets, me), held_here(targets, me)
    normed, codes, keep = lax.optimization_barrier((normed, codes, keep))
    return attention_and_pages(me, codes, keep, normed, weight)


def solution(mesh):
    placed = (
        P(None, "tensor", "seq", None),
        P(),
        P(),
        P(),
        P("seq", None),
        P(),
        P("seq", "tensor"),
        P("seq"),
        P("seq"),
    )
    return jax.shard_map(
        on_device,
        mesh=mesh,
        in_specs=placed,
        out_specs=(P("seq", "tensor"), P("seq", None, None, "tensor")),
        check_vma=False,
    )
```

```python
import functools

import jax
import jax.numpy as jnp
import numpy as np
from jax import lax
from jax.experimental import pallas as pl
from jax.experimental.pallas import tpu as pltpu
from jax.sharding import PartitionSpec as P

HD = 128
PAGE = 8
GROUP = 4
LAT = 16
BLK = 320
PAGES = 40
MOST = 3
SEQ = 32
ROWS = 5
COLS = 2
FRAMES = 4
EXT = (ROWS + 2) * (COLS + 2)
TOK = 384
TILE = 256
QROWS = GROUP * BLK
STATE = HD + 8
VMEM = 24 * 1024 * 1024


def params(**extra):
    return pltpu.CompilerParams(vmem_limit_bytes=VMEM, **extra)


def cost(blocks):
    scores = blocks * 2 * QROWS * BLK
    return pl.CostEstimate(flops=4 * HD * scores, bytes_accessed=3 << 20, transcendentals=scores)


def roll_lanes(value, shift):
    shift = shift % value.shape[1]
    return pltpu.roll(value, shift, 1) if shift else value


def conv_kernel(feat_ref, weight_ref, out_ref, grid_ref):
    grid_ref[...] = jnp.zeros_like(grid_ref)
    for frame in range(FRAMES):
        for row in range(ROWS):
            start = frame * EXT + (row + 1) * (COLS + 2) + 1
            value = feat_ref[frame, row].astype(jnp.float32)
            grid_ref[start : start + COLS, :] = value / (1.0 + jnp.exp(-value))
    active = grid_ref[...].astype(jnp.bfloat16)
    product = lax.dot_general(
        weight_ref[...], active, (((1,), (1,)), ((), ())), preferred_element_type=jnp.float32
    )
    lane = lax.broadcasted_iota(jnp.int32, (LAT, 128), 1)
    total = jnp.zeros((LAT, 128), jnp.float32)
    for time in range(3):
        part = jnp.zeros((LAT, 128), jnp.float32)
        for row in range(3):
            for col in range(3):
                index = (time * 3 + row) * 3 + col
                piece = product[index * LAT : (index + 1) * LAT, :]
                part = part + roll_lanes(piece, -((row - 1) * (COLS + 2) + col - 1))
        delay = (2 - time) * EXT
        if delay:
            part = jnp.where(lane >= delay, roll_lanes(part, delay), 0.0)
        total = total + part
    padded = jnp.concatenate([total, jnp.zeros((128 - LAT, 128), jnp.float32)], axis=0)
    out_ref[...] = jnp.transpose(padded)[:, :LAT]


def partial_latents(features, conv_weight):
    weight = jnp.transpose(conv_weight, (0, 1, 2, 4, 3)).reshape(-1, conv_weight.shape[3])
    return pl.pallas_call(
        conv_kernel,
        out_shape=jax.ShapeDtypeStruct((128, LAT), jnp.float32),
        scratch_shapes=[pltpu.VMEM((128, features.shape[-1]), jnp.float32)],
        compiler_params=params(),
        name="conv",
    )(features, weight)


def split_three(value):
    high = value.astype(jnp.bfloat16)
    rest = value - high.astype(jnp.float32)
    middle = rest.astype(jnp.bfloat16)
    low = (rest - middle.astype(jnp.float32)).astype(jnp.bfloat16)
    return high, middle, low


def place_kernel(offset_ref, parts_ref, token_ref, out_ref):
    count = parts_ref.shape[0]
    token = lax.broadcasted_iota(jnp.int32, (TOK, count), 0) - offset_ref[0] * BLK
    pick = jnp.where(token == token_ref[...], 1.0, 0.0).astype(jnp.bfloat16)
    total = jnp.zeros((LAT, TOK), jnp.float32)
    for part in reversed(split_three(parts_ref[...])):
        total = total + lax.dot_general(
            part, pick, (((0,), (1,)), ((), ())), preferred_element_type=jnp.float32
        )
    out_ref[...] = total


def place_table():
    row = np.arange(ROWS + 2).reshape(1, -1, 1) - 1
    col = np.arange(COLS + 2).reshape(1, 1, -1) - 1
    width = np.arange(SEQ).reshape(-1, 1, 1) * COLS + col
    inside = (width >= 0) & (width < SEQ * COLS)
    token = np.where(inside, row * SEQ * COLS + width, -(1 << 20))
    return token.astype(np.int32).reshape(1, SEQ * EXT)


def place_latents(parts, offset):
    return pl.pallas_call(
        place_kernel,
        in_specs=[pl.BlockSpec(memory_space=pltpu.SMEM)]
        + [pl.BlockSpec(memory_space=pltpu.VMEM)] * 2,
        out_shape=jax.ShapeDtypeStruct((LAT, TOK), jnp.float32),
        compiler_params=params(),
        name="place",
    )(offset.reshape(1), parts, jnp.asarray(place_table()))


def hidden_kernel(latent_ref, embed_ref, table_ref, gain_ref, out_ref, hid_ref, sq_ref):
    step = pl.program_id(0)
    width = table_ref.shape[1]
    latent = latent_ref[...][:, :BLK]
    latent = jnp.concatenate(split_three(latent), axis=0)
    embed = embed_ref[...]
    hidden = lax.dot_general(
        latent,
        jnp.concatenate([embed, embed, embed], axis=0),
        (((0,), (0,)), ((), ())),
        preferred_element_type=jnp.float32,
    ) + table_ref[...].astype(jnp.float32)
    hid_ref[step] = hidden
    squares = jnp.zeros((BLK, 128), jnp.float32)
    for lane in range(0, width, 128):
        piece = hidden[:, lane : lane + 128]
        squares = squares + piece * piece

    @pl.when(step == 0)
    def _():
        sq_ref[...] = squares

    @pl.when(step > 0)
    def _():
        sq_ref[...] += squares

    @pl.when(step == pl.num_programs(0) - 1)
    def _():
        count = hid_ref.shape[0]
        mean = jnp.sum(sq_ref[...], axis=1, keepdims=True) / (count * width)
        factor = lax.rsqrt(mean + 1e-05)
        for tile in range(count):
            gain = gain_ref[:, tile * width : (tile + 1) * width].astype(jnp.float32)
            normed = hid_ref[tile] * factor * gain
            out_ref[:, tile * width : (tile + 1) * width] = normed.astype(jnp.bfloat16)


def normed_hidden(latent, embed_weight, position_table, gain):
    depth = position_table.shape[1]
    steps = 8
    width = depth // steps
    return pl.pallas_call(
        hidden_kernel,
        grid=(steps,),
        in_specs=[
            pl.BlockSpec((LAT, TOK), lambda i: (0, 0)),
            pl.BlockSpec((LAT, width), lambda i: (0, i)),
            pl.BlockSpec((BLK, width), lambda i: (0, i)),
            pl.BlockSpec((1, depth), lambda i: (0, 0)),
        ],
        out_specs=pl.BlockSpec((BLK, depth), lambda i: (0, 0)),
        out_shape=jax.ShapeDtypeStruct((BLK, depth), jnp.bfloat16),
        scratch_shapes=[
            pltpu.VMEM((steps, BLK, width), jnp.float32),
            pltpu.VMEM((BLK, 128), jnp.float32),
        ],
        compiler_params=params(dimension_semantics=("arbitrary",)),
        name="hidden",
    )(latent, embed_weight, position_table, gain)


def attend_block(masked, partner_full, keys, values, q_ref, state_ref):
    scale = 1.4426950408889634 / HD**0.5
    tiles = 2 * QROWS // TILE

    def score(tile):
        return lax.dot_general(
            keys,
            q_ref[tile * TILE : (tile + 1) * TILE, :],
            (((1,), (1,)), ((), ())),
            preferred_element_type=jnp.float32,
        )

    upcoming = score(0)
    for tile in range(tiles):
        scores = upcoming
        if tile + 1 < tiles:
            upcoming = score(tile + 1)
        cut = slice(tile * TILE, (tile + 1) * TILE)
        allowed = None
        if masked:
            key = lax.broadcasted_iota(jnp.int32, scores.shape, 0)
            query = tile * TILE + lax.broadcasted_iota(jnp.int32, (1, TILE), 1)
            if tile * TILE >= QROWS:
                query = jnp.where(partner_full, BLK, -1) + 0 * query
            else:
                for head in range(GROUP - 1, 0, -1):
                    query = jnp.where(query >= head * BLK, query - head * BLK, query)
            allowed = key <= query
            scores = jnp.where(allowed, scores, -1e30)
        peak = jnp.max(scores, axis=0, keepdims=True)
        if masked:
            best = peak
        else:
            old = state_ref[HD : HD + 1, cut]
            best = jnp.maximum(old, peak)
            factor = jnp.exp2((old - best) * scale)
        weights = jnp.exp2((scores - best) * scale)
        if masked:
            weights = jnp.where(allowed, weights, 0.0)
        total = jnp.sum(weights, axis=0, keepdims=True)
        summed = lax.dot_general(
            values,
            weights.astype(jnp.bfloat16),
            (((0,), (0,)), ((), ())),
            preferred_element_type=jnp.float32,
        )
        if not masked:
            total = total + state_ref[HD + 1 : HD + 2, cut] * factor
            summed = summed + state_ref[:HD, cut] * factor
        state_ref[HD : HD + 1, cut] = best
        state_ref[HD + 1 : HD + 2, cut] = total
        state_ref[:HD, cut] = summed


def first_kernel(core_ref, own_ref, pair_ref, kv_ref, state_ref, q_ref):
    for index, ref in enumerate((own_ref, pair_ref)):
        for head in range(GROUP):
            start = (index * GROUP + head) * BLK
            q_ref[start : start + BLK, :] = ref[:, head * HD : (head + 1) * HD]
    state_ref[HD + 2 :, :] = jnp.zeros((STATE - HD - 2, 2 * QROWS), jnp.float32)
    attend_block(True, core_ref[0] == 0, kv_ref[:, :HD], kv_ref[:, HD:], q_ref, state_ref)


def attend_first(core, own, pair, kv):
    return pl.pallas_call(
        first_kernel,
        in_specs=[pl.BlockSpec(memory_space=pltpu.SMEM)]
        + [pl.BlockSpec(memory_space=pltpu.VMEM)] * 3,
        out_shape=(
            jax.ShapeDtypeStruct((STATE, 2 * QROWS), jnp.float32),
            jax.ShapeDtypeStruct((2 * QROWS, HD), jnp.bfloat16),
        ),
        compiler_params=params(),
        cost_estimate=cost(1),
        name="first",
    )(core.reshape(1), own, pair, kv)


def more_kernel(count, split, flag_ref, q_ref, state_ref, *rest):
    arrays, rest = rest[:count], rest[count:]
    if split:
        own_out_ref, pair_out_ref, held_ref, sems, work_ref = rest
    else:
        work_ref, held_ref, sems = rest
    copies = []
    for index, array in enumerate(arrays):
        unit = array.shape[0]
        held = held_ref.at[pl.ds(index * unit, unit), :]
        copies.append(pltpu.make_async_copy(array, held, sems.at[index]))
        copies[-1].start()
    work_ref[...] = state_ref[...]
    for copy in copies:
        copy.wait()

    every = jnp.int32(unit == BLK)
    for index in range(count):
        every = every * flag_ref[index]

    if unit == BLK:

        @pl.when(every != 0)
        def _():
            attend_block(False, None, held_ref[:, :HD], held_ref[:, HD:], q_ref, work_ref)

    def body(index, carry):
        @pl.when(flag_ref[index] != 0)
        def _():
            rows = pl.ds(pl.multiple_of(index * unit, unit), unit)
            attend_block(False, None, held_ref[rows, :HD], held_ref[rows, HD:], q_ref, work_ref)

        return carry

    @pl.when(every == 0)
    def _():
        lax.fori_loop(0, count, body, 0)

    if split:
        own_out_ref[...] = work_ref[:, :QROWS]
        pair_out_ref[...] = work_ref[:, QROWS:]


def attend_more(flags, queries, state, arrays, split=False):
    unit, count = arrays[0].shape[0], len(arrays)
    half = jax.ShapeDtypeStruct((STATE, QROWS), jnp.float32)
    whole = jax.ShapeDtypeStruct((STATE, 2 * QROWS), jnp.float32)
    scratch = [
        pltpu.VMEM((count * unit, 2 * HD), jnp.bfloat16),
        pltpu.SemaphoreType.DMA((count,)),
    ]
    if split:
        scratch.append(pltpu.VMEM((STATE, 2 * QROWS), jnp.float32))
    return pl.pallas_call(
        functools.partial(more_kernel, count, split),
        in_specs=[pl.BlockSpec(memory_space=pltpu.SMEM)]
        + [pl.BlockSpec(memory_space=pltpu.VMEM)] * 2
        + [pl.BlockSpec(memory_space=pl.ANY)] * count,
        out_shape=(half, half) if split else whole,
        scratch_shapes=scratch,
        compiler_params=params(),
        cost_estimate=cost(count * unit // BLK),
        name="more",
    )(flags, queries, state, *arrays)


def finish_kernel(own_ref, got_ref, out_ref, row_ref):
    scale = 1.4426950408889634 / HD**0.5
    for start in range(0, QROWS, TILE):
        cut = slice(start, start + TILE)
        first, second = own_ref[HD : HD + 1, cut], got_ref[HD : HD + 1, cut]
        best = jnp.maximum(first, second)
        first = jnp.exp2((first - best) * scale)
        second = jnp.exp2((second - best) * scale)
        total = own_ref[HD + 1 : HD + 2, cut] * first + got_ref[HD + 1 : HD + 2, cut] * second
        summed = own_ref[:HD, cut] * first + got_ref[:HD, cut] * second
        row_ref[cut, :] = jnp.transpose(summed / total)
    for head in range(GROUP):
        rows = row_ref[head * BLK : (head + 1) * BLK, :]
        out_ref[:, head * HD : (head + 1) * HD] = rows.astype(jnp.bfloat16)


def finish(own, got):
    return pl.pallas_call(
        finish_kernel,
        out_shape=jax.ShapeDtypeStruct((BLK, GROUP * HD), jnp.bfloat16),
        scratch_shapes=[pltpu.VMEM((QROWS, HD), jnp.float32)],
        compiler_params=params(),
        name="finish",
    )(own, got)


def page_kernel(place_ref, code_ref, *rest):
    arrays, (own_ref, pair_ref, pool_ref, held_ref, sems) = rest[:-5], rest[-5:]
    copies = []
    for by_y in range(4):
        for by_z in range(4):
            block = by_y * 4 + by_z
            index, base = by_z, 0
            if by_y > 0:
                index, base = 3 + by_y + (0, 3, 6, 3)[by_z], by_z // 3 * BLK
            copies.append(
                pltpu.make_async_copy(
                    arrays[index].at[pl.ds(base, BLK), :],
                    pool_ref.at[pl.ds(block * BLK, BLK), :],
                    sems.at[block],
                )
            )
            copies[-1].start()
    held_ref[...] = jnp.zeros_like(held_ref)
    y, z, core = place_ref[0], place_ref[1], place_ref[2]
    for copy in copies:
        copy.wait()

    def body(step, carry):
        block, owner = step >> 1, step & 1
        source = (((y - (block >> 2)) & 3) * 4 + ((z - block) & 3)) * 2 + core

        def entry(number):
            code = code_ref[(source * 2 + owner) * MOST + number]

            @pl.when(code >= 0)
            def _():
                page = code >> 6
                slot = (code & 63) + owner * PAGES
                row = pl.multiple_of(block * BLK + (page >> 1) * 2 * PAGE, 2 * PAGE)
                rows = pool_ref[pl.ds(row, 2 * PAGE), :].astype(jnp.float32)
                rows = jnp.where((page & 1) == 1, rows[PAGE:], rows[:PAGE])
                held_ref[pl.ds(pl.multiple_of(slot * PAGE, PAGE), PAGE), :] = rows
                if number + 1 < MOST:
                    entry(number + 1)

        entry(0)
        return carry

    lax.fori_loop(0, 2 * 16, body, 0)
    own_ref[...] = held_ref[: PAGES * PAGE].astype(jnp.bfloat16)
    pair_ref[...] = held_ref[PAGES * PAGE :].astype(jnp.bfloat16)


def fetch_pages(place, codes, arrays):
    out = jax.ShapeDtypeStruct((PAGES * PAGE, 2 * HD), jnp.bfloat16)
    return pl.pallas_call(
        page_kernel,
        in_specs=[pl.BlockSpec(memory_space=pltpu.SMEM)] * 2
        + [pl.BlockSpec(memory_space=pl.ANY)] * len(arrays),
        out_shape=(out, out),
        scratch_shapes=[
            pltpu.VMEM((16 * BLK, 2 * HD), jnp.bfloat16),
            pltpu.VMEM((2 * PAGES * PAGE, 2 * HD), jnp.float32),
            pltpu.SemaphoreType.DMA((16,)),
        ],
        compiler_params=params(),
        name="pages",
    )(place, codes, *arrays)


def moves(step):
    pairs = []
    for y in range(4):
        for z in range(4):
            for core in range(2):
                to_y, to_z, to_core = step(y, z, core)
                pairs.append(((y * 4 + z) * 2 + core, (to_y * 4 + to_z) * 2 + to_core))
    return pairs


def along_y(value, count):
    return lax.ppermute(value, "seq", moves(lambda y, z, c: ((y + count) % 4, z, c)))


def along_z(value, count):
    return lax.ppermute(value, "seq", moves(lambda y, z, c: (y, (z + count) % 4, c)))


def other_core(value):
    return lax.ppermute(value, "seq", moves(lambda y, z, c: (y, z, 1 - c)))


def page_codes(targets, me):
    index = jnp.arange(PAGES, dtype=jnp.int32)
    codes = []
    for owner in (me, me ^ 1):
        slot = targets - owner * PAGES
        match = (slot >= 0) & (slot < PAGES)
        before = match[:, None, :] & (index[None, :] < index[:, None])
        rank = jnp.sum(before.astype(jnp.int32), axis=2)
        code = index * 64 + slot + 1
        for entry in range(MOST):
            codes.append(jnp.sum(jnp.where(match & (rank == entry), code, 0), axis=1) - 1)
    return jnp.stack(codes, axis=1).reshape(-1)


def held_here(targets, me):
    mine = me * PAGES + jnp.arange(PAGES, dtype=jnp.int32)
    same_core = (jnp.arange(SEQ, dtype=jnp.int32) % 2 == me % 2)[:, None]
    match = (targets[None] == mine[:, None, None]) & same_core[None]
    return jnp.any(match, axis=(1, 2))


def project(normed, weight):
    return jnp.dot(normed, weight, preferred_element_type=jnp.float32).astype(jnp.bfloat16)


def attention_and_pages(me, codes, keep, normed, weight):
    core, z, y = me % 2, (me // 2) % 4, me // 8
    kv = project(normed, weight[:, GROUP * HD :])
    normed, kv = lax.optimization_barrier((normed, kv))
    by_z = {0: kv, 1: along_z(kv, 1), 3: along_z(kv, 3)}
    none = {count: along_y(kv, count) for count in (1, 3, 2)}
    own_queries = project(normed, weight[:, : GROUP * HD])
    pair_queries = other_core(own_queries)

    def flag(*conditions):
        return jnp.stack([jnp.asarray(value, jnp.int32) for value in conditions])

    state, queries = attend_first(core, own_queries, pair_queries, kv)
    state, by_z[1], by_z[3] = lax.optimization_barrier((state, by_z[1], by_z[3]))
    kv, odd = lax.optimization_barrier((kv, jnp.concatenate([by_z[1], by_z[3]], axis=0)))
    by_z[2] = along_z(kv, 2)
    odd = {count: along_y(odd, count) for count in (1, 3, 2)}
    state = attend_more(
        flag(y >= 1, y >= 3, y >= 2), queries, state, [none[1], none[3], none[2]]
    )
    state, by_z[2] = lax.optimization_barrier((state, by_z[2]))
    two = {count: along_y(by_z[2], count) for count in (1, 3, 2)}
    state = attend_more(
        flag(z >= 1, z >= 3, z >= 2), queries, state, [by_z[1], by_z[3], by_z[2]]
    )
    state, odd[1], odd[3], odd[2] = lax.optimization_barrier((state, odd[1], odd[3], odd[2]))
    state = attend_more(flag(y >= 1, y >= 3, y >= 2), queries, state, [odd[1], odd[3], odd[2]])
    state, two[1], two[3], two[2] = lax.optimization_barrier((state, two[1], two[3], two[2]))
    own, sent = attend_more(
        flag(y >= 1, y >= 3, y >= 2), queries, state, [two[1], two[3], two[2]], split=True
    )
    got = other_core(sent)

    arrays = [by_z[count] for count in range(4)]
    arrays += [group[count] for group in (none, odd, two) for count in (1, 2, 3)]
    place = jnp.stack([y, z, core])
    own_pages, sent_pages = fetch_pages(place, codes, arrays)
    got_pages = other_core(sent_pages)
    attention = finish(own, got)
    keep = keep.reshape(PAGES, 1, 1, 1)
    shape = (PAGES, PAGE, 2, HD)
    kv_cache = jnp.where(keep, own_pages.reshape(shape), got_pages.reshape(shape))
    return attention, kv_cache


def on_device(
    features,
    conv_weight,
    conv_bias,
    embed_weight,
    position_table,
    norm_gain,
    qkv_weight,
    page_owner,
    page_slot,
):
    me = lax.axis_index("seq").astype(jnp.int32)
    tensor = lax.axis_index("tensor").astype(jnp.int32)
    tensor_count = lax.axis_size("tensor")
    weight = lax.all_gather(qkv_weight, "seq", axis=0, tiled=True)
    parts = partial_latents(features, conv_weight)
    own = parts[: FRAMES * EXT].reshape(FRAMES, EXT * LAT)
    target = (page_owner * PAGES + page_slot).astype(jnp.float32)
    target = jnp.broadcast_to(target, (FRAMES, PAGES))
    message = jnp.concatenate([own, target], axis=1)
    message = jnp.pad(message, ((0, 0), (0, 512 - message.shape[1])))
    message = jnp.broadcast_to(message[:, None], (FRAMES, SEQ // FRAMES, 512)).reshape(SEQ, 512)
    message = lax.all_to_all(message, "seq", split_axis=0, concat_axis=0, tiled=True)
    gain = norm_gain.reshape(1, -1)
    message, gain = lax.optimization_barrier((message, gain))
    targets = message[:, EXT * LAT : EXT * LAT + PAGES].astype(jnp.int32)
    offset = tensor - me % (SEQ // FRAMES)
    latent = place_latents(message[:, : EXT * LAT].reshape(SEQ * EXT, LAT), offset)
    for bit in (1, 2, 4):
        swap = [(i, i ^ bit) for i in range(tensor_count)]
        latent = latent + lax.ppermute(latent, "tensor", swap)
    latent = latent + conv_bias[:, None]
    normed = normed_hidden(latent, embed_weight, position_table, gain)
    codes, keep = page_codes(targets, me), held_here(targets, me)
    normed, codes, keep = lax.optimization_barrier((normed, codes, keep))
    return attention_and_pages(me, codes, keep, normed, weight)


def solution(mesh):
    placed = (
        P(None, "tensor", "seq", None),
        P(),
        P(),
        P(),
        P("seq", None),
        P(),
        P("seq", "tensor"),
        P("seq"),
        P("seq"),
    )
    return jax.shard_map(
        on_device,
        mesh=mesh,
        in_specs=placed,
        out_specs=(P("seq", "tensor"), P("seq", None, None, "tensor")),
        check_vma=False,
    )
```

```python
import functools

import jax
import jax.numpy as jnp
import numpy as np
from jax import lax
from jax.experimental import pallas as pl
from jax.experimental.pallas import tpu as pltpu
from jax.sharding import PartitionSpec as P

HD = 128
PAGE = 8
GROUP = 4
LAT = 16
BLK = 320
PAGES = 40
MOST = 3
SEQ = 32
ROWS = 5
COLS = 2
FRAMES = 4
EXT = (ROWS + 2) * (COLS + 2)
TOK = 384
TILE = 256
QROWS = GROUP * BLK
STATE = HD + 8
VMEM = 24 * 1024 * 1024


def params(**extra):
    return pltpu.CompilerParams(vmem_limit_bytes=VMEM, **extra)


def cost(blocks):
    scores = blocks * 2 * QROWS * BLK
    return pl.CostEstimate(flops=4 * HD * scores, bytes_accessed=3 << 20, transcendentals=scores)


def roll_lanes(value, shift):
    shift = shift % value.shape[1]
    return pltpu.roll(value, shift, 1) if shift else value


def conv_kernel(feat_ref, weight_ref, out_ref, grid_ref):
    grid_ref[...] = jnp.zeros_like(grid_ref)
    for frame in range(FRAMES):
        for row in range(ROWS):
            start = frame * EXT + (row + 1) * (COLS + 2) + 1
            value = feat_ref[frame, row].astype(jnp.float32)
            grid_ref[start : start + COLS, :] = value / (1.0 + jnp.exp(-value))
    active = grid_ref[...].astype(jnp.bfloat16)
    product = lax.dot_general(
        weight_ref[...], active, (((1,), (1,)), ((), ())), preferred_element_type=jnp.float32
    )
    lane = lax.broadcasted_iota(jnp.int32, (LAT, 128), 1)
    total = jnp.zeros((LAT, 128), jnp.float32)
    for time in range(3):
        part = jnp.zeros((LAT, 128), jnp.float32)
        for row in range(3):
            for col in range(3):
                index = (time * 3 + row) * 3 + col
                piece = product[index * LAT : (index + 1) * LAT, :]
                part = part + roll_lanes(piece, -((row - 1) * (COLS + 2) + col - 1))
        delay = (2 - time) * EXT
        if delay:
            part = jnp.where(lane >= delay, roll_lanes(part, delay), 0.0)
        total = total + part
    padded = jnp.concatenate([total, jnp.zeros((128 - LAT, 128), jnp.float32)], axis=0)
    out_ref[...] = jnp.transpose(padded)[:, :LAT]


def partial_latents(features, conv_weight):
    weight = jnp.transpose(conv_weight, (0, 1, 2, 4, 3)).reshape(-1, conv_weight.shape[3])
    return pl.pallas_call(
        conv_kernel,
        out_shape=jax.ShapeDtypeStruct((128, LAT), jnp.float32),
        scratch_shapes=[pltpu.VMEM((128, features.shape[-1]), jnp.float32)],
        compiler_params=params(),
        name="conv",
    )(features, weight)


def split_three(value):
    high = value.astype(jnp.bfloat16)
    rest = value - high.astype(jnp.float32)
    middle = rest.astype(jnp.bfloat16)
    low = (rest - middle.astype(jnp.float32)).astype(jnp.bfloat16)
    return high, middle, low


def place_kernel(offset_ref, parts_ref, token_ref, out_ref):
    count = parts_ref.shape[0]
    token = lax.broadcasted_iota(jnp.int32, (TOK, count), 0) - offset_ref[0] * BLK
    pick = jnp.where(token == token_ref[...], 1.0, 0.0).astype(jnp.bfloat16)
    total = jnp.zeros((LAT, TOK), jnp.float32)
    for part in reversed(split_three(parts_ref[...])):
        total = total + lax.dot_general(
            part, pick, (((0,), (1,)), ((), ())), preferred_element_type=jnp.float32
        )
    out_ref[...] = total


def place_table():
    row = np.arange(ROWS + 2).reshape(1, -1, 1) - 1
    col = np.arange(COLS + 2).reshape(1, 1, -1) - 1
    width = np.arange(SEQ).reshape(-1, 1, 1) * COLS + col
    inside = (width >= 0) & (width < SEQ * COLS)
    token = np.where(inside, row * SEQ * COLS + width, -(1 << 20))
    return token.astype(np.int32).reshape(1, SEQ * EXT)


def place_latents(parts, offset):
    return pl.pallas_call(
        place_kernel,
        in_specs=[pl.BlockSpec(memory_space=pltpu.SMEM)]
        + [pl.BlockSpec(memory_space=pltpu.VMEM)] * 2,
        out_shape=jax.ShapeDtypeStruct((LAT, TOK), jnp.float32),
        compiler_params=params(),
        name="place",
    )(offset.reshape(1), parts, jnp.asarray(place_table()))


def hidden_kernel(latent_ref, embed_ref, table_ref, gain_ref, out_ref, hid_ref, sq_ref):
    step = pl.program_id(0)
    width = table_ref.shape[1]
    latent = latent_ref[...][:, :BLK]
    latent = jnp.concatenate(split_three(latent), axis=0)
    embed = embed_ref[...]
    hidden = lax.dot_general(
        latent,
        jnp.concatenate([embed, embed, embed], axis=0),
        (((0,), (0,)), ((), ())),
        preferred_element_type=jnp.float32,
    ) + table_ref[...].astype(jnp.float32)
    hid_ref[step] = hidden
    squares = jnp.zeros((BLK, 128), jnp.float32)
    for lane in range(0, width, 128):
        piece = hidden[:, lane : lane + 128]
        squares = squares + piece * piece

    @pl.when(step == 0)
    def _():
        sq_ref[...] = squares

    @pl.when(step > 0)
    def _():
        sq_ref[...] += squares

    @pl.when(step == pl.num_programs(0) - 1)
    def _():
        count = hid_ref.shape[0]
        mean = jnp.sum(sq_ref[...], axis=1, keepdims=True) / (count * width)
        factor = lax.rsqrt(mean + 1e-05)
        for tile in range(count):
            gain = gain_ref[:, tile * width : (tile + 1) * width].astype(jnp.float32)
            normed = hid_ref[tile] * factor * gain
            out_ref[:, tile * width : (tile + 1) * width] = normed.astype(jnp.bfloat16)


def normed_hidden(latent, embed_weight, position_table, gain):
    depth = position_table.shape[1]
    steps = 8
    width = depth // steps
    return pl.pallas_call(
        hidden_kernel,
        grid=(steps,),
        in_specs=[
            pl.BlockSpec((LAT, TOK), lambda i: (0, 0)),
            pl.BlockSpec((LAT, width), lambda i: (0, i)),
            pl.BlockSpec((BLK, width), lambda i: (0, i)),
            pl.BlockSpec((1, depth), lambda i: (0, 0)),
        ],
        out_specs=pl.BlockSpec((BLK, depth), lambda i: (0, 0)),
        out_shape=jax.ShapeDtypeStruct((BLK, depth), jnp.bfloat16),
        scratch_shapes=[
            pltpu.VMEM((steps, BLK, width), jnp.float32),
            pltpu.VMEM((BLK, 128), jnp.float32),
        ],
        compiler_params=params(dimension_semantics=("arbitrary",)),
        name="hidden",
    )(latent, embed_weight, position_table, gain)


def attend_block(masked, partner_full, keys, values, q_ref, state_ref):
    scale = 1.4426950408889634 / HD**0.5
    tiles = 2 * QROWS // TILE

    def score(tile):
        return lax.dot_general(
            keys,
            q_ref[tile * TILE : (tile + 1) * TILE, :],
            (((1,), (1,)), ((), ())),
            preferred_element_type=jnp.float32,
        )

    upcoming = score(0)
    for tile in range(tiles):
        scores = upcoming
        if tile + 1 < tiles:
            upcoming = score(tile + 1)
        cut = slice(tile * TILE, (tile + 1) * TILE)
        allowed = None
        if masked:
            key = lax.broadcasted_iota(jnp.int32, scores.shape, 0)
            query = tile * TILE + lax.broadcasted_iota(jnp.int32, (1, TILE), 1)
            if tile * TILE >= QROWS:
                query = jnp.where(partner_full, BLK, -1) + 0 * query
            else:
                for head in range(GROUP - 1, 0, -1):
                    query = jnp.where(query >= head * BLK, query - head * BLK, query)
            allowed = key <= query
            scores = jnp.where(allowed, scores, -1e30)
        peak = jnp.max(scores, axis=0, keepdims=True)
        if masked:
            best = peak
        else:
            old = state_ref[HD : HD + 1, cut]
            best = jnp.maximum(old, peak)
            factor = jnp.exp2((old - best) * scale)
        weights = jnp.exp2((scores - best) * scale)
        if masked:
            weights = jnp.where(allowed, weights, 0.0)
        total = jnp.sum(weights, axis=0, keepdims=True)
        summed = lax.dot_general(
            values,
            weights.astype(jnp.bfloat16),
            (((0,), (0,)), ((), ())),
            preferred_element_type=jnp.float32,
        )
        if not masked:
            total = total + state_ref[HD + 1 : HD + 2, cut] * factor
            summed = summed + state_ref[:HD, cut] * factor
        state_ref[HD : HD + 1, cut] = best
        state_ref[HD + 1 : HD + 2, cut] = total
        state_ref[:HD, cut] = summed


def attend_rolled(keys, values, q_ref, state_ref, score_ref):
    scale = 1.4426950408889634 / HD**0.5
    tiles = 2 * QROWS // TILE
    rows = keys.shape[0]

    def score(tile, slot):
        start = pl.multiple_of(jnp.minimum(tile, tiles - 1) * TILE, TILE)
        score_ref[slot, :rows, :] = lax.dot_general(
            keys,
            q_ref[pl.ds(start, TILE), :],
            (((1,), (1,)), ((), ())),
            preferred_element_type=jnp.float32,
        )

    def update(tile, slot):
        cut = pl.ds(pl.multiple_of(tile * TILE, TILE), TILE)
        scores = score_ref[slot, :rows, :]
        old = state_ref[HD : HD + 1, cut]
        best = jnp.maximum(old, jnp.max(scores, axis=0, keepdims=True))
        factor = jnp.exp2((old - best) * scale)
        weights = jnp.exp2((scores - best) * scale)
        total = jnp.sum(weights, axis=0, keepdims=True)
        summed = lax.dot_general(
            values,
            weights.astype(jnp.bfloat16),
            (((0,), (0,)), ((), ())),
            preferred_element_type=jnp.float32,
        )
        state_ref[HD : HD + 1, cut] = best
        state_ref[HD + 1 : HD + 2, cut] = total + state_ref[HD + 1 : HD + 2, cut] * factor
        state_ref[:HD, cut] = summed + state_ref[:HD, cut] * factor

    score(0, 0)

    def body(pair, carry):
        score(2 * pair + 1, 1)
        update(2 * pair, 0)
        score(2 * pair + 2, 0)
        update(2 * pair + 1, 1)
        return carry

    lax.fori_loop(0, tiles // 2, body, 0)


def first_kernel(core_ref, own_ref, pair_ref, kv_ref, state_ref, q_ref):
    for index, ref in enumerate((own_ref, pair_ref)):
        for head in range(GROUP):
            start = (index * GROUP + head) * BLK
            q_ref[start : start + BLK, :] = ref[:, head * HD : (head + 1) * HD]
    state_ref[HD + 2 :, :] = jnp.zeros((STATE - HD - 2, 2 * QROWS), jnp.float32)
    attend_block(True, core_ref[0] == 0, kv_ref[:, :HD], kv_ref[:, HD:], q_ref, state_ref)


def attend_first(core, own, pair, kv):
    return pl.pallas_call(
        first_kernel,
        in_specs=[pl.BlockSpec(memory_space=pltpu.SMEM)]
        + [pl.BlockSpec(memory_space=pltpu.VMEM)] * 3,
        out_shape=(
            jax.ShapeDtypeStruct((STATE, 2 * QROWS), jnp.float32),
            jax.ShapeDtypeStruct((2 * QROWS, HD), jnp.bfloat16),
        ),
        compiler_params=params(),
        cost_estimate=cost(1),
        name="first",
    )(core.reshape(1), own, pair, kv)


def more_kernel(count, split, flag_ref, q_ref, state_ref, *rest):
    arrays, rest = rest[:count], rest[count:]
    if split:
        own_out_ref, pair_out_ref, held_ref, sems, score_ref, work_ref = rest
    else:
        work_ref, held_ref, sems, score_ref = rest
    copies = []
    for index, array in enumerate(arrays):
        unit = array.shape[0]
        held = held_ref.at[pl.ds(index * unit, unit), :]
        copies.append(pltpu.make_async_copy(array, held, sems.at[index]))
        copies[-1].start()
    work_ref[...] = state_ref[...]
    for copy in copies:
        copy.wait()

    every = jnp.int32(unit == BLK)
    for index in range(count):
        every = every * flag_ref[index]

    if unit == BLK:

        @pl.when(every != 0)
        def _():
            attend_rolled(held_ref[:, :HD], held_ref[:, HD:], q_ref, work_ref, score_ref)

    def body(index, carry):
        @pl.when(flag_ref[index] != 0)
        def _():
            rows = pl.ds(pl.multiple_of(index * unit, unit), unit)
            attend_block(False, None, held_ref[rows, :HD], held_ref[rows, HD:], q_ref, work_ref)

        return carry

    @pl.when(every == 0)
    def _():
        lax.fori_loop(0, count, body, 0)

    if split:
        own_out_ref[...] = work_ref[:, :QROWS]
        pair_out_ref[...] = work_ref[:, QROWS:]


def attend_more(flags, queries, state, arrays, split=False):
    unit, count = arrays[0].shape[0], len(arrays)
    half = jax.ShapeDtypeStruct((STATE, QROWS), jnp.float32)
    whole = jax.ShapeDtypeStruct((STATE, 2 * QROWS), jnp.float32)
    scratch = [
        pltpu.VMEM((count * unit, 2 * HD), jnp.bfloat16),
        pltpu.SemaphoreType.DMA((count,)),
        pltpu.VMEM((2, 3 * BLK if unit == BLK else 8, TILE), jnp.float32),
    ]
    if split:
        scratch.append(pltpu.VMEM((STATE, 2 * QROWS), jnp.float32))
    return pl.pallas_call(
        functools.partial(more_kernel, count, split),
        in_specs=[pl.BlockSpec(memory_space=pltpu.SMEM)]
        + [pl.BlockSpec(memory_space=pltpu.VMEM)] * 2
        + [pl.BlockSpec(memory_space=pl.ANY)] * count,
        out_shape=(half, half) if split else whole,
        scratch_shapes=scratch,
        compiler_params=params(),
        cost_estimate=cost(count * unit // BLK),
        name="more",
    )(flags, queries, state, *arrays)


def finish_kernel(own_ref, got_ref, out_ref, row_ref):
    scale = 1.4426950408889634 / HD**0.5
    for start in range(0, QROWS, TILE):
        cut = slice(start, start + TILE)
        first, second = own_ref[HD : HD + 1, cut], got_ref[HD : HD + 1, cut]
        best = jnp.maximum(first, second)
        first = jnp.exp2((first - best) * scale)
        second = jnp.exp2((second - best) * scale)
        total = own_ref[HD + 1 : HD + 2, cut] * first + got_ref[HD + 1 : HD + 2, cut] * second
        summed = own_ref[:HD, cut] * first + got_ref[:HD, cut] * second
        row_ref[cut, :] = jnp.transpose(summed / total)
    for head in range(GROUP):
        rows = row_ref[head * BLK : (head + 1) * BLK, :]
        out_ref[:, head * HD : (head + 1) * HD] = rows.astype(jnp.bfloat16)


def finish(own, got):
    return pl.pallas_call(
        finish_kernel,
        out_shape=jax.ShapeDtypeStruct((BLK, GROUP * HD), jnp.bfloat16),
        scratch_shapes=[pltpu.VMEM((QROWS, HD), jnp.float32)],
        compiler_params=params(),
        name="finish",
    )(own, got)


def page_kernel(place_ref, code_ref, *rest):
    count = (len(rest) - 4) // 2
    remote, own_ref, pair_ref = rest[:count], rest[count], rest[count + 1]
    held_ref, sems, arrays = rest[count + 2], rest[count + 3], rest[count + 4 :]
    copies = [
        pltpu.make_async_copy(remote[index], arrays[index], sems.at[index])
        for index in range(count)
    ]
    for copy in copies:
        copy.start()
    held_ref[...] = jnp.zeros_like(held_ref)
    y, z, core = place_ref[0], place_ref[1], place_ref[2]
    waited = set()
    for by_y in range(4):
        for by_z in range(4):
            if by_y == 0:
                index, base = by_z, 0
            else:
                index, base = 3 + by_y + (0, 3, 6, 3)[by_z], by_z // 3 * BLK
            if index not in waited:
                copies[index].wait()
                waited.add(index)
            array = arrays[index]
            source = (((y - by_y) & 3) * 4 + ((z - by_z) & 3)) * 2 + core
            for entry in range(2 * MOST):
                code = code_ref[source * 2 * MOST + entry]

                @pl.when(code >= 0)
                def _():
                    page = code >> 6
                    slot = (code & 63) + entry // MOST * PAGES
                    row = pl.multiple_of(base + (page >> 1) * 2 * PAGE, 2 * PAGE)
                    rows = array[pl.ds(row, 2 * PAGE), :].astype(jnp.float32)
                    rows = jnp.where((page & 1) == 1, rows[PAGE:], rows[:PAGE])
                    held_ref[pl.ds(pl.multiple_of(slot * PAGE, PAGE), PAGE), :] = rows

    own_ref[...] = held_ref[: PAGES * PAGE].astype(jnp.bfloat16)
    pair_ref[...] = held_ref[PAGES * PAGE :].astype(jnp.bfloat16)


def fetch_pages(place, codes, arrays):
    out = jax.ShapeDtypeStruct((PAGES * PAGE, 2 * HD), jnp.bfloat16)
    return pl.pallas_call(
        page_kernel,
        in_specs=[pl.BlockSpec(memory_space=pltpu.SMEM)] * 2
        + [pl.BlockSpec(memory_space=pl.ANY)] * len(arrays),
        out_shape=(out, out),
        scratch_shapes=[
            pltpu.VMEM((2 * PAGES * PAGE, 2 * HD), jnp.float32),
            pltpu.SemaphoreType.DMA((len(arrays),)),
        ]
        + [pltpu.VMEM(array.shape, array.dtype) for array in arrays],
        compiler_params=params(),
        name="pages",
    )(place, codes, *arrays)


def moves(step):
    pairs = []
    for y in range(4):
        for z in range(4):
            for core in range(2):
                to_y, to_z, to_core = step(y, z, core)
                pairs.append(((y * 4 + z) * 2 + core, (to_y * 4 + to_z) * 2 + to_core))
    return pairs


def along_y(value, count):
    return lax.ppermute(value, "seq", moves(lambda y, z, c: ((y + count) % 4, z, c)))


def along_z(value, count):
    return lax.ppermute(value, "seq", moves(lambda y, z, c: (y, (z + count) % 4, c)))


def other_core(value):
    return lax.ppermute(value, "seq", moves(lambda y, z, c: (y, z, 1 - c)))


def page_codes(targets, me):
    index = jnp.arange(PAGES, dtype=jnp.int32)
    codes = []
    for owner in (me, me ^ 1):
        slot = targets - owner * PAGES
        match = (slot >= 0) & (slot < PAGES)
        before = match[:, None, :] & (index[None, :] < index[:, None])
        rank = jnp.sum(before.astype(jnp.int32), axis=2)
        code = index * 64 + slot + 1
        for entry in range(MOST):
            codes.append(jnp.sum(jnp.where(match & (rank == entry), code, 0), axis=1) - 1)
    return jnp.stack(codes, axis=1).reshape(-1)


def held_here(targets, me):
    mine = me * PAGES + jnp.arange(PAGES, dtype=jnp.int32)
    same_core = (jnp.arange(SEQ, dtype=jnp.int32) % 2 == me % 2)[:, None]
    match = (targets[None] == mine[:, None, None]) & same_core[None]
    return jnp.any(match, axis=(1, 2))


def project(normed, weight):
    return jnp.dot(normed, weight, preferred_element_type=jnp.float32).astype(jnp.bfloat16)


def attention_and_pages(me, codes, keep, normed, weight):
    core, z, y = me % 2, (me // 2) % 4, me // 8
    kv = project(normed, weight[:, GROUP * HD :])
    normed, kv = lax.optimization_barrier((normed, kv))
    by_z = {0: kv, 1: along_z(kv, 1), 3: along_z(kv, 3)}
    none = {count: along_y(kv, count) for count in (1, 3, 2)}
    own_queries = project(normed, weight[:, : GROUP * HD])
    pair_queries = other_core(own_queries)

    def flag(*conditions):
        return jnp.stack([jnp.asarray(value, jnp.int32) for value in conditions])

    state, queries = attend_first(core, own_queries, pair_queries, kv)
    state, by_z[1], by_z[3] = lax.optimization_barrier((state, by_z[1], by_z[3]))
    kv, odd = lax.optimization_barrier((kv, jnp.concatenate([by_z[1], by_z[3]], axis=0)))
    by_z[2] = along_z(kv, 2)
    odd = {count: along_y(odd, count) for count in (1, 3, 2)}
    state = attend_more(
        flag(y >= 1, y >= 3, y >= 2), queries, state, [none[1], none[3], none[2]]
    )
    state, by_z[2] = lax.optimization_barrier((state, by_z[2]))
    two = {count: along_y(by_z[2], count) for count in (1, 3, 2)}
    state = attend_more(
        flag(z >= 1, z >= 3, z >= 2), queries, state, [by_z[1], by_z[3], by_z[2]]
    )
    state, odd[1], odd[3], odd[2] = lax.optimization_barrier((state, odd[1], odd[3], odd[2]))
    state = attend_more(flag(y >= 1, y >= 3, y >= 2), queries, state, [odd[1], odd[3], odd[2]])
    state, two[1], two[3], two[2] = lax.optimization_barrier((state, two[1], two[3], two[2]))
    own, sent = attend_more(
        flag(y >= 1, y >= 3, y >= 2), queries, state, [two[1], two[3], two[2]], split=True
    )
    got = other_core(sent)

    arrays = [by_z[count] for count in range(4)]
    arrays += [group[count] for group in (none, odd, two) for count in (1, 2, 3)]
    place = jnp.stack([y, z, core])
    own_pages, sent_pages = fetch_pages(place, codes, arrays)
    got_pages = other_core(sent_pages)
    attention = finish(own, got)
    attention, got_pages = lax.optimization_barrier((attention, got_pages))
    keep = keep.reshape(PAGES, 1, 1, 1)
    shape = (PAGES, PAGE, 2, HD)
    kv_cache = jnp.where(keep, own_pages.reshape(shape), got_pages.reshape(shape))
    return attention, kv_cache


def on_device(
    features,
    conv_weight,
    conv_bias,
    embed_weight,
    position_table,
    norm_gain,
    qkv_weight,
    page_owner,
    page_slot,
):
    me = lax.axis_index("seq").astype(jnp.int32)
    tensor = lax.axis_index("tensor").astype(jnp.int32)
    tensor_count = lax.axis_size("tensor")
    weight = lax.all_gather(qkv_weight, "seq", axis=0, tiled=True)
    parts = partial_latents(features, conv_weight)
    own = parts[: FRAMES * EXT].reshape(FRAMES, EXT * LAT)
    target = (page_owner * PAGES + page_slot).astype(jnp.float32)
    target = jnp.broadcast_to(target, (FRAMES, PAGES))
    message = jnp.concatenate([own, target], axis=1)
    message = jnp.pad(message, ((0, 0), (0, 512 - message.shape[1])))
    message = jnp.broadcast_to(message[:, None], (FRAMES, SEQ // FRAMES, 512)).reshape(SEQ, 512)
    message = lax.all_to_all(message, "seq", split_axis=0, concat_axis=0, tiled=True)
    gain = norm_gain.reshape(1, -1)
    message, gain = lax.optimization_barrier((message, gain))
    targets = message[:, EXT * LAT : EXT * LAT + PAGES].astype(jnp.int32)
    offset = tensor - me % (SEQ // FRAMES)
    latent = place_latents(message[:, : EXT * LAT].reshape(SEQ * EXT, LAT), offset)
    for bit in (1, 2, 4):
        swap = [(i, i ^ bit) for i in range(tensor_count)]
        latent = latent + lax.ppermute(latent, "tensor", swap)
    latent = latent + conv_bias[:, None]
    normed = normed_hidden(latent, embed_weight, position_table, gain)
    codes, keep = page_codes(targets, me), held_here(targets, me)
    normed, codes, keep = lax.optimization_barrier((normed, codes, keep))
    return attention_and_pages(me, codes, keep, normed, weight)


def solution(mesh):
    placed = (
        P(None, "tensor", "seq", None),
        P(),
        P(),
        P(),
        P("seq", None),
        P(),
        P("seq", "tensor"),
        P("seq"),
        P("seq"),
    )
    return jax.shard_map(
        on_device,
        mesh=mesh,
        in_specs=placed,
        out_specs=(P("seq", "tensor"), P("seq", None, None, "tensor")),
        check_vma=False,
    )
```

```python
import functools

import jax
import jax.numpy as jnp
import numpy as np
from jax import lax
from jax.experimental import pallas as pl
from jax.experimental.pallas import tpu as pltpu
from jax.sharding import PartitionSpec as P

HD = 128
PAGE = 8
GROUP = 4
LAT = 16
BLK = 320
PAGES = 40
MOST = 3
SEQ = 32
ROWS = 5
COLS = 2
FRAMES = 4
EXT = (ROWS + 2) * (COLS + 2)
TOK = 384
TILE = 256
QROWS = GROUP * BLK
STATE = HD + 8
VMEM = 24 * 1024 * 1024


def params(**extra):
    return pltpu.CompilerParams(vmem_limit_bytes=VMEM, **extra)


def cost(blocks):
    scores = blocks * 2 * QROWS * BLK
    return pl.CostEstimate(flops=4 * HD * scores, bytes_accessed=3 << 20, transcendentals=scores)


def roll_lanes(value, shift):
    shift = shift % value.shape[1]
    return pltpu.roll(value, shift, 1) if shift else value


def conv_kernel(feat_ref, weight_ref, out_ref, grid_ref):
    grid_ref[...] = jnp.zeros_like(grid_ref)
    for frame in range(FRAMES):
        for row in range(ROWS):
            start = frame * EXT + (row + 1) * (COLS + 2) + 1
            value = feat_ref[frame, row].astype(jnp.float32)
            grid_ref[start : start + COLS, :] = value / (1.0 + jnp.exp(-value))
    active = grid_ref[...].astype(jnp.bfloat16)
    product = lax.dot_general(
        weight_ref[...], active, (((1,), (1,)), ((), ())), preferred_element_type=jnp.float32
    )
    lane = lax.broadcasted_iota(jnp.int32, (LAT, 128), 1)
    total = jnp.zeros((LAT, 128), jnp.float32)
    for time in range(3):
        part = jnp.zeros((LAT, 128), jnp.float32)
        for row in range(3):
            for col in range(3):
                index = (time * 3 + row) * 3 + col
                piece = product[index * LAT : (index + 1) * LAT, :]
                part = part + roll_lanes(piece, -((row - 1) * (COLS + 2) + col - 1))
        delay = (2 - time) * EXT
        if delay:
            part = jnp.where(lane >= delay, roll_lanes(part, delay), 0.0)
        total = total + part
    padded = jnp.concatenate([total, jnp.zeros((128 - LAT, 128), jnp.float32)], axis=0)
    out_ref[...] = jnp.transpose(padded)[:, :LAT]


def partial_latents(features, conv_weight):
    weight = jnp.transpose(conv_weight, (0, 1, 2, 4, 3)).reshape(-1, conv_weight.shape[3])
    return pl.pallas_call(
        conv_kernel,
        out_shape=jax.ShapeDtypeStruct((128, LAT), jnp.float32),
        scratch_shapes=[pltpu.VMEM((128, features.shape[-1]), jnp.float32)],
        compiler_params=params(),
        name="conv",
    )(features, weight)


def split_three(value):
    high = value.astype(jnp.bfloat16)
    rest = value - high.astype(jnp.float32)
    middle = rest.astype(jnp.bfloat16)
    low = (rest - middle.astype(jnp.float32)).astype(jnp.bfloat16)
    return high, middle, low


def place_kernel(offset_ref, parts_ref, token_ref, out_ref):
    count = parts_ref.shape[0]
    token = lax.broadcasted_iota(jnp.int32, (TOK, count), 0) - offset_ref[0] * BLK
    pick = jnp.where(token == token_ref[...], 1.0, 0.0).astype(jnp.bfloat16)
    total = jnp.zeros((LAT, TOK), jnp.float32)
    for part in reversed(split_three(parts_ref[...])):
        total = total + lax.dot_general(
            part, pick, (((0,), (1,)), ((), ())), preferred_element_type=jnp.float32
        )
    out_ref[...] = total


def place_table():
    row = np.arange(ROWS + 2).reshape(1, -1, 1) - 1
    col = np.arange(COLS + 2).reshape(1, 1, -1) - 1
    width = np.arange(SEQ).reshape(-1, 1, 1) * COLS + col
    inside = (width >= 0) & (width < SEQ * COLS)
    token = np.where(inside, row * SEQ * COLS + width, -(1 << 20))
    return token.astype(np.int32).reshape(1, SEQ * EXT)


def place_latents(parts, offset):
    return pl.pallas_call(
        place_kernel,
        in_specs=[pl.BlockSpec(memory_space=pltpu.SMEM)]
        + [pl.BlockSpec(memory_space=pltpu.VMEM)] * 2,
        out_shape=jax.ShapeDtypeStruct((LAT, TOK), jnp.float32),
        compiler_params=params(),
        name="place",
    )(offset.reshape(1), parts, jnp.asarray(place_table()))


def hidden_kernel(latent_ref, embed_ref, table_ref, gain_ref, out_ref, hid_ref, sq_ref):
    step = pl.program_id(0)
    width = table_ref.shape[1]
    latent = latent_ref[...][:, :BLK]
    latent = jnp.concatenate(split_three(latent), axis=0)
    embed = embed_ref[...]
    hidden = lax.dot_general(
        latent,
        jnp.concatenate([embed, embed, embed], axis=0),
        (((0,), (0,)), ((), ())),
        preferred_element_type=jnp.float32,
    ) + table_ref[...].astype(jnp.float32)
    hid_ref[step] = hidden
    squares = jnp.zeros((BLK, 128), jnp.float32)
    for lane in range(0, width, 128):
        piece = hidden[:, lane : lane + 128]
        squares = squares + piece * piece

    @pl.when(step == 0)
    def _():
        sq_ref[...] = squares

    @pl.when(step > 0)
    def _():
        sq_ref[...] += squares

    @pl.when(step == pl.num_programs(0) - 1)
    def _():
        count = hid_ref.shape[0]
        mean = jnp.sum(sq_ref[...], axis=1, keepdims=True) / (count * width)
        factor = lax.rsqrt(mean + 1e-05)
        for tile in range(count):
            gain = gain_ref[:, tile * width : (tile + 1) * width].astype(jnp.float32)
            normed = hid_ref[tile] * factor * gain
            out_ref[:, tile * width : (tile + 1) * width] = normed.astype(jnp.bfloat16)


def normed_hidden(latent, embed_weight, position_table, gain):
    depth = position_table.shape[1]
    steps = 8
    width = depth // steps
    return pl.pallas_call(
        hidden_kernel,
        grid=(steps,),
        in_specs=[
            pl.BlockSpec((LAT, TOK), lambda i: (0, 0)),
            pl.BlockSpec((LAT, width), lambda i: (0, i)),
            pl.BlockSpec((BLK, width), lambda i: (0, i)),
            pl.BlockSpec((1, depth), lambda i: (0, 0)),
        ],
        out_specs=pl.BlockSpec((BLK, depth), lambda i: (0, 0)),
        out_shape=jax.ShapeDtypeStruct((BLK, depth), jnp.bfloat16),
        scratch_shapes=[
            pltpu.VMEM((steps, BLK, width), jnp.float32),
            pltpu.VMEM((BLK, 128), jnp.float32),
        ],
        compiler_params=params(dimension_semantics=("arbitrary",)),
        name="hidden",
    )(latent, embed_weight, position_table, gain)


def attend_block(masked, partner_full, keys, values, q_ref, state_ref):
    scale = 1.4426950408889634 / HD**0.5
    tiles = 2 * QROWS // TILE

    def score(tile):
        return lax.dot_general(
            keys,
            q_ref[tile * TILE : (tile + 1) * TILE, :],
            (((1,), (1,)), ((), ())),
            preferred_element_type=jnp.float32,
        )

    upcoming = score(0)
    for tile in range(tiles):
        scores = upcoming
        if tile + 1 < tiles:
            upcoming = score(tile + 1)
        cut = slice(tile * TILE, (tile + 1) * TILE)
        allowed = None
        if masked:
            key = lax.broadcasted_iota(jnp.int32, scores.shape, 0)
            query = tile * TILE + lax.broadcasted_iota(jnp.int32, (1, TILE), 1)
            if tile * TILE >= QROWS:
                query = jnp.where(partner_full, BLK, -1) + 0 * query
            else:
                for head in range(GROUP - 1, 0, -1):
                    query = jnp.where(query >= head * BLK, query - head * BLK, query)
            allowed = key <= query
            scores = jnp.where(allowed, scores, -1e30)
        peak = jnp.max(scores, axis=0, keepdims=True)
        if masked:
            best = peak
        else:
            old = state_ref[HD : HD + 1, cut]
            best = jnp.maximum(old, peak)
            factor = jnp.exp2((old - best) * scale)
        weights = jnp.exp2((scores - best) * scale)
        if masked:
            weights = jnp.where(allowed, weights, 0.0)
        total = jnp.sum(weights, axis=0, keepdims=True)
        summed = lax.dot_general(
            values,
            weights.astype(jnp.bfloat16),
            (((0,), (0,)), ((), ())),
            preferred_element_type=jnp.float32,
        )
        if not masked:
            total = total + state_ref[HD + 1 : HD + 2, cut] * factor
            summed = summed + state_ref[:HD, cut] * factor
        state_ref[HD : HD + 1, cut] = best
        state_ref[HD + 1 : HD + 2, cut] = total
        state_ref[:HD, cut] = summed


def attend_rolled(keys, values, q_ref, state_ref, score_ref):
    scale = 1.4426950408889634 / HD**0.5
    tiles = 2 * QROWS // TILE
    rows = keys.shape[0]

    def score(tile, slot):
        start = pl.multiple_of(jnp.minimum(tile, tiles - 1) * TILE, TILE)
        score_ref[slot, :rows, :] = lax.dot_general(
            keys,
            q_ref[pl.ds(start, TILE), :],
            (((1,), (1,)), ((), ())),
            preferred_element_type=jnp.float32,
        )

    def update(tile, slot):
        cut = pl.ds(pl.multiple_of(tile * TILE, TILE), TILE)
        scores = score_ref[slot, :rows, :]
        old = state_ref[HD : HD + 1, cut]
        best = jnp.maximum(old, jnp.max(scores, axis=0, keepdims=True))
        factor = jnp.exp2((old - best) * scale)
        weights = jnp.exp2((scores - best) * scale)
        total = jnp.sum(weights, axis=0, keepdims=True)
        summed = lax.dot_general(
            values,
            weights.astype(jnp.bfloat16),
            (((0,), (0,)), ((), ())),
            preferred_element_type=jnp.float32,
        )
        state_ref[HD : HD + 1, cut] = best
        state_ref[HD + 1 : HD + 2, cut] = total + state_ref[HD + 1 : HD + 2, cut] * factor
        state_ref[:HD, cut] = summed + state_ref[:HD, cut] * factor

    score(0, 0)

    def body(pair, carry):
        score(2 * pair + 1, 1)
        update(2 * pair, 0)
        score(2 * pair + 2, 0)
        update(2 * pair + 1, 1)
        return carry

    lax.fori_loop(0, tiles // 2, body, 0)


def first_kernel(core_ref, own_ref, pair_ref, kv_ref, state_ref, q_ref):
    for index, ref in enumerate((own_ref, pair_ref)):
        for head in range(GROUP):
            start = (index * GROUP + head) * BLK
            q_ref[start : start + BLK, :] = ref[:, head * HD : (head + 1) * HD]
    state_ref[HD + 2 :, :] = jnp.zeros((STATE - HD - 2, 2 * QROWS), jnp.float32)
    attend_block(True, core_ref[0] == 0, kv_ref[:, :HD], kv_ref[:, HD:], q_ref, state_ref)


def attend_first(core, own, pair, kv):
    return pl.pallas_call(
        first_kernel,
        in_specs=[pl.BlockSpec(memory_space=pltpu.SMEM)]
        + [pl.BlockSpec(memory_space=pltpu.VMEM)] * 3,
        out_shape=(
            jax.ShapeDtypeStruct((STATE, 2 * QROWS), jnp.float32),
            jax.ShapeDtypeStruct((2 * QROWS, HD), jnp.bfloat16),
        ),
        compiler_params=params(),
        cost_estimate=cost(1),
        name="first",
    )(core.reshape(1), own, pair, kv)


def more_kernel(count, split, flag_ref, q_ref, state_ref, *rest):
    arrays, rest = rest[:count], rest[count:]
    if split:
        own_out_ref, pair_out_ref, held_ref, sems, score_ref, work_ref = rest
    else:
        work_ref, held_ref, sems, score_ref = rest
    copies = []
    for index, array in enumerate(arrays):
        unit = array.shape[0]
        held = held_ref.at[pl.ds(index * unit, unit), :]
        copies.append(pltpu.make_async_copy(array, held, sems.at[index]))
        copies[-1].start()
    work_ref[...] = state_ref[...]
    for copy in copies:
        copy.wait()

    every = jnp.int32(unit == BLK)
    for index in range(count):
        every = every * flag_ref[index]

    if unit == BLK:

        @pl.when(every != 0)
        def _():
            attend_rolled(held_ref[:, :HD], held_ref[:, HD:], q_ref, work_ref, score_ref)

    def body(index, carry):
        @pl.when(flag_ref[index] != 0)
        def _():
            rows = pl.ds(pl.multiple_of(index * unit, unit), unit)
            attend_block(False, None, held_ref[rows, :HD], held_ref[rows, HD:], q_ref, work_ref)

        return carry

    @pl.when(every == 0)
    def _():
        lax.fori_loop(0, count, body, 0)

    if split:
        own_out_ref[...] = work_ref[:, :QROWS]
        pair_out_ref[...] = work_ref[:, QROWS:]


def attend_more(flags, queries, state, arrays, split=False):
    unit, count = arrays[0].shape[0], len(arrays)
    half = jax.ShapeDtypeStruct((STATE, QROWS), jnp.float32)
    whole = jax.ShapeDtypeStruct((STATE, 2 * QROWS), jnp.float32)
    scratch = [
        pltpu.VMEM((count * unit, 2 * HD), jnp.bfloat16),
        pltpu.SemaphoreType.DMA((count,)),
        pltpu.VMEM((2, 3 * BLK if unit == BLK else 8, TILE), jnp.float32),
    ]
    if split:
        scratch.append(pltpu.VMEM((STATE, 2 * QROWS), jnp.float32))
    return pl.pallas_call(
        functools.partial(more_kernel, count, split),
        in_specs=[pl.BlockSpec(memory_space=pltpu.SMEM)]
        + [pl.BlockSpec(memory_space=pltpu.VMEM)] * 2
        + [pl.BlockSpec(memory_space=pl.ANY)] * count,
        out_shape=(half, half) if split else whole,
        scratch_shapes=scratch,
        compiler_params=params(),
        cost_estimate=cost(count * unit // BLK),
        name="more",
    )(flags, queries, state, *arrays)


def finish_kernel(own_ref, got_ref, out_ref, row_ref):
    scale = 1.4426950408889634 / HD**0.5
    for start in range(0, QROWS, TILE):
        cut = slice(start, start + TILE)
        first, second = own_ref[HD : HD + 1, cut], got_ref[HD : HD + 1, cut]
        best = jnp.maximum(first, second)
        first = jnp.exp2((first - best) * scale)
        second = jnp.exp2((second - best) * scale)
        total = own_ref[HD + 1 : HD + 2, cut] * first + got_ref[HD + 1 : HD + 2, cut] * second
        summed = own_ref[:HD, cut] * first + got_ref[:HD, cut] * second
        row_ref[cut, :] = jnp.transpose(summed / total)
    for head in range(GROUP):
        rows = row_ref[head * BLK : (head + 1) * BLK, :]
        out_ref[:, head * HD : (head + 1) * HD] = rows.astype(jnp.bfloat16)


def finish(own, got):
    return pl.pallas_call(
        finish_kernel,
        out_shape=jax.ShapeDtypeStruct((BLK, GROUP * HD), jnp.bfloat16),
        scratch_shapes=[pltpu.VMEM((QROWS, HD), jnp.float32)],
        compiler_params=params(),
        name="finish",
    )(own, got)


def page_kernel(place_ref, code_ref, *rest):
    count = (len(rest) - 4) // 2
    remote, own_ref, pair_ref = rest[:count], rest[count], rest[count + 1]
    held_ref, sems, arrays = rest[count + 2], rest[count + 3], rest[count + 4 :]
    copies = [
        pltpu.make_async_copy(remote[index], arrays[index], sems.at[index])
        for index in range(count)
    ]
    for copy in copies:
        copy.start()
    held_ref[...] = jnp.zeros_like(held_ref)
    y, z, core = place_ref[0], place_ref[1], place_ref[2]
    waited = set()
    for by_y in range(4):
        for by_z in range(4):
            if by_y == 0:
                index, base = by_z, 0
            else:
                index, base = 3 + by_y + (0, 3, 6, 3)[by_z], by_z // 3 * BLK
            if index not in waited:
                copies[index].wait()
                waited.add(index)
            array = arrays[index]
            source = (((y - by_y) & 3) * 4 + ((z - by_z) & 3)) * 2 + core
            for entry in range(2 * MOST):
                code = code_ref[source * 2 * MOST + entry]

                @pl.when(code >= 0)
                def _():
                    page = code >> 6
                    slot = (code & 63) + entry // MOST * PAGES
                    row = pl.multiple_of(base + (page >> 1) * 2 * PAGE, 2 * PAGE)
                    rows = array[pl.ds(row, 2 * PAGE), :].astype(jnp.float32)
                    rows = jnp.where((page & 1) == 1, rows[PAGE:], rows[:PAGE])
                    held_ref[pl.ds(pl.multiple_of(slot * PAGE, PAGE), PAGE), :] = rows

    own_ref[...] = held_ref[: PAGES * PAGE].astype(jnp.bfloat16)
    pair_ref[...] = held_ref[PAGES * PAGE :].astype(jnp.bfloat16)


def fetch_pages(place, codes, arrays):
    out = jax.ShapeDtypeStruct((PAGES * PAGE, 2 * HD), jnp.bfloat16)
    return pl.pallas_call(
        page_kernel,
        in_specs=[pl.BlockSpec(memory_space=pltpu.SMEM)] * 2
        + [pl.BlockSpec(memory_space=pl.ANY)] * len(arrays),
        out_shape=(out, out),
        scratch_shapes=[
            pltpu.VMEM((2 * PAGES * PAGE, 2 * HD), jnp.float32),
            pltpu.SemaphoreType.DMA((len(arrays),)),
        ]
        + [pltpu.VMEM(array.shape, array.dtype) for array in arrays],
        compiler_params=params(),
        name="pages",
    )(place, codes, *arrays)


def moves(step):
    pairs = []
    for y in range(4):
        for z in range(4):
            for core in range(2):
                to_y, to_z, to_core = step(y, z, core)
                pairs.append(((y * 4 + z) * 2 + core, (to_y * 4 + to_z) * 2 + to_core))
    return pairs


def along_y(value, count):
    return lax.ppermute(value, "seq", moves(lambda y, z, c: ((y + count) % 4, z, c)))


def along_z(value, count):
    return lax.ppermute(value, "seq", moves(lambda y, z, c: (y, (z + count) % 4, c)))


def other_core(value):
    return lax.ppermute(value, "seq", moves(lambda y, z, c: (y, z, 1 - c)))


def page_codes(targets, me):
    index = jnp.arange(PAGES, dtype=jnp.int32)
    codes = []
    for owner in (me, me ^ 1):
        slot = targets - owner * PAGES
        match = (slot >= 0) & (slot < PAGES)
        before = match[:, None, :] & (index[None, :] < index[:, None])
        rank = jnp.sum(before.astype(jnp.int32), axis=2)
        code = index * 64 + slot + 1
        for entry in range(MOST):
            codes.append(jnp.sum(jnp.where(match & (rank == entry), code, 0), axis=1) - 1)
    return jnp.stack(codes, axis=1).reshape(-1)


def held_here(targets, me):
    mine = me * PAGES + jnp.arange(PAGES, dtype=jnp.int32)
    same_core = (jnp.arange(SEQ, dtype=jnp.int32) % 2 == me % 2)[:, None]
    match = (targets[None] == mine[:, None, None]) & same_core[None]
    return jnp.any(match, axis=(1, 2))


def project(normed, weight):
    return jnp.dot(normed, weight, preferred_element_type=jnp.float32).astype(jnp.bfloat16)


def attention_and_pages(me, codes, keep, normed, weight):
    core, z, y = me % 2, (me // 2) % 4, me // 8
    kv = project(normed, weight[:, GROUP * HD :])
    normed, kv = lax.optimization_barrier((normed, kv))
    by_z = {0: kv, 1: along_z(kv, 1), 3: along_z(kv, 3)}
    none = {count: along_y(kv, count) for count in (1, 3, 2)}
    by_z[1], by_z[3], normed = lax.optimization_barrier((by_z[1], by_z[3], normed))
    own_queries = project(normed, weight[:, : GROUP * HD])
    pair_queries = other_core(own_queries)

    def flag(*conditions):
        return jnp.stack([jnp.asarray(value, jnp.int32) for value in conditions])

    state, queries = attend_first(core, own_queries, pair_queries, kv)
    kv, odd = lax.optimization_barrier((kv, jnp.concatenate([by_z[1], by_z[3]], axis=0)))
    by_z[2] = along_z(kv, 2)
    odd = {count: along_y(odd, count) for count in (1, 3, 2)}
    state = attend_more(
        flag(y >= 1, y >= 3, y >= 2), queries, state, [none[1], none[3], none[2]]
    )
    state, by_z[2] = lax.optimization_barrier((state, by_z[2]))
    two = {count: along_y(by_z[2], count) for count in (1, 3, 2)}
    state = attend_more(
        flag(z >= 1, z >= 3, z >= 2), queries, state, [by_z[1], by_z[3], by_z[2]]
    )
    state, odd[1], odd[3], odd[2] = lax.optimization_barrier((state, odd[1], odd[3], odd[2]))
    state = attend_more(flag(y >= 1, y >= 3, y >= 2), queries, state, [odd[1], odd[3], odd[2]])
    state, two[1], two[3], two[2] = lax.optimization_barrier((state, two[1], two[3], two[2]))
    own, sent = attend_more(
        flag(y >= 1, y >= 3, y >= 2), queries, state, [two[1], two[3], two[2]], split=True
    )
    got = other_core(sent)

    arrays = [by_z[count] for count in range(4)]
    arrays += [group[count] for group in (none, odd, two) for count in (1, 2, 3)]
    place = jnp.stack([y, z, core])
    own_pages, sent_pages = fetch_pages(place, codes, arrays)
    got_pages = other_core(sent_pages)
    attention = finish(own, got)
    attention, got_pages = lax.optimization_barrier((attention, got_pages))
    keep = keep.reshape(PAGES, 1, 1, 1)
    shape = (PAGES, PAGE, 2, HD)
    kv_cache = jnp.where(keep, own_pages.reshape(shape), got_pages.reshape(shape))
    return attention, kv_cache


def on_device(
    features,
    conv_weight,
    conv_bias,
    embed_weight,
    position_table,
    norm_gain,
    qkv_weight,
    page_owner,
    page_slot,
):
    me = lax.axis_index("seq").astype(jnp.int32)
    tensor = lax.axis_index("tensor").astype(jnp.int32)
    tensor_count = lax.axis_size("tensor")
    weight = lax.all_gather(qkv_weight, "seq", axis=0, tiled=True)
    parts = partial_latents(features, conv_weight)
    own = parts[: FRAMES * EXT].reshape(FRAMES, EXT * LAT)
    target = (page_owner * PAGES + page_slot).astype(jnp.float32)
    target = jnp.broadcast_to(target, (FRAMES, PAGES))
    message = jnp.concatenate([own, target], axis=1)
    message = jnp.pad(message, ((0, 0), (0, 512 - message.shape[1])))
    message = jnp.broadcast_to(message[:, None], (FRAMES, SEQ // FRAMES, 512)).reshape(SEQ, 512)
    message = lax.all_to_all(message, "seq", split_axis=0, concat_axis=0, tiled=True)
    gain = norm_gain.reshape(1, -1)
    message, gain = lax.optimization_barrier((message, gain))
    targets = message[:, EXT * LAT : EXT * LAT + PAGES].astype(jnp.int32)
    offset = tensor - me % (SEQ // FRAMES)
    latent = place_latents(message[:, : EXT * LAT].reshape(SEQ * EXT, LAT), offset)
    for bit in (1, 2, 4):
        swap = [(i, i ^ bit) for i in range(tensor_count)]
        latent = latent + lax.ppermute(latent, "tensor", swap)
    latent = latent + conv_bias[:, None]
    normed = normed_hidden(latent, embed_weight, position_table, gain)
    codes, keep = page_codes(targets, me), held_here(targets, me)
    normed, codes, keep = lax.optimization_barrier((normed, codes, keep))
    return attention_and_pages(me, codes, keep, normed, weight)


def solution(mesh):
    placed = (
        P(None, "tensor", "seq", None),
        P(),
        P(),
        P(),
        P("seq", None),
        P(),
        P("seq", "tensor"),
        P("seq"),
        P("seq"),
    )
    return jax.shard_map(
        on_device,
        mesh=mesh,
        in_specs=placed,
        out_specs=(P("seq", "tensor"), P("seq", None, None, "tensor")),
        check_vma=False,
    )
```

```python
import functools

import jax
import jax.numpy as jnp
import numpy as np
from jax import lax
from jax.experimental import pallas as pl
from jax.experimental.pallas import tpu as pltpu
from jax.sharding import PartitionSpec as P

HD = 128
PAGE = 8
GROUP = 4
LAT = 16
BLK = 320
PAGES = 40
MOST = 3
SEQ = 32
ROWS = 5
COLS = 2
FRAMES = 4
EXT = (ROWS + 2) * (COLS + 2)
TOK = 384
TILE = 256
QROWS = GROUP * BLK
STATE = HD + 8
VMEM = 24 * 1024 * 1024


def params(**extra):
    return pltpu.CompilerParams(vmem_limit_bytes=VMEM, **extra)


def cost(blocks):
    scores = blocks * 2 * QROWS * BLK
    return pl.CostEstimate(flops=4 * HD * scores, bytes_accessed=3 << 20, transcendentals=scores)


def roll_lanes(value, shift):
    shift = shift % value.shape[1]
    return pltpu.roll(value, shift, 1) if shift else value


def conv_kernel(feat_ref, weight_ref, out_ref, grid_ref):
    grid_ref[...] = jnp.zeros_like(grid_ref)
    for frame in range(FRAMES):
        for row in range(ROWS):
            start = frame * EXT + (row + 1) * (COLS + 2) + 1
            value = feat_ref[frame, row].astype(jnp.float32)
            grid_ref[start : start + COLS, :] = value / (1.0 + jnp.exp(-value))
    active = grid_ref[...].astype(jnp.bfloat16)
    product = lax.dot_general(
        weight_ref[...], active, (((1,), (1,)), ((), ())), preferred_element_type=jnp.float32
    )
    lane = lax.broadcasted_iota(jnp.int32, (LAT, 128), 1)
    total = jnp.zeros((LAT, 128), jnp.float32)
    for time in range(3):
        part = jnp.zeros((LAT, 128), jnp.float32)
        for row in range(3):
            for col in range(3):
                index = (time * 3 + row) * 3 + col
                piece = product[index * LAT : (index + 1) * LAT, :]
                part = part + roll_lanes(piece, -((row - 1) * (COLS + 2) + col - 1))
        delay = (2 - time) * EXT
        if delay:
            part = jnp.where(lane >= delay, roll_lanes(part, delay), 0.0)
        total = total + part
    padded = jnp.concatenate([total, jnp.zeros((128 - LAT, 128), jnp.float32)], axis=0)
    out_ref[...] = jnp.transpose(padded)[:, :LAT]


def partial_latents(features, conv_weight):
    weight = jnp.transpose(conv_weight, (0, 1, 2, 4, 3)).reshape(-1, conv_weight.shape[3])
    return pl.pallas_call(
        conv_kernel,
        out_shape=jax.ShapeDtypeStruct((128, LAT), jnp.float32),
        scratch_shapes=[pltpu.VMEM((128, features.shape[-1]), jnp.float32)],
        compiler_params=params(),
        name="conv",
    )(features, weight)


def split_three(value):
    high = value.astype(jnp.bfloat16)
    rest = value - high.astype(jnp.float32)
    middle = rest.astype(jnp.bfloat16)
    low = (rest - middle.astype(jnp.float32)).astype(jnp.bfloat16)
    return high, middle, low


def place_kernel(offset_ref, parts_ref, token_ref, out_ref):
    count = parts_ref.shape[0]
    token = lax.broadcasted_iota(jnp.int32, (TOK, count), 0) - offset_ref[0] * BLK
    pick = jnp.where(token == token_ref[...], 1.0, 0.0).astype(jnp.bfloat16)
    total = jnp.zeros((LAT, TOK), jnp.float32)
    for part in reversed(split_three(parts_ref[...])):
        total = total + lax.dot_general(
            part, pick, (((0,), (1,)), ((), ())), preferred_element_type=jnp.float32
        )
    out_ref[...] = total


def place_table():
    row = np.arange(ROWS + 2).reshape(1, -1, 1) - 1
    col = np.arange(COLS + 2).reshape(1, 1, -1) - 1
    width = np.arange(SEQ).reshape(-1, 1, 1) * COLS + col
    inside = (width >= 0) & (width < SEQ * COLS)
    token = np.where(inside, row * SEQ * COLS + width, -(1 << 20))
    return token.astype(np.int32).reshape(1, SEQ * EXT)


def place_latents(parts, offset):
    return pl.pallas_call(
        place_kernel,
        in_specs=[pl.BlockSpec(memory_space=pltpu.SMEM)]
        + [pl.BlockSpec(memory_space=pltpu.VMEM)] * 2,
        out_shape=jax.ShapeDtypeStruct((LAT, TOK), jnp.float32),
        compiler_params=params(),
        name="place",
    )(offset.reshape(1), parts, jnp.asarray(place_table()))


def hidden_kernel(latent_ref, embed_ref, table_ref, gain_ref, out_ref, hid_ref, sq_ref):
    step = pl.program_id(0)
    width = table_ref.shape[1]
    latent = latent_ref[...][:, :BLK]
    latent = jnp.concatenate(split_three(latent), axis=0)
    embed = embed_ref[...]
    hidden = lax.dot_general(
        latent,
        jnp.concatenate([embed, embed, embed], axis=0),
        (((0,), (0,)), ((), ())),
        preferred_element_type=jnp.float32,
    ) + table_ref[...].astype(jnp.float32)
    hid_ref[step] = hidden
    squares = jnp.zeros((BLK, 128), jnp.float32)
    for lane in range(0, width, 128):
        piece = hidden[:, lane : lane + 128]
        squares = squares + piece * piece

    @pl.when(step == 0)
    def _():
        sq_ref[...] = squares

    @pl.when(step > 0)
    def _():
        sq_ref[...] += squares

    @pl.when(step == pl.num_programs(0) - 1)
    def _():
        count = hid_ref.shape[0]
        mean = jnp.sum(sq_ref[...], axis=1, keepdims=True) / (count * width)
        factor = lax.rsqrt(mean + 1e-05)
        for tile in range(count):
            gain = gain_ref[:, tile * width : (tile + 1) * width].astype(jnp.float32)
            normed = hid_ref[tile] * factor * gain
            out_ref[:, tile * width : (tile + 1) * width] = normed.astype(jnp.bfloat16)


def normed_hidden(latent, embed_weight, position_table, gain):
    depth = position_table.shape[1]
    steps = 8
    width = depth // steps
    return pl.pallas_call(
        hidden_kernel,
        grid=(steps,),
        in_specs=[
            pl.BlockSpec((LAT, TOK), lambda i: (0, 0)),
            pl.BlockSpec((LAT, width), lambda i: (0, i)),
            pl.BlockSpec((BLK, width), lambda i: (0, i)),
            pl.BlockSpec((1, depth), lambda i: (0, 0)),
        ],
        out_specs=pl.BlockSpec((BLK, depth), lambda i: (0, 0)),
        out_shape=jax.ShapeDtypeStruct((BLK, depth), jnp.bfloat16),
        scratch_shapes=[
            pltpu.VMEM((steps, BLK, width), jnp.float32),
            pltpu.VMEM((BLK, 128), jnp.float32),
        ],
        compiler_params=params(dimension_semantics=("arbitrary",)),
        name="hidden",
    )(latent, embed_weight, position_table, gain)


def attend_block(masked, partner_full, keys, values, q_ref, state_ref):
    scale = 1.4426950408889634 / HD**0.5
    tiles = 2 * QROWS // TILE

    def score(tile):
        return lax.dot_general(
            keys,
            q_ref[tile * TILE : (tile + 1) * TILE, :],
            (((1,), (1,)), ((), ())),
            preferred_element_type=jnp.float32,
        )

    upcoming = score(0)
    for tile in range(tiles):
        scores = upcoming
        if tile + 1 < tiles:
            upcoming = score(tile + 1)
        cut = slice(tile * TILE, (tile + 1) * TILE)
        allowed = None
        if masked:
            key = lax.broadcasted_iota(jnp.int32, scores.shape, 0)
            query = tile * TILE + lax.broadcasted_iota(jnp.int32, (1, TILE), 1)
            if tile * TILE >= QROWS:
                query = jnp.where(partner_full, BLK, -1) + 0 * query
            else:
                for head in range(GROUP - 1, 0, -1):
                    query = jnp.where(query >= head * BLK, query - head * BLK, query)
            allowed = key <= query
            scores = jnp.where(allowed, scores, -1e30)
        peak = jnp.max(scores, axis=0, keepdims=True)
        if masked:
            best = peak
        else:
            old = state_ref[HD : HD + 1, cut]
            best = jnp.maximum(old, peak)
            factor = jnp.exp2((old - best) * scale)
        weights = jnp.exp2((scores - best) * scale)
        if masked:
            weights = jnp.where(allowed, weights, 0.0)
        total = jnp.sum(weights, axis=0, keepdims=True)
        summed = lax.dot_general(
            values,
            weights.astype(jnp.bfloat16),
            (((0,), (0,)), ((), ())),
            preferred_element_type=jnp.float32,
        )
        if not masked:
            total = total + state_ref[HD + 1 : HD + 2, cut] * factor
            summed = summed + state_ref[:HD, cut] * factor
        state_ref[HD : HD + 1, cut] = best
        state_ref[HD + 1 : HD + 2, cut] = total
        state_ref[:HD, cut] = summed


def attend_rolled(keys, values, q_ref, state_ref, score_ref):
    scale = 1.4426950408889634 / HD**0.5
    tiles = 2 * QROWS // TILE
    rows = keys.shape[0]

    def score(tile, slot):
        start = pl.multiple_of(jnp.minimum(tile, tiles - 1) * TILE, TILE)
        score_ref[slot, :rows, :] = lax.dot_general(
            keys,
            q_ref[pl.ds(start, TILE), :],
            (((1,), (1,)), ((), ())),
            preferred_element_type=jnp.float32,
        )

    def update(tile, slot):
        cut = pl.ds(pl.multiple_of(tile * TILE, TILE), TILE)
        scores = score_ref[slot, :rows, :]
        old = state_ref[HD : HD + 1, cut]
        best = jnp.maximum(old, jnp.max(scores, axis=0, keepdims=True))
        factor = jnp.exp2((old - best) * scale)
        weights = jnp.exp2((scores - best) * scale)
        total = jnp.sum(weights, axis=0, keepdims=True)
        summed = lax.dot_general(
            values,
            weights.astype(jnp.bfloat16),
            (((0,), (0,)), ((), ())),
            preferred_element_type=jnp.float32,
        )
        state_ref[HD : HD + 1, cut] = best
        state_ref[HD + 1 : HD + 2, cut] = total + state_ref[HD + 1 : HD + 2, cut] * factor
        state_ref[:HD, cut] = summed + state_ref[:HD, cut] * factor

    score(0, 0)

    def body(pair, carry):
        score(2 * pair + 1, 1)
        update(2 * pair, 0)
        score(2 * pair + 2, 0)
        update(2 * pair + 1, 1)
        return carry

    lax.fori_loop(0, tiles // 2, body, 0)


def first_kernel(core_ref, own_ref, pair_ref, kv_ref, state_ref, q_ref):
    for index, ref in enumerate((own_ref, pair_ref)):
        for head in range(GROUP):
            start = (index * GROUP + head) * BLK
            q_ref[start : start + BLK, :] = ref[:, head * HD : (head + 1) * HD]
    state_ref[HD + 2 :, :] = jnp.zeros((STATE - HD - 2, 2 * QROWS), jnp.float32)
    attend_block(True, core_ref[0] == 0, kv_ref[:, :HD], kv_ref[:, HD:], q_ref, state_ref)


def attend_first(core, own, pair, kv):
    return pl.pallas_call(
        first_kernel,
        in_specs=[pl.BlockSpec(memory_space=pltpu.SMEM)]
        + [pl.BlockSpec(memory_space=pltpu.VMEM)] * 3,
        out_shape=(
            jax.ShapeDtypeStruct((STATE, 2 * QROWS), jnp.float32),
            jax.ShapeDtypeStruct((2 * QROWS, HD), jnp.bfloat16),
        ),
        compiler_params=params(),
        cost_estimate=cost(1),
        name="first",
    )(core.reshape(1), own, pair, kv)


def more_kernel(count, split, flag_ref, q_ref, state_ref, *rest):
    arrays, rest = rest[:count], rest[count:]
    if split:
        own_out_ref, pair_out_ref, held_ref, sems, score_ref, work_ref = rest
    else:
        work_ref, held_ref, sems, score_ref = rest
    copies = []
    for index, array in enumerate(arrays):
        unit = array.shape[0]
        held = held_ref.at[pl.ds(index * unit, unit), :]
        copies.append(pltpu.make_async_copy(array, held, sems.at[index]))
        copies[-1].start()
    work_ref[...] = state_ref[...]
    for copy in copies:
        copy.wait()

    every = jnp.int32(unit == BLK)
    for index in range(count):
        every = every * flag_ref[index]

    if unit == BLK:

        @pl.when(every != 0)
        def _():
            attend_rolled(held_ref[:, :HD], held_ref[:, HD:], q_ref, work_ref, score_ref)

    def body(index, carry):
        @pl.when(flag_ref[index] != 0)
        def _():
            rows = pl.ds(pl.multiple_of(index * unit, unit), unit)
            attend_block(False, None, held_ref[rows, :HD], held_ref[rows, HD:], q_ref, work_ref)

        return carry

    @pl.when(every == 0)
    def _():
        lax.fori_loop(0, count, body, 0)

    if split:
        own_out_ref[...] = work_ref[:, :QROWS]
        pair_out_ref[...] = work_ref[:, QROWS:]


def attend_more(flags, queries, state, arrays, split=False):
    unit, count = arrays[0].shape[0], len(arrays)
    half = jax.ShapeDtypeStruct((STATE, QROWS), jnp.float32)
    whole = jax.ShapeDtypeStruct((STATE, 2 * QROWS), jnp.float32)
    scratch = [
        pltpu.VMEM((count * unit, 2 * HD), jnp.bfloat16),
        pltpu.SemaphoreType.DMA((count,)),
        pltpu.VMEM((2, 3 * BLK if unit == BLK else 8, TILE), jnp.float32),
    ]
    if split:
        scratch.append(pltpu.VMEM((STATE, 2 * QROWS), jnp.float32))
    return pl.pallas_call(
        functools.partial(more_kernel, count, split),
        in_specs=[pl.BlockSpec(memory_space=pltpu.SMEM)]
        + [pl.BlockSpec(memory_space=pltpu.VMEM)] * 2
        + [pl.BlockSpec(memory_space=pl.ANY)] * count,
        out_shape=(half, half) if split else whole,
        scratch_shapes=scratch,
        compiler_params=params(),
        cost_estimate=cost(count * unit // BLK),
        name="more",
    )(flags, queries, state, *arrays)


def finish_kernel(own_ref, got_ref, out_ref, row_ref):
    scale = 1.4426950408889634 / HD**0.5
    for start in range(0, QROWS, TILE):
        cut = slice(start, start + TILE)
        first, second = own_ref[HD : HD + 1, cut], got_ref[HD : HD + 1, cut]
        best = jnp.maximum(first, second)
        first = jnp.exp2((first - best) * scale)
        second = jnp.exp2((second - best) * scale)
        total = own_ref[HD + 1 : HD + 2, cut] * first + got_ref[HD + 1 : HD + 2, cut] * second
        summed = own_ref[:HD, cut] * first + got_ref[:HD, cut] * second
        row_ref[cut, :] = jnp.transpose(summed / total)
    for head in range(GROUP):
        rows = row_ref[head * BLK : (head + 1) * BLK, :]
        out_ref[:, head * HD : (head + 1) * HD] = rows.astype(jnp.bfloat16)


def finish(own, got):
    return pl.pallas_call(
        finish_kernel,
        out_shape=jax.ShapeDtypeStruct((BLK, GROUP * HD), jnp.bfloat16),
        scratch_shapes=[pltpu.VMEM((QROWS, HD), jnp.float32)],
        compiler_params=params(),
        name="finish",
    )(own, got)


def take_pages(group, owner, entry, base, code_ref, array, held_ref):
    code = code_ref[group * MOST + entry]

    @pl.when(code >= 0)
    def _():
        page = code >> 6
        slot = (code & 63) + owner * PAGES
        row = pl.multiple_of(base + (page >> 1) * 2 * PAGE, 2 * PAGE)
        rows = array[pl.ds(row, 2 * PAGE), :].astype(jnp.float32)
        rows = jnp.where((page & 1) == 1, rows[PAGE:], rows[:PAGE])
        held_ref[pl.ds(pl.multiple_of(slot * PAGE, PAGE), PAGE), :] = rows
        if entry + 1 < MOST:
            take_pages(group, owner, entry + 1, base, code_ref, array, held_ref)


def page_kernel(place_ref, code_ref, *rest):
    count = (len(rest) - 4) // 2
    remote, own_ref, pair_ref = rest[:count], rest[count], rest[count + 1]
    held_ref, sems, arrays = rest[count + 2], rest[count + 3], rest[count + 4 :]
    copies = [
        pltpu.make_async_copy(remote[index], arrays[index], sems.at[index])
        for index in range(count)
    ]
    for copy in copies:
        copy.start()
    held_ref[...] = jnp.zeros_like(held_ref)
    y, z, core = place_ref[0], place_ref[1], place_ref[2]
    waited = set()
    for by_y in range(4):
        for by_z in range(4):
            if by_y == 0:
                index, base = by_z, 0
            else:
                index, base = 3 + by_y + (0, 3, 6, 3)[by_z], by_z // 3 * BLK
            if index not in waited:
                copies[index].wait()
                waited.add(index)
            array = arrays[index]
            source = (((y - by_y) & 3) * 4 + ((z - by_z) & 3)) * 2 + core
            for owner in range(2):
                take_pages(source * 2 + owner, owner, 0, base, code_ref, array, held_ref)

    own_ref[...] = held_ref[: PAGES * PAGE].astype(jnp.bfloat16)
    pair_ref[...] = held_ref[PAGES * PAGE :].astype(jnp.bfloat16)


def fetch_pages(place, codes, arrays):
    out = jax.ShapeDtypeStruct((PAGES * PAGE, 2 * HD), jnp.bfloat16)
    return pl.pallas_call(
        page_kernel,
        in_specs=[pl.BlockSpec(memory_space=pltpu.SMEM)] * 2
        + [pl.BlockSpec(memory_space=pl.ANY)] * len(arrays),
        out_shape=(out, out),
        scratch_shapes=[
            pltpu.VMEM((2 * PAGES * PAGE, 2 * HD), jnp.float32),
            pltpu.SemaphoreType.DMA((len(arrays),)),
        ]
        + [pltpu.VMEM(array.shape, array.dtype) for array in arrays],
        compiler_params=params(),
        name="pages",
    )(place, codes, *arrays)


def moves(step):
    pairs = []
    for y in range(4):
        for z in range(4):
            for core in range(2):
                to_y, to_z, to_core = step(y, z, core)
                pairs.append(((y * 4 + z) * 2 + core, (to_y * 4 + to_z) * 2 + to_core))
    return pairs


def along_y(value, count):
    return lax.ppermute(value, "seq", moves(lambda y, z, c: ((y + count) % 4, z, c)))


def along_z(value, count):
    return lax.ppermute(value, "seq", moves(lambda y, z, c: (y, (z + count) % 4, c)))


def other_core(value):
    return lax.ppermute(value, "seq", moves(lambda y, z, c: (y, z, 1 - c)))


def page_codes(targets, me):
    index = jnp.arange(PAGES, dtype=jnp.int32)
    codes = []
    for owner in (me, me ^ 1):
        slot = targets - owner * PAGES
        match = (slot >= 0) & (slot < PAGES)
        before = match[:, None, :] & (index[None, :] < index[:, None])
        rank = jnp.sum(before.astype(jnp.int32), axis=2)
        code = index * 64 + slot + 1
        for entry in range(MOST):
            codes.append(jnp.sum(jnp.where(match & (rank == entry), code, 0), axis=1) - 1)
    return jnp.stack(codes, axis=1).reshape(-1)


def held_here(targets, me):
    mine = me * PAGES + jnp.arange(PAGES, dtype=jnp.int32)
    same_core = (jnp.arange(SEQ, dtype=jnp.int32) % 2 == me % 2)[:, None]
    match = (targets[None] == mine[:, None, None]) & same_core[None]
    return jnp.any(match, axis=(1, 2))


def project(normed, weight):
    return jnp.dot(normed, weight, preferred_element_type=jnp.float32).astype(jnp.bfloat16)


def attention_and_pages(me, codes, keep, normed, weight):
    core, z, y = me % 2, (me // 2) % 4, me // 8
    kv = project(normed, weight[:, GROUP * HD :])
    normed, kv = lax.optimization_barrier((normed, kv))
    by_z = {0: kv, 1: along_z(kv, 1), 3: along_z(kv, 3)}
    none = {count: along_y(kv, count) for count in (1, 3, 2)}
    own_queries = project(normed, weight[:, : GROUP * HD])
    pair_queries = other_core(own_queries)

    def flag(*conditions):
        return jnp.stack([jnp.asarray(value, jnp.int32) for value in conditions])

    state, queries = attend_first(core, own_queries, pair_queries, kv)
    state, by_z[1], by_z[3] = lax.optimization_barrier((state, by_z[1], by_z[3]))
    kv, odd = lax.optimization_barrier((kv, jnp.concatenate([by_z[1], by_z[3]], axis=0)))
    by_z[2] = along_z(kv, 2)
    odd = {count: along_y(odd, count) for count in (1, 3, 2)}
    state = attend_more(
        flag(y >= 1, y >= 3, y >= 2), queries, state, [none[1], none[3], none[2]]
    )
    state, by_z[2] = lax.optimization_barrier((state, by_z[2]))
    two = {count: along_y(by_z[2], count) for count in (1, 3, 2)}
    state = attend_more(
        flag(z >= 1, z >= 3, z >= 2), queries, state, [by_z[1], by_z[3], by_z[2]]
    )
    state, odd[1], odd[3], odd[2] = lax.optimization_barrier((state, odd[1], odd[3], odd[2]))
    state = attend_more(flag(y >= 1, y >= 3, y >= 2), queries, state, [odd[1], odd[3], odd[2]])
    state, two[1], two[3], two[2] = lax.optimization_barrier((state, two[1], two[3], two[2]))
    own, sent = attend_more(
        flag(y >= 1, y >= 3, y >= 2), queries, state, [two[1], two[3], two[2]], split=True
    )
    got = other_core(sent)

    arrays = [by_z[count] for count in range(4)]
    arrays += [group[count] for group in (none, odd, two) for count in (1, 2, 3)]
    place = jnp.stack([y, z, core])
    own_pages, sent_pages = fetch_pages(place, codes, arrays)
    got_pages = other_core(sent_pages)
    attention = finish(own, got)
    attention, got_pages = lax.optimization_barrier((attention, got_pages))
    keep = keep.reshape(PAGES, 1, 1, 1)
    shape = (PAGES, PAGE, 2, HD)
    kv_cache = jnp.where(keep, own_pages.reshape(shape), got_pages.reshape(shape))
    return attention, kv_cache


def on_device(
    features,
    conv_weight,
    conv_bias,
    embed_weight,
    position_table,
    norm_gain,
    qkv_weight,
    page_owner,
    page_slot,
):
    me = lax.axis_index("seq").astype(jnp.int32)
    tensor = lax.axis_index("tensor").astype(jnp.int32)
    tensor_count = lax.axis_size("tensor")
    weight = lax.all_gather(qkv_weight, "seq", axis=0, tiled=True)
    parts = partial_latents(features, conv_weight)
    own = parts[: FRAMES * EXT].reshape(FRAMES, EXT * LAT)
    target = (page_owner * PAGES + page_slot).astype(jnp.float32)
    target = jnp.broadcast_to(target, (FRAMES, PAGES))
    message = jnp.concatenate([own, target], axis=1)
    message = jnp.pad(message, ((0, 0), (0, 512 - message.shape[1])))
    message = jnp.broadcast_to(message[:, None], (FRAMES, SEQ // FRAMES, 512)).reshape(SEQ, 512)
    message = lax.all_to_all(message, "seq", split_axis=0, concat_axis=0, tiled=True)
    gain = norm_gain.reshape(1, -1)
    message, gain = lax.optimization_barrier((message, gain))
    targets = message[:, EXT * LAT : EXT * LAT + PAGES].astype(jnp.int32)
    offset = tensor - me % (SEQ // FRAMES)
    latent = place_latents(message[:, : EXT * LAT].reshape(SEQ * EXT, LAT), offset)
    for bit in (1, 2, 4):
        swap = [(i, i ^ bit) for i in range(tensor_count)]
        latent = latent + lax.ppermute(latent, "tensor", swap)
    latent = latent + conv_bias[:, None]
    normed = normed_hidden(latent, embed_weight, position_table, gain)
    codes, keep = page_codes(targets, me), held_here(targets, me)
    normed, codes, keep = lax.optimization_barrier((normed, codes, keep))
    return attention_and_pages(me, codes, keep, normed, weight)


def solution(mesh):
    placed = (
        P(None, "tensor", "seq", None),
        P(),
        P(),
        P(),
        P("seq", None),
        P(),
        P("seq", "tensor"),
        P("seq"),
        P("seq"),
    )
    return jax.shard_map(
        on_device,
        mesh=mesh,
        in_specs=placed,
        out_specs=(P("seq", "tensor"), P("seq", None, None, "tensor")),
        check_vma=False,
    )
```
